32 devices in a mesh: narrow: 2 (over x), wide: 16 (over z, y, core).
Axes of the slice: x: 2, y: 2, z: 4, core: 2. Of those that a mesh axis runs over, the one named last changes fastest.
Arguments:
- features: float32 [512, 49, 512], P(('narrow', 'wide')), may hold values from -6 to 6
- cotangent: bfloat16 [512, 49, 512], P(('narrow', 'wide')), may hold values from -6 to 6
- counts: int32 [32], P(('narrow', 'wide')), may hold values from 1 to 16, as said below
- hidden_weight: float32 [512, 2048], P(None, 'wide'), may hold values from -0.25 to 0.25
- hidden_bias: float32 [2048], replicated, may hold values from -3 to 3
- output_weight: float32 [2048, 512], P('wide'), may hold values from -0.125 to 0.125
- vectors: float32 [7, 512], replicated
- hidden_moment: float32 [512, 2048], P(None, 'wide'), may hold values from -32 to 32
- hidden_square: float32 [512, 2048], P(None, 'wide'), may hold values from 2.25792 to 9.03168
- bias_moment: float32 [2048], replicated, may hold values from -32 to 32
- bias_square: float32 [2048], replicated, may hold values from 2.25792 to 9.03168
- output_moment: float32 [2048, 512], P('wide'), may hold values from -56 to 56
- output_square: float32 [2048, 512], P('wide'), may hold values from 6.272 to 25.088
- vector_moment: float32 [7, 512], replicated, may hold values from -80 to 80
- vector_square: float32 [7, 512], replicated, may hold values from 16.05632 to 65.2288
Outputs:
- block_out: float32 [512, 49, 512], P(('narrow', 'wide'))
- input_grad: float32 [512, 49, 512], P(('narrow', 'wide'))
- hidden_weight_new: float32 [512, 2048], P(None, 'wide')
- hidden_moment_new: float32 [512, 2048], P(None, 'wide')
- hidden_square_new: float32 [512, 2048], P(None, 'wide')
- hidden_bias_new: float32 [2048], replicated
- bias_moment_new: float32 [2048], replicated
- bias_square_new: float32 [2048], replicated
- output_weight_new: float32 [2048, 512], P('wide')
- output_moment_new: float32 [2048, 512], P('wide')
- output_square_new: float32 [2048, 512], P('wide')
- vectors_new: float32 [7, 512], replicated
- vector_moment_new: float32 [7, 512], replicated
- vector_square_new: float32 [7, 512], replicated
The draws below stay inside these ranges and needn't reach their ends.
Inputs may be any that keep to these rules, and one draw needn't show every extreme that they name: Device i holds counts[i] valid images, in its first slots; the remaining slots of its 16 are padding; the last device's slots are all valid.
All inputs are finite; a program needn't handle non-finite values.
Results may differ from the reference program's by a relative error of at most 0.0062.
Values may be sent and summed in bfloat16 or wider, within the bound.
No kernel may reach another device: no remote copies, remote signals or barrier semaphores. Data moves between devices by JAX's collectives and lax.ppermute only.
A program may use at most 320 MiB of HBM per device.

```python
import math
import jax
import jax.numpy as jnp
from jax import lax

D = 512
HID = 2048
SIDE = 7
STEP = 5
IMG_DEV = 16
PIX = 49
IMAGES = 512
ROWS = 25088
N_NARROW = 2
N_WIDE = 16


def draw_counts(key, part):
    key = jax.random.fold_in(key, 11)
    total_devices = N_NARROW * N_WIDE
    device_index = jnp.arange(total_devices, dtype=jnp.int32)
    extent = N_WIDE * N_NARROW - 1
    position = device_index % N_WIDE + N_WIDE * (device_index // N_WIDE)
    base_count = IMG_DEV * (extent + 2 * position) // (3 * extent)
    jitter = jax.random.randint(key, (total_devices,), -1, 2)
    counts = jnp.clip(base_count + jitter, 1, IMG_DEV)
    return jnp.where(device_index == total_devices - 1, IMG_DEV, counts).astype(jnp.int32)


def draw_vectors(key, part):
    key = jax.random.fold_in(key, 5)
    split_keys = jax.random.split(key, 3)
    gains = 1.0 + 0.6 * jax.random.uniform(split_keys[0], (2, D), jnp.float32, -1.0, 1.0)
    shifts = 0.5 * jax.random.normal(split_keys[1], (3, D), jnp.float32)
    scales = jnp.exp(jax.random.uniform(split_keys[2], (2, D), jnp.float32, math.log(0.5), math.log(2.0)))
    return jnp.stack([gains[0], shifts[0], scales[0], gains[1], shifts[1], scales[1], shifts[2]]).astype(jnp.float32)


def block_levels(stream_key, dims, pieces, least, largest):
    def one(axis_at, shards_of):
        steps = jax.random.uniform(jax.random.fold_in(jax.random.fold_in(stream_key, 6), axis_at), (shards_of,), jnp.float32, least / len(pieces), largest / len(pieces))
        return jnp.repeat(jnp.exp(steps), dims[axis_at] // shards_of).reshape((-1,) + (1,) * (len(dims) - axis_at - 1))

    factor_of = one(*pieces[0])
    for cut in pieces[1:]:
        factor_of = factor_of * one(*cut)
    return factor_of


def normal_values(own_key, shape, scale, bound, pieces=(), held_as=jnp.bfloat16):
    entries = jax.random.normal(own_key, shape, jnp.float32) * scale
    if len(pieces) > 0:
        entries = block_levels(own_key, shape, pieces, -0.22, 0.18) * entries
    return jnp.clip(entries, min=-bound, max=bound).astype(held_as)


def setup_inputs(seed: int = 0) -> dict:
    key_list = jax.random.split(jax.random.key(seed), 16)
    return {
        "features": normal_values(key_list[0], (IMAGES, PIX, D), 1.0, 6.0, ((0, 32),), jnp.float32),
        "cotangent": normal_values(key_list[1], (IMAGES, PIX, D), 1.0, 6.0, ((0, 32),)),
        "counts": draw_counts(jax.random.fold_in(key_list[15], 71), 0),
        "hidden_weight": normal_values(key_list[3], (D, HID), D ** -0.5, 0.25, ((1, 16),), jnp.float32),
        "hidden_bias": normal_values(key_list[4], (HID,), 0.5, 3.0, (), jnp.float32),
        "output_weight": normal_values(key_list[5], (HID, D), HID ** -0.5, 0.125, ((0, 16),), jnp.float32),
        "vectors": draw_vectors(jax.random.fold_in(key_list[15], 71), 0),
        "hidden_moment": normal_values(key_list[7], (D, HID), (0.033 * ROWS ** 0.5), 32.0, ((1, 16),), jnp.float32),
        "hidden_square": jnp.clip(jnp.exp(math.log(9.03168) - 1.3862944 * jax.random.uniform(key_list[8], (D, HID), jnp.float32) ** block_levels(key_list[8], (D, HID), ((1, 16),), -0.2, 0.2)), 2.25792, 9.03168),
        "bias_moment": normal_values(key_list[9], (HID,), (0.033 * ROWS ** 0.5), 32.0, (), jnp.float32),
        "bias_square": jnp.clip(jnp.exp(jax.random.uniform(key_list[10], (HID,), jnp.float32, math.log(2.25792), math.log(9.03168))), 2.25792, 9.03168),
        "output_moment": normal_values(key_list[11], (HID, D), (0.055 * ROWS ** 0.5), 56.0, ((0, 16),), jnp.float32),
        "output_square": jnp.clip(jnp.exp(math.log(25.088) - 1.3862944 * jax.random.uniform(key_list[12], (HID, D), jnp.float32) ** block_levels(key_list[12], (HID, D), ((0, 16),), -0.2, 0.2)), 6.272, 25.088),
        "vector_moment": normal_values(key_list[13], (7, D), (0.09 * ROWS ** 0.5), 80.0, (), jnp.float32),
        "vector_square": jnp.clip(jnp.exp(jax.random.uniform(key_list[14], (7, D), jnp.float32, math.log(16.05632), math.log(65.2288))), 16.05632, 65.2288),
    }


@jax.custom_vjp
def low(v):
    return lax.optimization_barrier(v.astype(jnp.bfloat16)).astype(jnp.float32)

@jax.custom_vjp
def low_back(v):
    return v

def low_keep(v):
    return (low(v), None)

def low_pass(kept, grad):
    return (grad,)

def back_keep(v):
    return (v, None)

def back_low(kept, grad):
    return (low(grad),)
low.defvjp(low_keep, low_pass)
low_back.defvjp(back_keep, back_low)
norm_epsilon = 1e-05
first_decay = 0.9
second_decay = 0.999
adam_epsilon = 1e-08
weight_shrink = 0.05

def pool_matrix(side):
    places = jnp.arange(side * side, dtype=jnp.int32)
    place_row = places // side
    place_col = places % side
    nearby = (jnp.abs(place_row[:, None] - place_row[None, :]) <= 1) & (jnp.abs(place_col[:, None] - place_col[None, :]) <= 1)
    nearby = nearby.astype(jnp.float32)
    return nearby / lax.optimization_barrier(jnp.sum(nearby, axis=1, keepdims=True))

def group_norm(values, gain, shift):
    centre = lax.optimization_barrier(jnp.mean(values, axis=(1, 2), keepdims=True))
    spread = lax.optimization_barrier(jnp.mean((values - centre) ** 2, axis=(1, 2), keepdims=True))
    return (values - centre) * lax.rsqrt(spread + norm_epsilon) * gain + shift

def forward(inputs, vectors, hidden_weight, hidden_bias, output_weight):
    pool = pool_matrix(SIDE)
    normed = group_norm(inputs, vectors[0], vectors[1])
    mixed = jnp.einsum('pq,iqc->ipc', pool, normed, precision=lax.Precision.HIGHEST) - normed
    middle = inputs + vectors[2] * mixed
    second = low(group_norm(middle, vectors[3], vectors[4]))
    flat_rows = second.reshape(-1, D)
    hidden = low_back(jnp.dot(flat_rows, low(hidden_weight), precision=lax.Precision.HIGHEST) + hidden_bias)
    active = low(jax.nn.gelu(hidden, approximate=False))
    branch = low_back(jnp.dot(active, low(output_weight), precision=lax.Precision.HIGHEST))
    branch = (branch + vectors[6]).reshape(inputs.shape)
    return middle + vectors[5] * branch

def adamw_update(param, grad, moment, square, rate, shrink):
    moment_new = first_decay * moment + (1.0 - first_decay) * grad
    square_new = second_decay * square + (1.0 - second_decay) * grad * grad
    moment_hat = moment_new / (1.0 - first_decay ** STEP)
    square_hat = square_new / (1.0 - second_decay ** STEP)
    param_new = param - rate * (moment_hat / (jnp.sqrt(square_hat) + adam_epsilon) + shrink * param)
    return (param_new, moment_new, square_new)

def reference(features, cotangent, counts, hidden_weight, hidden_bias, output_weight, vectors, hidden_moment, hidden_square, bias_moment, bias_square, output_moment, output_square, vector_moment, vector_square):
    slots = jnp.arange(IMAGES, dtype=jnp.int32)
    valid = (slots % IMG_DEV < counts[slots // IMG_DEV]).astype(jnp.float32)
    weighted = cotangent.astype(jnp.float32) * valid[:, None, None]
    groups = IMAGES // 64
    block_inputs = features.reshape(groups, 64, PIX, D)
    block_grads = weighted.reshape(groups, 64, PIX, D)

    def one_group(carry, pair):
        group_in, group_grad = pair
        result, pullback = jax.vjp(forward, group_in, vectors, hidden_weight, hidden_bias, output_weight)
        grad_in, grad_vec, grad_hidden, grad_bias, grad_output = pullback(group_grad)
        carry = (carry[0] + grad_vec, carry[1] + grad_hidden, carry[2] + grad_bias, carry[3] + grad_output)
        return (carry, (result, grad_in))
    start_carry = (jnp.zeros((7, D), jnp.float32), jnp.zeros((D, HID), jnp.float32), jnp.zeros((HID,), jnp.float32), jnp.zeros((HID, D), jnp.float32))
    totals, stacked = lax.scan(one_group, start_carry, (block_inputs, block_grads))
    block_out = stacked[0].reshape(IMAGES, PIX, D)
    input_grad = stacked[1].reshape(IMAGES, PIX, D)
    grad_vec, grad_hidden, grad_bias, grad_output = totals
    hidden_new = adamw_update(hidden_weight, grad_hidden, hidden_moment, hidden_square, 0.04, weight_shrink)
    bias_new = adamw_update(hidden_bias, grad_bias, bias_moment, bias_square, 0.2, 0.0)
    output_new = adamw_update(output_weight, grad_output, output_moment, output_square, 0.02, weight_shrink)
    vector_new = adamw_update(vectors, grad_vec, vector_moment, vector_square, 0.3, 0.0)
    return (block_out, input_grad, hidden_new[0], hidden_new[1], hidden_new[2], bias_new[0], bias_new[1], bias_new[2], output_new[0], output_new[1], output_new[2], vector_new[0], vector_new[1], vector_new[2])
```

```python
import functools
import math

import jax
import jax.numpy as jnp
from jax import lax
from jax.experimental import pallas as pl
from jax.experimental.pallas import tpu as pltpu
from jax.sharding import PartitionSpec as P

SIDE = 7
STEP = 5


norm_epsilon = 1e-05
first_decay = 0.9
second_decay = 0.999
adam_epsilon = 1e-08
weight_shrink = 0.05


def pool_matrix(side):
    places = jnp.arange(side * side, dtype=jnp.int32)
    place_row = places // side
    place_col = places % side
    nearby = (jnp.abs(place_row[:, None] - place_row[None, :]) <= 1) & (
        jnp.abs(place_col[:, None] - place_col[None, :]) <= 1
    )
    nearby = nearby.astype(jnp.float32)
    return nearby / jnp.sum(nearby, axis=1, keepdims=True)


def norm_parts(values, gain, shift):
    centre = jnp.mean(values, axis=(1, 2), keepdims=True)
    spread = jnp.mean((values - centre) ** 2, axis=(1, 2), keepdims=True)
    inverse = lax.rsqrt(spread + norm_epsilon)
    scaled = (values - centre) * inverse
    return (scaled * gain + shift, scaled, inverse)


def norm_back(upstream, scaled, inverse):
    first_mean = jnp.mean(upstream, axis=(1, 2), keepdims=True)
    second_mean = jnp.mean(upstream * scaled, axis=(1, 2), keepdims=True)
    return inverse * (upstream - first_mean - scaled * second_mean)


def gelu_slope(values):
    return 0.5 * (1.0 + lax.erf(values / math.sqrt(2.0))) + values * jnp.exp(
        -0.5 * values * values
    ) / math.sqrt(2.0 * math.pi)


def contract_rows(left, right):
    return lax.dot_general(
        left, right, (((0,), (0,)), ((), ())), preferred_element_type=jnp.float32
    )


def contract_cols(left, right):
    return lax.dot_general(
        left, right, (((1,), (1,)), ((), ())), preferred_element_type=jnp.float32
    )


def adamw_update(param, grad, moment, square, rate, shrink):
    moment_new = first_decay * moment + (1.0 - first_decay) * grad
    square_new = second_decay * square + (1.0 - second_decay) * grad * grad
    moment_hat = moment_new / (1.0 - first_decay**STEP)
    square_hat = square_new / (1.0 - second_decay**STEP)
    param_new = param - rate * (moment_hat / (jnp.sqrt(square_hat) + adam_epsilon) + shrink * param)
    return (param_new, moment_new, square_new)


def local(
    features,
    cotangent,
    counts,
    hidden_weight,
    hidden_bias,
    output_weight,
    vectors,
    hidden_moment,
    hidden_square,
    bias_moment,
    bias_square,
    output_moment,
    output_square,
    vector_moment,
    vector_square,
):
    images, pixels, width = features.shape
    rows = images * pixels
    units = hidden_weight.shape[1]
    pool = pool_matrix(SIDE)
    valid = (jnp.arange(images, dtype=jnp.int32) < counts[0]).astype(jnp.float32)
    weighted = cotangent.astype(jnp.float32) * valid[:, None, None]
    normed, first_scaled, first_inverse = norm_parts(features, vectors[0], vectors[1])
    mixed = jnp.einsum("pq,iqc->ipc", pool, normed, precision=lax.Precision.HIGHEST) - normed
    middle = features + vectors[2] * mixed
    second, second_scaled, second_inverse = norm_parts(middle, vectors[3], vectors[4])
    second_low = second.reshape(rows, width).astype(jnp.bfloat16)
    hidden_low = hidden_weight.astype(jnp.bfloat16)
    output_low = output_weight.astype(jnp.bfloat16)
    branch_grad = (weighted * vectors[5]).reshape(rows, width)
    branch_low = branch_grad.astype(jnp.bfloat16)
    offset = lax.axis_index("wide") * units
    local_bias = lax.dynamic_slice_in_dim(hidden_bias, offset, units)
    hidden_all = (
        jnp.dot(
            lax.all_gather(second_low, "wide", axis=0, tiled=True),
            hidden_low,
            preferred_element_type=jnp.float32,
        )
        + local_bias
    )
    active_all = jax.nn.gelu(hidden_all, approximate=False).astype(jnp.bfloat16)
    slope_all = gelu_slope(hidden_all)
    block = active_all
    branch = lax.psum_scatter(
        jnp.dot(block, output_low, preferred_element_type=jnp.float32),
        "wide",
        scatter_dimension=0,
        tiled=True,
    )
    piece = lax.all_gather(branch_low, "wide", axis=0, tiled=True)
    block = active_all
    output_total = contract_rows(block, piece)
    active_grad = contract_cols(piece, output_low)
    hidden_grad = (active_grad * slope_all).astype(jnp.bfloat16)
    local_bias_grad = jnp.sum(hidden_grad.astype(jnp.float32), axis=0)
    bias_part = lax.dynamic_update_slice_in_dim(
        jnp.zeros(hidden_bias.shape, jnp.float32), local_bias_grad, offset, 0
    )
    block = hidden_grad
    second_grad = lax.psum_scatter(
        contract_cols(block, hidden_low), "wide", scatter_dimension=0, tiled=True
    )
    block = hidden_grad
    hidden_part = contract_rows(lax.all_gather(second_low, "wide", axis=0, tiled=True), block)
    branch_full = (branch + vectors[6]).reshape(images, pixels, width)
    block_out = middle + vectors[5] * branch_full
    grad_scale_two = jnp.sum(weighted * branch_full, axis=(0, 1))
    grad_shift_out = jnp.sum(branch_grad, axis=0)
    second_grad = second_grad.reshape(images, pixels, width)
    grad_gain_two = jnp.sum(second_grad * second_scaled, axis=(0, 1))
    grad_shift_two = jnp.sum(second_grad, axis=(0, 1))
    middle_grad = weighted + norm_back(second_grad * vectors[3], second_scaled, second_inverse)
    grad_scale_one = jnp.sum(middle_grad * mixed, axis=(0, 1))
    mixed_grad = middle_grad * vectors[2]
    normed_grad = (
        jnp.einsum("qp,iqc->ipc", pool, mixed_grad, precision=lax.Precision.HIGHEST) - mixed_grad
    )
    grad_gain_one = jnp.sum(normed_grad * first_scaled, axis=(0, 1))
    grad_shift_one = jnp.sum(normed_grad, axis=(0, 1))
    input_grad = middle_grad + norm_back(normed_grad * vectors[0], first_scaled, first_inverse)
    vector_part = jnp.stack(
        [
            grad_gain_one,
            grad_shift_one,
            grad_scale_one,
            grad_gain_two,
            grad_shift_two,
            grad_scale_two,
            grad_shift_out,
        ]
    )
    vector_grad, bias_grad = lax.psum((vector_part, bias_part), ("narrow", "wide"))
    hidden_grad_sum, output_grad_sum = lax.psum((hidden_part, output_total), "narrow")
    hidden_new = adamw_update(
        hidden_weight, hidden_grad_sum, hidden_moment, hidden_square, 0.04, weight_shrink
    )
    bias_new = adamw_update(hidden_bias, bias_grad, bias_moment, bias_square, 0.2, 0.0)
    output_new = adamw_update(
        output_weight, output_grad_sum, output_moment, output_square, 0.02, weight_shrink
    )
    vector_new = adamw_update(vectors, vector_grad, vector_moment, vector_square, 0.3, 0.0)
    return (
        block_out,
        input_grad,
        hidden_new[0],
        hidden_new[1],
        hidden_new[2],
        bias_new[0],
        bias_new[1],
        bias_new[2],
        output_new[0],
        output_new[1],
        output_new[2],
        vector_new[0],
        vector_new[1],
        vector_new[2],
    )


BLOCKS = 8
PAIRS = BLOCKS // 2
f32 = jnp.float32
bf16 = jnp.bfloat16
VMEM = pl.BlockSpec(memory_space=pltpu.VMEM)
SMEM = pl.BlockSpec(memory_space=pltpu.SMEM)


def row_total(values):
    return jnp.sum(values, axis=1, keepdims=True)


def span(i):
    return min(i + 1, SIDE - 1) - max(i - 1, 0) + 1


def near_share(p):
    return 1.0 / (span(p // SIDE) * span(p % SIDE))


def along_row(load, p):
    c = p % SIDE
    total = load(p)
    if c > 0:
        total = total + load(p - 1)
    if c < SIDE - 1:
        total = total + load(p + 1)
    return total


def along_col(load, p):
    r = p // SIDE
    total = load(p)
    if r > 0:
        total = total + load(p - SIDE)
    if r < SIDE - 1:
        total = total + load(p + SIDE)
    return total


def valid_gate(counts_ref, shape):
    slots = lax.broadcasted_iota(jnp.int32, shape, 0)
    return jnp.where(slots < counts_ref[0], 1.0, 0.0)


def pre_kernel(counts_ref, x_ref, cot_ref, vec_ref, sb_ref, q_ref, stat_ref, d_ref, h_ref):
    pixels, images, width = x_ref.shape
    size = pixels * width
    zero = jnp.zeros((images, width), f32)

    def loop(body, init):
        return lax.fori_loop(0, pixels, body, init, unroll=7)

    mu1 = row_total(loop(lambda p, s: s + x_ref[p], zero)) / size

    def centre(p, s):
        d = x_ref[p] - mu1
        d_ref[p] = d
        return s + d * d

    r1 = lax.rsqrt(row_total(loop(centre, zero)) / size + norm_epsilon)
    for p in range(pixels):
        h_ref[p] = along_row(lambda i: d_ref[i], p)
    lift = vec_ref[2:3, :] * (r1 * vec_ref[0:1, :])
    total = zero
    for p in range(pixels):
        q = along_col(lambda i: h_ref[i], p) * near_share(p) - d_ref[p]
        q_ref[p] = q
        total = total + (x_ref[p] + lift * q)
    mu2 = row_total(total) / size

    def spread(p, s):
        d = x_ref[p] + lift * q_ref[p] - mu2
        d_ref[p] = d
        return s + d * d

    r2 = lax.rsqrt(row_total(loop(spread, zero)) / size + norm_epsilon)
    scale = r2 * vec_ref[3:4, :]
    shift = jnp.broadcast_to(vec_ref[4:5, :], (images, width))
    gate = valid_gate(counts_ref, (images, width)) * vec_ref[5:6, :]

    def finish(p, carry):
        sb_ref[0, p] = (d_ref[p] * scale + shift).astype(bf16)
        sb_ref[1, p] = (cot_ref[p].astype(f32) * gate).astype(bf16)
        return carry

    loop(finish, 0)
    for i, stat in enumerate((mu1, r1, mu2, r2)):
        stat_ref[i] = jnp.broadcast_to(stat, (images, 128))


def normal_parts(h):
    a = jnp.abs(h)
    t = 1.0 / (1.0 + (0.3275911 / math.sqrt(2.0)) * a)
    series = 0.5 * 1.061405429
    for c in (-1.453152027, 1.421413741, -0.284496736, 0.254829592):
        series = series * t + 0.5 * c
    e = jnp.exp(-0.5 * h * h)
    tail = series * t * e
    phi = jnp.where(h < 0.0, tail, 1.0 - tail)
    return phi, phi + h * (e * (1.0 / math.sqrt(2.0 * math.pi)))


def dot(left, right, dims):
    return lax.dot_general(left, right, (dims, ((), ())), preferred_element_type=f32)


def hidden_kernel(place_ref, own_ref, oth_ref, bias_ref, *refs):
    w_refs, (act_ref, slope_ref, grad_ref, w_ref, h_ref) = refs[:BLOCKS], refs[BLOCKS:]
    j = pl.program_id(0)

    @pl.when(j == 0)
    def _():
        for k in range(BLOCKS):
            w_ref[k // 2, :, (k % 2) * 128 : (k % 2 + 1) * 128] = w_refs[k][...]

    bias = jnp.concatenate(
        [bias_ref[pl.ds(place_ref[2 * j], 1), :], bias_ref[pl.ds(place_ref[2 * j + 1], 1), :]], axis=1
    )
    weight = w_ref[j]
    grad = None
    for r, sb_ref in enumerate((own_ref, oth_ref)):
        h_ref[...] = dot(sb_ref[0], weight, ((1,), (0,))) + bias

        def tile(i, carry):
            rows = pl.ds(pl.multiple_of(i * 112, 16), 112)
            h = h_ref[rows, :]
            phi, slope = normal_parts(h)
            act_ref[r, rows, :] = (h * phi).astype(bf16)
            slope_ref[r, rows, :] = slope.astype(bf16)
            return carry

        lax.fori_loop(0, h_ref.shape[0] // 112, tile, 0)
        part = dot(sb_ref[1], act_ref[r], ((0,), (0,)))
        grad = part if grad is None else grad + part
    for k in range(2):
        grad_ref[k] = grad[:, k * 128 : (k + 1) * 128].astype(bf16)


def slope_kernel(place_ref, own_ref, oth_ref, slope_ref, *refs):
    w_refs, (hg_ref, grad_ref, sums_ref, w_ref) = refs[:BLOCKS], refs[BLOCKS:]
    j = pl.program_id(0)

    @pl.when(j == 0)
    def _():
        sums_ref[...] = jnp.zeros_like(sums_ref)
        for k in range(BLOCKS):
            w_ref[k // 2, :, (k % 2) * 128 : (k % 2 + 1) * 128] = w_refs[k][...]

    weight = w_ref[j]
    grad = sums = None
    for r, sb_ref in enumerate((own_ref, oth_ref)):
        back = dot(sb_ref[1], weight, ((1,), (0,)))
        low = (back * slope_ref[r].astype(f32)).astype(bf16)
        hg_ref[r] = low
        column = jnp.sum(low.astype(f32), axis=0, keepdims=True)
        part = dot(sb_ref[0], low, ((0,), (0,)))
        grad = part if grad is None else grad + part
        sums = column if sums is None else sums + column
    for k in range(2):
        grad_ref[k] = grad[:, k * 128 : (k + 1) * 128].astype(bf16)
        sums_ref[pl.ds(place_ref[2 * j + k], 1), :] = sums[:, k * 128 : (k + 1) * 128]


def back_kernel(act_ref, hg_ref, *refs):
    a_refs, b_refs, (out_ref,) = refs[:BLOCKS], refs[BLOCKS : 2 * BLOCKS], refs[2 * BLOCKS :]
    for i, (left_ref, w_refs) in enumerate(((act_ref, b_refs), (hg_ref, a_refs))):
        total = None
        for j in range(PAIRS):
            weight = jnp.concatenate([w_refs[2 * j][...], w_refs[2 * j + 1][...]], axis=1)
            part = dot(left_ref[0, :, j * 256 : (j + 1) * 256], weight, ((1,), (1,)))
            total = part if total is None else total + part
        out_ref[i] = total.astype(out_ref.dtype)


def post_kernel(
    counts_ref, x_ref, cot_ref, vec_ref, q_ref, stat_ref, own_ref, got_ref,
    out_ref, grad_ref, sums_ref, t_ref, h_ref,
):
    pixels, images, width = x_ref.shape
    size = pixels * width
    zero = jnp.zeros((images, width), f32)
    gate = valid_gate(counts_ref, (images, width))
    mu1, r1, mu2, r2 = (stat_ref[i][:, 0:1] for i in range(4))
    gain1, mix, gain2, scale, lower = (vec_ref[i : i + 1, :] for i in (0, 2, 3, 5, 6))
    lift = mix * (r1 * gain1)

    def loop(body, init):
        return lax.fori_loop(0, pixels, body, init, unroll=7)

    def column(values):
        return jnp.sum(values, axis=0, keepdims=True)

    def first(p, carry):
        g_scale, g_lower, g_gain2, g_shift2 = carry
        middle = x_ref[p] + lift * q_ref[p]
        branch = own_ref[0, p] + got_ref[0, p].astype(f32) + lower
        out_ref[p] = middle + scale * branch
        weighted = cot_ref[p].astype(f32) * gate
        back = own_ref[1, p] + got_ref[1, p].astype(f32)
        h2 = (middle - mu2) * r2
        return (g_scale + weighted * branch, g_lower + weighted, g_gain2 + back * h2, g_shift2 + back)

    g_scale, g_lower, g_gain2, g_shift2 = loop(first, (zero,) * 4)
    mean2 = row_total(g_shift2 * gain2) / size
    mean2h = row_total(g_gain2 * gain2) / size

    def second(p, g_mix):
        middle = x_ref[p] + lift * q_ref[p]
        back = own_ref[1, p] + got_ref[1, p].astype(f32)
        h2 = (middle - mu2) * r2
        grad = cot_ref[p].astype(f32) * gate + r2 * (back * gain2 - mean2 - h2 * mean2h)
        grad_ref[p] = grad
        t_ref[p] = grad * mix
        return g_mix + grad * q_ref[p]

    g_mix = loop(second, zero) * (r1 * gain1)
    for p in range(pixels):
        h_ref[p] = along_row(lambda i: t_ref[i] * near_share(i), p)
    g_gain1 = g_shift1 = zero
    for p in range(pixels):
        ng = along_col(lambda i: h_ref[i], p) - t_ref[p]
        t_ref[p] = ng
        g_gain1 = g_gain1 + ng * ((x_ref[p] - mu1) * r1)
        g_shift1 = g_shift1 + ng
    mean1 = row_total(g_shift1 * gain1) / size
    mean1h = row_total(g_gain1 * gain1) / size

    def third(p, carry):
        h1 = (x_ref[p] - mu1) * r1
        grad_ref[p] = grad_ref[p] + r1 * (t_ref[p] * gain1 - mean1 - h1 * mean1h)
        return carry

    loop(third, 0)
    for i, total in enumerate((g_gain1, g_shift1, g_mix, g_gain2, g_shift2, g_scale, g_lower * scale)):
        sums_ref[i : i + 1, :] = column(total)


def call(kernel, outs, ins, scratch=(), vmem=48, **kw):
    return pl.pallas_call(
        kernel,
        out_shape=outs,
        scratch_shapes=list(scratch),
        compiler_params=pltpu.CompilerParams(vmem_limit_bytes=vmem * 2**20),
        **kw,
    )(*ins)


def struct(shape, dtype=f32):
    return jax.ShapeDtypeStruct(shape, dtype)


def joint(change):
    return [(n * 16 + w, n * 16 + change(n, w)) for n in range(2) for w in range(16)]


BOTH = ("narrow", "wide")


def flip(values, bit):
    return lax.ppermute(values, "wide", [(w, w ^ bit) for w in range(16)])


def far(values):
    return lax.ppermute(values, BOTH, joint(lambda n, w: w ^ (12 if n else 8)))


def across(values):
    return lax.ppermute(values, "narrow", [(0, 1), (1, 0)])


def gather_blocks(own):
    z1 = flip(own, 4)
    zf = far(own)
    y0 = flip(own, 2)
    y1 = flip(z1, 2)
    yf = flip(zf, 2)
    zo = across(zf)
    yo = across(yf)
    return [own, z1, zf, zo, y0, y1, yf, yo]


def reduce_blocks(g):
    x = across(jnp.stack([g[3], g[7]]))
    y = flip(g[4:6], 2)
    wide = lambda v: v.astype(f32)
    yf = flip((wide(g[6]) + wide(x[1])).astype(bf16), 2)
    z1 = flip((wide(g[1]) + wide(y[1])).astype(bf16), 4)
    zf = far((wide(g[2]) + wide(x[0]) + wide(yf)).astype(bf16))
    own = (wide(g[0]) + wide(y[0]) + wide(z1) + wide(zf)).astype(bf16)
    return wide(own) + wide(across(own))


def sum_all(values):
    for bit in (1, 2):
        values = values + flip(values, bit)
    values = values + across(values)
    for bit in (4, 8):
        values = values + flip(values, bit)
    return values


def local_tree(
    features,
    cotangent,
    counts,
    hidden_weight,
    hidden_bias,
    output_weight,
    vectors,
    hidden_moment,
    hidden_square,
    bias_moment,
    bias_square,
    output_moment,
    output_square,
    vector_moment,
    vector_square,
):
    images, pixels, width = features.shape
    rows = images * pixels
    units = hidden_weight.shape[1]
    near, wide = lax.axis_index("narrow"), lax.axis_index("wide")
    first_far = jnp.where(near == 0, 8, 12)
    marks = jnp.stack([0 * first_far, 0 * first_far + 4, first_far, 20 - first_far])
    place = wide ^ jnp.concatenate([marks, marks ^ 2])
    place = place.astype(jnp.int32)

    x = features.transpose(1, 0, 2)
    cot = cotangent.transpose(1, 0, 2)
    a_blocks = gather_blocks(hidden_weight.astype(bf16))
    b_blocks = gather_blocks(output_weight.T.astype(bf16))
    big = struct((pixels, images, width))
    keep = pltpu.VMEM((pixels, images, width), f32)
    sb, q, stat = call(
        pre_kernel,
        [struct((2, pixels, images, width), bf16), big, struct((4, images, 128))],
        (counts, x, cot, vectors),
        [keep, keep],
        in_specs=[SMEM, VMEM, VMEM, VMEM],
        out_specs=[VMEM] * 3,
    )
    sb = sb.reshape(2, rows, width)
    other = flip(sb, 1)
    bias = hidden_bias.reshape(-1, 128)
    tall = pl.BlockSpec((2, rows, 256), lambda j: (0, 0, j))
    pair = pl.BlockSpec((2, width, 128), lambda j: (j, 0, 0))
    hidden = struct((2, rows, BLOCKS * 128), bf16)
    grads = struct((BLOCKS, width, 128), bf16)
    w_keep = pltpu.VMEM((PAIRS, width, 256), bf16)
    active, slope, out_part = call(
        hidden_kernel,
        [hidden, hidden, grads],
        (place, sb, other, bias, *a_blocks),
        [w_keep, pltpu.VMEM((rows, 256), f32)],
        grid=(PAIRS,),
        in_specs=[SMEM] + [VMEM] * (3 + BLOCKS),
        out_specs=[tall, tall, pair],
    )
    hidden_grad, hidden_part, bias_part = call(
        slope_kernel,
        [hidden, grads, struct(bias.shape)],
        (place, sb, other, slope, *b_blocks),
        [w_keep],
        grid=(PAIRS,),
        in_specs=[SMEM, VMEM, VMEM, tall] + [VMEM] * BLOCKS,
        out_specs=[tall, pair, pl.BlockSpec(bias.shape, lambda j: (0, 0))],
    )

    def back(r, dtype):
        half = pl.BlockSpec((1, rows, BLOCKS * 128), lambda j: (r, 0, 0))
        return call(
            back_kernel,
            struct((2, rows, width), dtype),
            (active, hidden_grad, *a_blocks, *b_blocks),
            grid=(1,),
            in_specs=[half, half] + [VMEM] * (2 * BLOCKS),
            out_specs=VMEM,
        )

    got = flip(back(1, bf16), 1).reshape(2, pixels, images, width)
    mine = back(0, f32).reshape(2, pixels, images, width)
    block_out, input_grad, vector_part = call(
        post_kernel,
        [big, big, struct((7, width))],
        (counts, x, cot, vectors, q, stat, mine, got),
        [keep, keep],
        in_specs=[SMEM] + [VMEM] * 7,
        out_specs=[VMEM] * 3,
    )
    output_grad = reduce_blocks(out_part).T
    weight_grad = reduce_blocks(hidden_part)
    sums = sum_all(jnp.concatenate([bias_part, vector_part.reshape(-1, 128)]))
    split = bias.shape[0]
    bias_grad = sums[:split].reshape(hidden_bias.shape)
    vector_grad = sums[split:].reshape(vectors.shape)
    hidden_new = adamw_update(
        hidden_weight, weight_grad, hidden_moment, hidden_square, 0.04, weight_shrink
    )
    bias_new = adamw_update(hidden_bias, bias_grad, bias_moment, bias_square, 0.2, 0.0)
    output_new = adamw_update(
        output_weight, output_grad, output_moment, output_square, 0.02, weight_shrink
    )
    vector_new = adamw_update(vectors, vector_grad, vector_moment, vector_square, 0.3, 0.0)
    return (
        block_out.transpose(1, 0, 2),
        input_grad.transpose(1, 0, 2),
        *hidden_new,
        *bias_new,
        *output_new,
        *vector_new,
    )


def solution(mesh):
    in_specs = (
        P(("narrow", "wide"), None, None),
        P(("narrow", "wide"), None, None),
        P(("narrow", "wide")),
        P(None, "wide"),
        P(),
        P("wide", None),
        P(),
        P(None, "wide"),
        P(None, "wide"),
        P(),
        P(),
        P("wide", None),
        P("wide", None),
        P(),
        P(),
    )
    out_specs = (
        P(("narrow", "wide"), None, None),
        P(("narrow", "wide"), None, None),
        P(None, "wide"),
        P(None, "wide"),
        P(None, "wide"),
        P(),
        P(),
        P(),
        P("wide", None),
        P("wide", None),
        P("wide", None),
        P(),
        P(),
        P(),
    )
    body = local_tree if dict(mesh.shape) == {"narrow": 2, "wide": 16} else local
    return jax.shard_map(body, mesh=mesh, in_specs=in_specs, out_specs=out_specs, check_vma=False)
```

```python
import functools
import math

import jax
import jax.numpy as jnp
from jax import lax
from jax.experimental import pallas as pl
from jax.experimental.pallas import tpu as pltpu
from jax.sharding import PartitionSpec as P

SIDE = 7
STEP = 5


norm_epsilon = 1e-05
first_decay = 0.9
second_decay = 0.999
adam_epsilon = 1e-08
weight_shrink = 0.05


def pool_matrix(side):
    places = jnp.arange(side * side, dtype=jnp.int32)
    place_row = places // side
    place_col = places % side
    nearby = (jnp.abs(place_row[:, None] - place_row[None, :]) <= 1) & (
        jnp.abs(place_col[:, None] - place_col[None, :]) <= 1
    )
    nearby = nearby.astype(jnp.float32)
    return nearby / jnp.sum(nearby, axis=1, keepdims=True)


def norm_parts(values, gain, shift):
    centre = jnp.mean(values, axis=(1, 2), keepdims=True)
    spread = jnp.mean((values - centre) ** 2, axis=(1, 2), keepdims=True)
    inverse = lax.rsqrt(spread + norm_epsilon)
    scaled = (values - centre) * inverse
    return (scaled * gain + shift, scaled, inverse)


def norm_back(upstream, scaled, inverse):
    first_mean = jnp.mean(upstream, axis=(1, 2), keepdims=True)
    second_mean = jnp.mean(upstream * scaled, axis=(1, 2), keepdims=True)
    return inverse * (upstream - first_mean - scaled * second_mean)


def gelu_slope(values):
    return 0.5 * (1.0 + lax.erf(values / math.sqrt(2.0))) + values * jnp.exp(
        -0.5 * values * values
    ) / math.sqrt(2.0 * math.pi)


def contract_rows(left, right):
    return lax.dot_general(
        left, right, (((0,), (0,)), ((), ())), preferred_element_type=jnp.float32
    )


def contract_cols(left, right):
    return lax.dot_general(
        left, right, (((1,), (1,)), ((), ())), preferred_element_type=jnp.float32
    )


def adamw_update(param, grad, moment, square, rate, shrink):
    moment_new = first_decay * moment + (1.0 - first_decay) * grad
    square_new = second_decay * square + (1.0 - second_decay) * grad * grad
    moment_hat = moment_new / (1.0 - first_decay**STEP)
    square_hat = square_new / (1.0 - second_decay**STEP)
    param_new = param - rate * (moment_hat / (jnp.sqrt(square_hat) + adam_epsilon) + shrink * param)
    return (param_new, moment_new, square_new)


def local(
    features,
    cotangent,
    counts,
    hidden_weight,
    hidden_bias,
    output_weight,
    vectors,
    hidden_moment,
    hidden_square,
    bias_moment,
    bias_square,
    output_moment,
    output_square,
    vector_moment,
    vector_square,
):
    images, pixels, width = features.shape
    rows = images * pixels
    units = hidden_weight.shape[1]
    pool = pool_matrix(SIDE)
    valid = (jnp.arange(images, dtype=jnp.int32) < counts[0]).astype(jnp.float32)
    weighted = cotangent.astype(jnp.float32) * valid[:, None, None]
    normed, first_scaled, first_inverse = norm_parts(features, vectors[0], vectors[1])
    mixed = jnp.einsum("pq,iqc->ipc", pool, normed, precision=lax.Precision.HIGHEST) - normed
    middle = features + vectors[2] * mixed
    second, second_scaled, second_inverse = norm_parts(middle, vectors[3], vectors[4])
    second_low = second.reshape(rows, width).astype(jnp.bfloat16)
    hidden_low = hidden_weight.astype(jnp.bfloat16)
    output_low = output_weight.astype(jnp.bfloat16)
    branch_grad = (weighted * vectors[5]).reshape(rows, width)
    branch_low = branch_grad.astype(jnp.bfloat16)
    offset = lax.axis_index("wide") * units
    local_bias = lax.dynamic_slice_in_dim(hidden_bias, offset, units)
    hidden_all = (
        jnp.dot(
            lax.all_gather(second_low, "wide", axis=0, tiled=True),
            hidden_low,
            preferred_element_type=jnp.float32,
        )
        + local_bias
    )
    active_all = jax.nn.gelu(hidden_all, approximate=False).astype(jnp.bfloat16)
    slope_all = gelu_slope(hidden_all)
    block = active_all
    branch = lax.psum_scatter(
        jnp.dot(block, output_low, preferred_element_type=jnp.float32),
        "wide",
        scatter_dimension=0,
        tiled=True,
    )
    piece = lax.all_gather(branch_low, "wide", axis=0, tiled=True)
    block = active_all
    output_total = contract_rows(block, piece)
    active_grad = contract_cols(piece, output_low)
    hidden_grad = (active_grad * slope_all).astype(jnp.bfloat16)
    local_bias_grad = jnp.sum(hidden_grad.astype(jnp.float32), axis=0)
    bias_part = lax.dynamic_update_slice_in_dim(
        jnp.zeros(hidden_bias.shape, jnp.float32), local_bias_grad, offset, 0
    )
    block = hidden_grad
    second_grad = lax.psum_scatter(
        contract_cols(block, hidden_low), "wide", scatter_dimension=0, tiled=True
    )
    block = hidden_grad
    hidden_part = contract_rows(lax.all_gather(second_low, "wide", axis=0, tiled=True), block)
    branch_full = (branch + vectors[6]).reshape(images, pixels, width)
    block_out = middle + vectors[5] * branch_full
    grad_scale_two = jnp.sum(weighted * branch_full, axis=(0, 1))
    grad_shift_out = jnp.sum(branch_grad, axis=0)
    second_grad = second_grad.reshape(images, pixels, width)
    grad_gain_two = jnp.sum(second_grad * second_scaled, axis=(0, 1))
    grad_shift_two = jnp.sum(second_grad, axis=(0, 1))
    middle_grad = weighted + norm_back(second_grad * vectors[3], second_scaled, second_inverse)
    grad_scale_one = jnp.sum(middle_grad * mixed, axis=(0, 1))
    mixed_grad = middle_grad * vectors[2]
    normed_grad = (
        jnp.einsum("qp,iqc->ipc", pool, mixed_grad, precision=lax.Precision.HIGHEST) - mixed_grad
    )
    grad_gain_one = jnp.sum(normed_grad * first_scaled, axis=(0, 1))
    grad_shift_one = jnp.sum(normed_grad, axis=(0, 1))
    input_grad = middle_grad + norm_back(normed_grad * vectors[0], first_scaled, first_inverse)
    vector_part = jnp.stack(
        [
            grad_gain_one,
            grad_shift_one,
            grad_scale_one,
            grad_gain_two,
            grad_shift_two,
            grad_scale_two,
            grad_shift_out,
        ]
    )
    vector_grad, bias_grad = lax.psum((vector_part, bias_part), ("narrow", "wide"))
    hidden_grad_sum, output_grad_sum = lax.psum((hidden_part, output_total), "narrow")
    hidden_new = adamw_update(
        hidden_weight, hidden_grad_sum, hidden_moment, hidden_square, 0.04, weight_shrink
    )
    bias_new = adamw_update(hidden_bias, bias_grad, bias_moment, bias_square, 0.2, 0.0)
    output_new = adamw_update(
        output_weight, output_grad_sum, output_moment, output_square, 0.02, weight_shrink
    )
    vector_new = adamw_update(vectors, vector_grad, vector_moment, vector_square, 0.3, 0.0)
    return (
        block_out,
        input_grad,
        hidden_new[0],
        hidden_new[1],
        hidden_new[2],
        bias_new[0],
        bias_new[1],
        bias_new[2],
        output_new[0],
        output_new[1],
        output_new[2],
        vector_new[0],
        vector_new[1],
        vector_new[2],
    )


f32 = jnp.float32
bf16 = jnp.bfloat16
VMEM = pl.BlockSpec(memory_space=pltpu.VMEM)
SMEM = pl.BlockSpec(memory_space=pltpu.SMEM)


def row_total(values):
    return jnp.sum(values, axis=1, keepdims=True)


def span(i):
    return min(i + 1, SIDE - 1) - max(i - 1, 0) + 1


def near_share(p):
    return 1.0 / (span(p // SIDE) * span(p % SIDE))


def along_row(load, p):
    c = p % SIDE
    total = load(p)
    if c > 0:
        total = total + load(p - 1)
    if c < SIDE - 1:
        total = total + load(p + 1)
    return total


def along_col(load, p):
    r = p // SIDE
    total = load(p)
    if r > 0:
        total = total + load(p - SIDE)
    if r < SIDE - 1:
        total = total + load(p + SIDE)
    return total


def valid_gate(counts_ref, shape):
    slots = lax.broadcasted_iota(jnp.int32, shape, 0)
    return jnp.where(slots < counts_ref[0], 1.0, 0.0)


def pre_kernel(counts_ref, x_ref, cot_ref, vec_ref, sb_ref, q_ref, stat_ref, d_ref, h_ref):
    pixels, images, width = x_ref.shape
    size = pixels * width
    zero = jnp.zeros((images, width), f32)

    def loop(body, init):
        return lax.fori_loop(0, pixels, body, init, unroll=7)

    mu1 = row_total(loop(lambda p, s: s + x_ref[p], zero)) / size

    def centre(p, s):
        d = x_ref[p] - mu1
        d_ref[p] = d
        return s + d * d

    r1 = lax.rsqrt(row_total(loop(centre, zero)) / size + norm_epsilon)
    for p in range(pixels):
        h_ref[p] = along_row(lambda i: d_ref[i], p)
    lift = vec_ref[2:3, :] * (r1 * vec_ref[0:1, :])
    total = zero
    for p in range(pixels):
        q = along_col(lambda i: h_ref[i], p) * near_share(p) - d_ref[p]
        q_ref[p] = q
        total = total + (x_ref[p] + lift * q)
    mu2 = row_total(total) / size

    def spread(p, s):
        d = x_ref[p] + lift * q_ref[p] - mu2
        d_ref[p] = d
        return s + d * d

    r2 = lax.rsqrt(row_total(loop(spread, zero)) / size + norm_epsilon)
    scale = r2 * vec_ref[3:4, :]
    shift = jnp.broadcast_to(vec_ref[4:5, :], (images, width))
    gate = valid_gate(counts_ref, (images, width)) * vec_ref[5:6, :]

    def finish(p, carry):
        sb_ref[0, p] = (d_ref[p] * scale + shift).astype(bf16)
        sb_ref[1, p] = (cot_ref[p].astype(f32) * gate).astype(bf16)
        return carry

    loop(finish, 0)
    for i, stat in enumerate((mu1, r1, mu2, r2)):
        stat_ref[i] = jnp.broadcast_to(stat, (images, 128))


def normal_parts(h):
    d = 1.0 + (0.3275911 / math.sqrt(2.0)) * jnp.abs(h)
    t = pl.reciprocal(d, approx=True)
    t = t * (2.0 - d * t)
    series = 0.5 * 1.061405429
    for c in (-1.453152027, 1.421413741, -0.284496736, 0.254829592):
        series = series * t + 0.5 * c
    e = jnp.exp2((-0.5 * math.log2(math.e)) * (h * h))
    tail = series * t * e
    phi = jnp.where(h < 0.0, tail, 1.0 - tail)
    return phi, phi + h * (e * (1.0 / math.sqrt(2.0 * math.pi)))


def dot(left, right, dims):
    return lax.dot_general(left, right, (dims, ((), ())), preferred_element_type=f32)


def side_by_side(refs, j):
    left, right = refs[2 * j], refs[2 * j + 1]
    return jnp.concatenate([left[...], right[...]], axis=1)


def cast_kernel(a_ref, b_ref, out_ref):
    out_ref[0] = a_ref[...].astype(bf16)
    out_ref[1] = b_ref[...].T.astype(bf16)


def block_kernel(first, count, started, place_ref, own_ref, oth_ref, bias_ref, *refs):
    w_refs, refs = refs[:count], refs[count:]
    old, refs = (refs[:2], refs[2:]) if started else (None, refs)
    totals, sums_ref, outs = refs[:2], refs[2], refs[3:]
    sums_ref[...] = jnp.zeros_like(sums_ref)
    sides = (own_ref, oth_ref)
    runs = [[None, None], [None, None]]
    for j in range(count // 2):
        lines = [pl.ds(place_ref[first + 2 * j + k], 1) for k in range(2)]
        bias = jnp.concatenate([bias_ref[line, :] for line in lines], axis=1)
        a, b = (jnp.concatenate([w_refs[2 * j + k][i] for k in range(2)], axis=1) for i in range(2))
        grads = [None, None]
        sums = None
        for r, sb_ref in enumerate(sides):
            h = dot(sb_ref[0], a, ((1,), (0,))) + bias
            back = dot(sb_ref[1], b, ((1,), (0,)))
            phi, slope = normal_parts(h)
            active = (h * phi).astype(bf16)
            low = (back * slope).astype(bf16)
            column = jnp.sum(low.astype(f32), axis=0, keepdims=True)
            sums = column if r == 0 else sums + column
            for i, (left, right) in enumerate(((sb_ref[0], low), (sb_ref[1], active))):
                part = dot(left, right, ((0,), (0,)))
                grads[i] = part if r == 0 else grads[i] + part
            for i, (left, right) in enumerate(((active, b), (low, a))):
                part = dot(left, right, ((1,), (1,)))
                runs[r][i] = part if j == 0 else runs[r][i] + part
        for k in range(2):
            half = slice(k * 128, (k + 1) * 128)
            sums_ref[lines[k], :] = sums[:, half]
            for i, grad in enumerate(grads):
                outs[2 * j + k][i] = grad[:, half].astype(outs[2 * j + k].dtype)
    for r, total_ref in enumerate(totals):
        for i in range(2):
            total = runs[r][i] if old is None else old[r][i] + runs[r][i]
            total_ref[i] = total.astype(total_ref.dtype)


def update_kernel(own_ref, got_ref, sums_ref, *refs):
    state, outs = [refs[i : i + 3] for i in range(0, 12, 3)], refs[12:]
    grads = own_ref[...].astype(f32) + got_ref[...].astype(f32)
    lines = state[1][0].shape[0]
    wide = [
        jnp.concatenate([sums_ref[lines + 4 * i + k : lines + 4 * i + k + 1, :] for k in range(4)], axis=1)
        for i in range(state[3][0].shape[0])
    ]
    settings = (
        (grads[0], 0.04, weight_shrink),
        (sums_ref[:lines, :], 0.2, 0.0),
        (grads[1].T, 0.02, weight_shrink),
        (jnp.concatenate(wide, axis=0), 0.3, 0.0),
    )
    for n, (grad, rate, shrink) in enumerate(settings):
        param, moment, square = (ref[...] for ref in state[n])
        new = adamw_update(param, grad, moment, square, rate, shrink)
        for ref, values in zip(outs[3 * n : 3 * n + 3], new):
            ref[...] = values


def post_kernel(
    counts_ref, x_ref, cot_ref, vec_ref, q_ref, stat_ref, own_ref, got_ref, *refs
):
    bias_refs, (out_ref, grad_ref, sums_ref, t_ref, h_ref) = refs[:-5], refs[-5:]
    pixels, images, width = x_ref.shape
    size = pixels * width
    zero = jnp.zeros((images, width), f32)
    gate = valid_gate(counts_ref, (images, width))
    mu1, r1, mu2, r2 = (stat_ref[i][:, 0:1] for i in range(4))
    gain1, mix, gain2, scale, lower = (vec_ref[i : i + 1, :] for i in (0, 2, 3, 5, 6))
    lift = mix * (r1 * gain1)

    def loop(body, init):
        return lax.fori_loop(0, pixels, body, init, unroll=7)

    def column(values):
        return jnp.sum(values, axis=0, keepdims=True)

    def first(p, carry):
        g_scale, g_lower, g_gain2, g_shift2 = carry
        middle = x_ref[p] + lift * q_ref[p]
        branch = own_ref[0, p] + got_ref[0, p].astype(f32) + lower
        out_ref[p] = middle + scale * branch
        weighted = cot_ref[p].astype(f32) * gate
        back = own_ref[1, p] + got_ref[1, p].astype(f32)
        h2 = (middle - mu2) * r2
        return (g_scale + weighted * branch, g_lower + weighted, g_gain2 + back * h2, g_shift2 + back)

    g_scale, g_lower, g_gain2, g_shift2 = loop(first, (zero,) * 4)
    mean2 = row_total(g_shift2 * gain2) / size
    mean2h = row_total(g_gain2 * gain2) / size

    def second(p, g_mix):
        middle = x_ref[p] + lift * q_ref[p]
        back = own_ref[1, p] + got_ref[1, p].astype(f32)
        h2 = (middle - mu2) * r2
        grad = cot_ref[p].astype(f32) * gate + r2 * (back * gain2 - mean2 - h2 * mean2h)
        grad_ref[p] = grad
        t_ref[p] = grad * mix
        return g_mix + grad * q_ref[p]

    g_mix = loop(second, zero) * (r1 * gain1)
    for p in range(pixels):
        h_ref[p] = along_row(lambda i: t_ref[i] * near_share(i), p)
    g_gain1 = g_shift1 = zero
    for p in range(pixels):
        ng = along_col(lambda i: h_ref[i], p) - t_ref[p]
        t_ref[p] = ng
        g_gain1 = g_gain1 + ng * ((x_ref[p] - mu1) * r1)
        g_shift1 = g_shift1 + ng
    mean1 = row_total(g_shift1 * gain1) / size
    mean1h = row_total(g_gain1 * gain1) / size

    def third(p, carry):
        h1 = (x_ref[p] - mu1) * r1
        grad_ref[p] = grad_ref[p] + r1 * (t_ref[p] * gain1 - mean1 - h1 * mean1h)
        return carry

    loop(third, 0)
    lines = bias_refs[0].shape[0]
    sums_ref[:lines, :] = bias_refs[0][...] + bias_refs[1][...] + bias_refs[2][...]
    for i, total in enumerate((g_gain1, g_shift1, g_mix, g_gain2, g_shift2, g_scale, g_lower * scale)):
        total = column(total)
        for k in range(width // 128):
            row = lines + (width // 128) * i + k
            sums_ref[row : row + 1, :] = total[:, k * 128 : (k + 1) * 128]


def call(kernel, outs, ins, scratch=(), vmem=12, flops=0, smem=0, hold=True):
    many = isinstance(outs, (list, tuple))
    arrays = (*ins, *(outs if many else [outs]))
    moved = sum(math.prod(v.shape) * v.dtype.itemsize for v in arrays)
    if hold:
        outs = [pltpu.VMEM(v.shape, v.dtype) for v in outs] if many else pltpu.VMEM(outs.shape, outs.dtype)
        ins = [v if i < smem else pltpu.with_memory_space_constraint(v, pltpu.VMEM) for i, v in enumerate(ins)]
    return pl.pallas_call(
        kernel,
        out_shape=outs,
        in_specs=[SMEM] * smem + [VMEM] * (len(ins) - smem),
        out_specs=[VMEM] * len(outs) if many else VMEM,
        scratch_shapes=list(scratch),
        name=getattr(kernel, "func", kernel).__name__,
        compiler_params=pltpu.CompilerParams(vmem_limit_bytes=vmem * 2**20),
        cost_estimate=pl.CostEstimate(flops=flops, bytes_accessed=moved, transcendentals=0),
    )(*ins)


def struct(shape, dtype=f32):
    return jax.ShapeDtypeStruct(shape, dtype)


BOTH = ("narrow", "wide")


def joint(values, change):
    pairs = [(n * 16 + w, change(n, w)) for n in range(2) for w in range(16)]
    return lax.ppermute(values, BOTH, [(s, n * 16 + w) for s, (n, w) in pairs])


def flip(values, bit):
    return lax.ppermute(values, "wide", [(w, w ^ bit) for w in range(16)])


def far(values):
    return joint(values, lambda n, w: (n, w ^ (12 if n else 8)))


def across(values):
    return lax.ppermute(values, "narrow", [(0, 1), (1, 0)])


def diagonal(values):
    return joint(values, lambda n, w: (1 - n, w ^ 2))


def after(values, *others):
    return lax.optimization_barrier((values, *others))[0]


def wide_sum(*parts):
    total = parts[0].astype(f32)
    for part in parts[1:]:
        total = total + part.astype(f32)
    return total


def local_tree(
    features,
    cotangent,
    counts,
    hidden_weight,
    hidden_bias,
    output_weight,
    vectors,
    hidden_moment,
    hidden_square,
    bias_moment,
    bias_square,
    output_moment,
    output_square,
    vector_moment,
    vector_square,
):
    images, pixels, width = features.shape
    rows = images * pixels
    units = hidden_weight.shape[1]
    near, wide = lax.axis_index("narrow"), lax.axis_index("wide")
    first_far = jnp.where(near == 0, 8, 12)
    last_far = 20 - first_far
    zero = 0 * first_far
    place = [zero, zero + 4, first_far, zero + 2, zero + 6, first_far ^ 2, last_far, last_far ^ 2]
    place = (wide ^ jnp.stack(place)).astype(jnp.int32)

    pair, pair_f = struct((2, width, units), bf16), struct((2, width, units))
    w0 = call(cast_kernel, pair, (hidden_weight, output_weight))
    wz1, wzf, wy0 = flip(w0, 4), far(w0), flip(w0, 2)
    features, cotangent, wz1, wy0 = lax.optimization_barrier((features, cotangent, wz1, wy0))
    wy1 = flip(wz1, 2)
    x = features.transpose(1, 0, 2)
    cot = cotangent.transpose(1, 0, 2)
    big = struct((pixels, images, width))
    keep = pltpu.VMEM((pixels, images, width), f32)
    sb, q, stat = call(
        pre_kernel,
        [struct((2, pixels, images, width), bf16), big, struct((4, images, 128))],
        (counts, x, cot, vectors),
        [keep, keep],
        smem=1,
    )
    sb = after(sb.reshape(2, rows, width), wzf, wy1)
    other = flip(sb, 1)
    wyf, wzo, wyo = flip(wzf, 2), across(wzf), diagonal(wzf)
    bias = hidden_bias.reshape(-1, 128)
    total, total_low = struct((2, rows, width)), struct((2, rows, width), bf16)

    def blocks(first, weights, grads, old=(), last=False):
        return call(
            functools.partial(block_kernel, first, len(weights), bool(old)),
            [total, total_low if last else total, struct(bias.shape), *grads],
            (place, sb, other, bias, *weights, *old),
            smem=1,
            vmem=20,
        )

    *old, sums1, g0, gz1, gzf, gy0 = blocks(0, [w0, wz1, wzf, wy0], [pair_f] * 3 + [pair])
    wy1, wyf, _ = lax.optimization_barrier((wy1, wyf, old[0]))
    *old, sums2, gy1, gyf = blocks(4, [wy1, wyf], [pair, pair], old)
    yf = flip(gyf, 2)
    wzo, wyo, _ = lax.optimization_barrier((wzo, wyo, old[0]))
    mine, theirs, sums3, gzo, gyo = blocks(6, [wzo, wyo], [pair, pair], old, True)
    xs, ds, got = across(gzo), diagonal(gyo), flip(theirs, 1)
    y1, y0 = flip(after(gy1, got), 2), flip(after(gy0, got), 2)

    shape = (2, pixels, images, width)
    payload = struct((bias.shape[0] + vectors.size // 128, 128))
    block_out, input_grad, sums = call(
        post_kernel,
        [big, big, payload],
        (counts, x, cot, vectors, q, stat, mine.reshape(shape), got.reshape(shape), sums1, sums2, sums3),
        [keep, keep],
        smem=1,
        hold=False,
    )
    xs, yf, ds, _ = lax.optimization_barrier((xs, yf, ds, sums))
    sum_f = wide_sum(gzf, xs, yf, ds).astype(bf16)
    zf = far(sum_f)
    y1, y0, _ = lax.optimization_barrier((y1, y0, sum_f))
    z1 = flip(wide_sum(gz1, y1).astype(bf16), 4)
    for bit in (1, 4, 8):
        sums = sums + flip(sums, bit)
    own = wide_sum(g0, y0, z1, zf).astype(bf16)
    own, sums = lax.optimization_barrier((own, sums))
    got = across(own)
    sums = sums + across(sums)
    sums = sums + flip(sums, 2)
    state = (
        (hidden_weight, hidden_moment, hidden_square),
        tuple(v.reshape(bias.shape) for v in (hidden_bias, bias_moment, bias_square)),
        (output_weight, output_moment, output_square),
        (vectors, vector_moment, vector_square),
    )
    new = call(
        update_kernel,
        [struct(v.shape) for group in state for v in group],
        (own, got, sums, *(v for group in state for v in group)),
        hold=False,
    )
    hidden_new, output_new, vector_new = new[:3], new[6:9], new[9:]
    bias_new = [v.reshape(hidden_bias.shape) for v in new[3:6]]
    return (
        block_out.transpose(1, 0, 2),
        input_grad.transpose(1, 0, 2),
        *hidden_new,
        *bias_new,
        *output_new,
        *vector_new,
    )


def solution(mesh):
    in_specs = (
        P(("narrow", "wide"), None, None),
        P(("narrow", "wide"), None, None),
        P(("narrow", "wide")),
        P(None, "wide"),
        P(),
        P("wide", None),
        P(),
        P(None, "wide"),
        P(None, "wide"),
        P(),
        P(),
        P("wide", None),
        P("wide", None),
        P(),
        P(),
    )
    out_specs = (
        P(("narrow", "wide"), None, None),
        P(("narrow", "wide"), None, None),
        P(None, "wide"),
        P(None, "wide"),
        P(None, "wide"),
        P(),
        P(),
        P(),
        P("wide", None),
        P("wide", None),
        P("wide", None),
        P(),
        P(),
        P(),
    )
    body = local_tree if dict(mesh.shape) == {"narrow": 2, "wide": 16} else local
    return jax.shard_map(body, mesh=mesh, in_specs=in_specs, out_specs=out_specs, check_vma=False)
```

```python
import functools
import math

import jax
import jax.numpy as jnp
from jax import lax
from jax.experimental import pallas as pl
from jax.experimental.pallas import tpu as pltpu
from jax.sharding import PartitionSpec as P

SIDE = 7
STEP = 5


norm_epsilon = 1e-05
first_decay = 0.9
second_decay = 0.999
adam_epsilon = 1e-08
weight_shrink = 0.05


def pool_matrix(side):
    places = jnp.arange(side * side, dtype=jnp.int32)
    place_row = places // side
    place_col = places % side
    nearby = (jnp.abs(place_row[:, None] - place_row[None, :]) <= 1) & (
        jnp.abs(place_col[:, None] - place_col[None, :]) <= 1
    )
    nearby = nearby.astype(jnp.float32)
    return nearby / jnp.sum(nearby, axis=1, keepdims=True)


def norm_parts(values, gain, shift):
    centre = jnp.mean(values, axis=(1, 2), keepdims=True)
    spread = jnp.mean((values - centre) ** 2, axis=(1, 2), keepdims=True)
    inverse = lax.rsqrt(spread + norm_epsilon)
    scaled = (values - centre) * inverse
    return (scaled * gain + shift, scaled, inverse)


def norm_back(upstream, scaled, inverse):
    first_mean = jnp.mean(upstream, axis=(1, 2), keepdims=True)
    second_mean = jnp.mean(upstream * scaled, axis=(1, 2), keepdims=True)
    return inverse * (upstream - first_mean - scaled * second_mean)


def gelu_slope(values):
    return 0.5 * (1.0 + lax.erf(values / math.sqrt(2.0))) + values * jnp.exp(
        -0.5 * values * values
    ) / math.sqrt(2.0 * math.pi)


def contract_rows(left, right):
    return lax.dot_general(
        left, right, (((0,), (0,)), ((), ())), preferred_element_type=jnp.float32
    )


def contract_cols(left, right):
    return lax.dot_general(
        left, right, (((1,), (1,)), ((), ())), preferred_element_type=jnp.float32
    )


def adamw_update(param, grad, moment, square, rate, shrink):
    moment_new = first_decay * moment + (1.0 - first_decay) * grad
    square_new = second_decay * square + (1.0 - second_decay) * grad * grad
    moment_hat = moment_new / (1.0 - first_decay**STEP)
    square_hat = square_new / (1.0 - second_decay**STEP)
    param_new = param - rate * (moment_hat / (jnp.sqrt(square_hat) + adam_epsilon) + shrink * param)
    return (param_new, moment_new, square_new)


def local(
    features,
    cotangent,
    counts,
    hidden_weight,
    hidden_bias,
    output_weight,
    vectors,
    hidden_moment,
    hidden_square,
    bias_moment,
    bias_square,
    output_moment,
    output_square,
    vector_moment,
    vector_square,
):
    images, pixels, width = features.shape
    rows = images * pixels
    units = hidden_weight.shape[1]
    pool = pool_matrix(SIDE)
    valid = (jnp.arange(images, dtype=jnp.int32) < counts[0]).astype(jnp.float32)
    weighted = cotangent.astype(jnp.float32) * valid[:, None, None]
    normed, first_scaled, first_inverse = norm_parts(features, vectors[0], vectors[1])
    mixed = jnp.einsum("pq,iqc->ipc", pool, normed, precision=lax.Precision.HIGHEST) - normed
    middle = features + vectors[2] * mixed
    second, second_scaled, second_inverse = norm_parts(middle, vectors[3], vectors[4])
    second_low = second.reshape(rows, width).astype(jnp.bfloat16)
    hidden_low = hidden_weight.astype(jnp.bfloat16)
    output_low = output_weight.astype(jnp.bfloat16)
    branch_grad = (weighted * vectors[5]).reshape(rows, width)
    branch_low = branch_grad.astype(jnp.bfloat16)
    offset = lax.axis_index("wide") * units
    local_bias = lax.dynamic_slice_in_dim(hidden_bias, offset, units)
    hidden_all = (
        jnp.dot(
            lax.all_gather(second_low, "wide", axis=0, tiled=True),
            hidden_low,
            preferred_element_type=jnp.float32,
        )
        + local_bias
    )
    active_all = jax.nn.gelu(hidden_all, approximate=False).astype(jnp.bfloat16)
    slope_all = gelu_slope(hidden_all)
    block = active_all
    branch = lax.psum_scatter(
        jnp.dot(block, output_low, preferred_element_type=jnp.float32),
        "wide",
        scatter_dimension=0,
        tiled=True,
    )
    piece = lax.all_gather(branch_low, "wide", axis=0, tiled=True)
    block = active_all
    output_total = contract_rows(block, piece)
    active_grad = contract_cols(piece, output_low)
    hidden_grad = (active_grad * slope_all).astype(jnp.bfloat16)
    local_bias_grad = jnp.sum(hidden_grad.astype(jnp.float32), axis=0)
    bias_part = lax.dynamic_update_slice_in_dim(
        jnp.zeros(hidden_bias.shape, jnp.float32), local_bias_grad, offset, 0
    )
    block = hidden_grad
    second_grad = lax.psum_scatter(
        contract_cols(block, hidden_low), "wide", scatter_dimension=0, tiled=True
    )
    block = hidden_grad
    hidden_part = contract_rows(lax.all_gather(second_low, "wide", axis=0, tiled=True), block)
    branch_full = (branch + vectors[6]).reshape(images, pixels, width)
    block_out = middle + vectors[5] * branch_full
    grad_scale_two = jnp.sum(weighted * branch_full, axis=(0, 1))
    grad_shift_out = jnp.sum(branch_grad, axis=0)
    second_grad = second_grad.reshape(images, pixels, width)
    grad_gain_two = jnp.sum(second_grad * second_scaled, axis=(0, 1))
    grad_shift_two = jnp.sum(second_grad, axis=(0, 1))
    middle_grad = weighted + norm_back(second_grad * vectors[3], second_scaled, second_inverse)
    grad_scale_one = jnp.sum(middle_grad * mixed, axis=(0, 1))
    mixed_grad = middle_grad * vectors[2]
    normed_grad = (
        jnp.einsum("qp,iqc->ipc", pool, mixed_grad, precision=lax.Precision.HIGHEST) - mixed_grad
    )
    grad_gain_one = jnp.sum(normed_grad * first_scaled, axis=(0, 1))
    grad_shift_one = jnp.sum(normed_grad, axis=(0, 1))
    input_grad = middle_grad + norm_back(normed_grad * vectors[0], first_scaled, first_inverse)
    vector_part = jnp.stack(
        [
            grad_gain_one,
            grad_shift_one,
            grad_scale_one,
            grad_gain_two,
            grad_shift_two,
            grad_scale_two,
            grad_shift_out,
        ]
    )
    vector_grad, bias_grad = lax.psum((vector_part, bias_part), ("narrow", "wide"))
    hidden_grad_sum, output_grad_sum = lax.psum((hidden_part, output_total), "narrow")
    hidden_new = adamw_update(
        hidden_weight, hidden_grad_sum, hidden_moment, hidden_square, 0.04, weight_shrink
    )
    bias_new = adamw_update(hidden_bias, bias_grad, bias_moment, bias_square, 0.2, 0.0)
    output_new = adamw_update(
        output_weight, output_grad_sum, output_moment, output_square, 0.02, weight_shrink
    )
    vector_new = adamw_update(vectors, vector_grad, vector_moment, vector_square, 0.3, 0.0)
    return (
        block_out,
        input_grad,
        hidden_new[0],
        hidden_new[1],
        hidden_new[2],
        bias_new[0],
        bias_new[1],
        bias_new[2],
        output_new[0],
        output_new[1],
        output_new[2],
        vector_new[0],
        vector_new[1],
        vector_new[2],
    )


f32 = jnp.float32
bf16 = jnp.bfloat16
VMEM = pl.BlockSpec(memory_space=pltpu.VMEM)
SMEM = pl.BlockSpec(memory_space=pltpu.SMEM)


def row_total(values):
    return jnp.sum(values, axis=1, keepdims=True)


def span(i):
    return min(i + 1, SIDE - 1) - max(i - 1, 0) + 1


def near_share(p):
    return 1.0 / (span(p // SIDE) * span(p % SIDE))


def along_row(load, p):
    c = p % SIDE
    total = load(p)
    if c > 0:
        total = total + load(p - 1)
    if c < SIDE - 1:
        total = total + load(p + 1)
    return total


def along_col(load, p):
    r = p // SIDE
    total = load(p)
    if r > 0:
        total = total + load(p - SIDE)
    if r < SIDE - 1:
        total = total + load(p + SIDE)
    return total


def valid_gate(counts_ref, shape):
    slots = lax.broadcasted_iota(jnp.int32, shape, 0)
    return jnp.where(slots < counts_ref[0], 1.0, 0.0)


def mixed_parts(x_ref, mu1, r1, vec_ref, h_ref, q_ref):
    for p in range(x_ref.shape[0]):
        h_ref[p] = along_row(lambda i: x_ref[i] - mu1, p)
    for p in range(x_ref.shape[0]):
        q_ref[p] = along_col(lambda i: h_ref[i], p) * near_share(p) - (x_ref[p] - mu1)
    return vec_ref[2:3, :] * (r1 * vec_ref[0:1, :])


def pre_kernel(counts_ref, x_ref, cot_ref, vec_ref, sb_ref, stat_ref, d_ref, h_ref):
    pixels, images, width = x_ref.shape
    size = pixels * width
    zero = jnp.zeros((images, width), f32)

    def loop(body, init):
        return lax.fori_loop(0, pixels, body, init, unroll=7)

    mu1 = row_total(loop(lambda p, s: s + x_ref[p], zero)) / size

    def centre(p, s):
        d = x_ref[p] - mu1
        return s + d * d

    r1 = lax.rsqrt(row_total(loop(centre, zero)) / size + norm_epsilon)
    lift = mixed_parts(x_ref, mu1, r1, vec_ref, h_ref, d_ref)

    def middle(p, s):
        m = x_ref[p] + lift * d_ref[p]
        h_ref[p] = m
        return s + m

    total = loop(middle, zero)
    mu2 = row_total(total) / size

    def spread(p, s):
        d = h_ref[p] - mu2
        d_ref[p] = d
        return s + d * d

    r2 = lax.rsqrt(row_total(loop(spread, zero)) / size + norm_epsilon)
    scale = r2 * vec_ref[3:4, :]
    shift = jnp.broadcast_to(vec_ref[4:5, :], (images, width))
    gate = valid_gate(counts_ref, (images, width)) * vec_ref[5:6, :]

    def finish(p, carry):
        sb_ref[0, p] = (d_ref[p] * scale + shift).astype(bf16)
        sb_ref[1, p] = (cot_ref[p].astype(f32) * gate).astype(bf16)
        return carry

    loop(finish, 0)
    for i, stat in enumerate((mu1, r1, mu2, r2)):
        stat_ref[i] = jnp.broadcast_to(stat, (images, 128))


def normal_parts(h):
    d = 1.0 + (0.3275911 / math.sqrt(2.0)) * jnp.abs(h)
    t = pl.reciprocal(d, approx=True)
    t = t * (2.0 - d * t)
    series = 0.5 * 1.061405429
    for c in (-1.453152027, 1.421413741, -0.284496736, 0.254829592):
        series = series * t + 0.5 * c
    e = jnp.exp2((-0.5 * math.log2(math.e)) * (h * h))
    tail = series * t * e
    phi = jnp.where(h < 0.0, tail, 1.0 - tail)
    return phi, phi + h * (e * (1.0 / math.sqrt(2.0 * math.pi)))


def dot(left, right, dims):
    return lax.dot_general(left, right, (dims, ((), ())), preferred_element_type=f32)


def side_by_side(refs, j):
    left, right = refs[2 * j], refs[2 * j + 1]
    return jnp.concatenate([left[...], right[...]], axis=1)


def cast_kernel(a_ref, b_ref, out_ref):
    out_ref[0] = a_ref[...].astype(bf16)
    out_ref[1] = b_ref[...].T.astype(bf16)


def joined(refs, i):
    return jnp.concatenate([refs[0][i], refs[1][i]], axis=1)


def block_kernel(first, count, started, place_ref, own_ref, oth_ref, bias_ref, *refs):
    w_refs, refs = refs[:count], refs[count:]
    old, refs = (refs[:2], refs[2:]) if started else (None, refs)
    totals, sums_ref, outs = refs[:2], refs[2], refs[3:]
    sums_ref[...] = jnp.zeros_like(sums_ref)
    runs = [[None, None], [None, None]]
    for j in range(count // 2):
        lines = [pl.ds(place_ref[first + 2 * j + k], 1) for k in range(2)]
        bias = jnp.concatenate([bias_ref[line, :] for line in lines], axis=1)
        a, b = (joined(w_refs[2 * j : 2 * j + 2], i) for i in range(2))
        grads = [None, None]
        sums = None
        for r, sb_ref in enumerate((own_ref, oth_ref)):
            h = dot(sb_ref[0], a, ((1,), (0,))) + bias
            back = dot(sb_ref[1], b, ((1,), (0,)))
            phi, slope = normal_parts(h)
            active = (h * phi).astype(bf16)
            low = (back * slope).astype(bf16)
            column = jnp.sum(low.astype(f32), axis=0, keepdims=True)
            sums = column if r == 0 else sums + column
            for i, (left, right) in enumerate(((sb_ref[0], low), (sb_ref[1], active))):
                part = dot(left, right, ((0,), (0,)))
                grads[i] = part if r == 0 else grads[i] + part
            for i, (left, right) in enumerate(((active, b), (low, a))):
                part = dot(left, right, ((1,), (1,)))
                runs[r][i] = part if j == 0 else runs[r][i] + part
        for k in range(2):
            half = slice(k * 128, (k + 1) * 128)
            sums_ref[lines[k], :] = sums[:, half]
            for i, grad in enumerate(grads):
                if len(outs) == 2 * count:
                    outs[2 * k + i][...] = grad[:, half].astype(bf16)
                else:
                    outs[2 * j + k][i] = grad[:, half].astype(outs[2 * j + k].dtype)
    for r, total_ref in enumerate(totals):
        for i in range(2):
            total = runs[r][i] if old is None else old[r][i] + runs[r][i]
            total_ref[i] = total.astype(total_ref.dtype)


def update_kernel(own_ref, got_ref, sums_ref, *refs):
    state, outs = [refs[i : i + 3] for i in range(0, 12, 3)], refs[12:]
    grads = wide_sum(own_ref[...], got_ref[...])
    lines = state[1][0].shape[0]
    wide = [
        jnp.concatenate([sums_ref[lines + 4 * i + k : lines + 4 * i + k + 1, :] for k in range(4)], axis=1)
        for i in range(state[3][0].shape[0])
    ]
    settings = (
        (grads[0], 0.04, weight_shrink),
        (sums_ref[:lines, :], 0.2, 0.0),
        (grads[1].T, 0.02, weight_shrink),
        (jnp.concatenate(wide, axis=0), 0.3, 0.0),
    )
    for n, (grad, rate, shrink) in enumerate(settings):
        param, moment, square = (ref[...] for ref in state[n])
        new = adamw_update(param, grad, moment, square, rate, shrink)
        for ref, values in zip(outs[3 * n : 3 * n + 3], new):
            ref[...] = values


def post_kernel(
    counts_ref, x_ref, cot_ref, vec_ref, stat_ref, own_ref, got_ref, *refs
):
    bias_refs, (out_ref, grad_ref, sums_ref, t_ref, h_ref, q_ref) = refs[:-6], refs[-6:]
    pixels, images, width = x_ref.shape
    size = pixels * width
    zero = jnp.zeros((images, width), f32)
    gate = valid_gate(counts_ref, (images, width))
    mu1, r1, mu2, r2 = (stat_ref[i][:, 0:1] for i in range(4))
    gain1, mix, gain2, scale, lower = (vec_ref[i : i + 1, :] for i in (0, 2, 3, 5, 6))
    lift = mixed_parts(x_ref, mu1, r1, vec_ref, h_ref, q_ref)

    def loop(body, init):
        return lax.fori_loop(0, pixels, body, init, unroll=7)

    def column(values):
        return jnp.sum(values, axis=0, keepdims=True)

    def first(p, carry):
        g_scale, g_lower, g_gain2, g_shift2 = carry
        middle = x_ref[p] + lift * q_ref[p]
        branch = own_ref[0, p] + got_ref[0, p].astype(f32) + lower
        out_ref[p] = middle + scale * branch
        weighted = cot_ref[p].astype(f32) * gate
        back = own_ref[1, p] + got_ref[1, p].astype(f32)
        h2 = (middle - mu2) * r2
        return (g_scale + weighted * branch, g_lower + weighted, g_gain2 + back * h2, g_shift2 + back)

    g_scale, g_lower, g_gain2, g_shift2 = loop(first, (zero,) * 4)
    mean2 = row_total(g_shift2 * gain2) / size
    mean2h = row_total(g_gain2 * gain2) / size

    def second(p, g_mix):
        middle = x_ref[p] + lift * q_ref[p]
        back = own_ref[1, p] + got_ref[1, p].astype(f32)
        h2 = (middle - mu2) * r2
        grad = cot_ref[p].astype(f32) * gate + r2 * (back * gain2 - mean2 - h2 * mean2h)
        grad_ref[p] = grad
        t_ref[p] = grad * mix
        return g_mix + grad * q_ref[p]

    g_mix = loop(second, zero) * (r1 * gain1)
    for p in range(pixels):
        h_ref[p] = along_row(lambda i: t_ref[i] * near_share(i), p)
    g_gain1 = g_shift1 = zero
    for p in range(pixels):
        ng = along_col(lambda i: h_ref[i], p) - t_ref[p]
        t_ref[p] = ng
        g_gain1 = g_gain1 + ng * ((x_ref[p] - mu1) * r1)
        g_shift1 = g_shift1 + ng
    mean1 = row_total(g_shift1 * gain1) / size
    mean1h = row_total(g_gain1 * gain1) / size

    def third(p, carry):
        h1 = (x_ref[p] - mu1) * r1
        grad_ref[p] = grad_ref[p] + r1 * (t_ref[p] * gain1 - mean1 - h1 * mean1h)
        return carry

    loop(third, 0)
    lines = bias_refs[0].shape[0]
    sums_ref[:lines, :] = bias_refs[0][...] + bias_refs[1][...] + bias_refs[2][...]
    for i, total in enumerate((g_gain1, g_shift1, g_mix, g_gain2, g_shift2, g_scale, g_lower * scale)):
        total = column(total)
        for k in range(width // 128):
            row = lines + (width // 128) * i + k
            sums_ref[row : row + 1, :] = total[:, k * 128 : (k + 1) * 128]


def call(kernel, outs, ins, scratch=(), vmem=12, smem=0, hold=True, loose=()):
    many = isinstance(outs, (list, tuple))
    arrays = (*ins, *(outs if many else [outs]))
    moved = sum(math.prod(v.shape) * v.dtype.itemsize for v in arrays)
    if hold:
        outs = [pltpu.VMEM(v.shape, v.dtype) for v in outs] if many else pltpu.VMEM(outs.shape, outs.dtype)
    ins = [
        v
        if i < smem or not (hold or i in loose)
        else pltpu.with_memory_space_constraint(v, pltpu.HBM if i in loose else pltpu.VMEM)
        for i, v in enumerate(ins)
    ]
    return pl.pallas_call(
        kernel,
        out_shape=outs,
        in_specs=[SMEM] * smem + [VMEM] * (len(ins) - smem),
        out_specs=[VMEM] * len(outs) if many else VMEM,
        scratch_shapes=list(scratch),
        name=getattr(kernel, "func", kernel).__name__,
        compiler_params=pltpu.CompilerParams(vmem_limit_bytes=vmem * 2**20),
        cost_estimate=pl.CostEstimate(flops=0, bytes_accessed=moved, transcendentals=0),
    )(*ins)


def struct(shape, dtype=f32):
    return jax.ShapeDtypeStruct(shape, dtype)


BOTH = ("narrow", "wide")


def joint(values, change):
    pairs = [(n * 16 + w, change(n, w)) for n in range(2) for w in range(16)]
    return lax.ppermute(values, BOTH, [(s, n * 16 + w) for s, (n, w) in pairs])


def flip(values, bit):
    return lax.ppermute(values, "wide", [(w, w ^ bit) for w in range(16)])


def far(values):
    return joint(values, lambda n, w: (n, w ^ (12 if n else 8)))


def across(values):
    return lax.ppermute(values, "narrow", [(0, 1), (1, 0)])


def diagonal(values):
    return joint(values, lambda n, w: (1 - n, w ^ 2))


def after(values, *others):
    return lax.optimization_barrier((values, *others))[0]


def wide_sum(*parts):
    total = parts[0].astype(f32)
    for part in parts[1:]:
        total = total + part.astype(f32)
    return total


def local_tree(
    features,
    cotangent,
    counts,
    hidden_weight,
    hidden_bias,
    output_weight,
    vectors,
    hidden_moment,
    hidden_square,
    bias_moment,
    bias_square,
    output_moment,
    output_square,
    vector_moment,
    vector_square,
):
    images, pixels, width = features.shape
    rows = images * pixels
    units = hidden_weight.shape[1]
    near, wide = lax.axis_index("narrow"), lax.axis_index("wide")
    first_far = jnp.where(near == 0, 8, 12)
    last_far = 20 - first_far
    zero = 0 * first_far
    place = [zero, zero + 4, zero + 2, zero + 6, first_far, last_far, first_far ^ 2, last_far ^ 2]
    place = (wide ^ jnp.stack(place)).astype(jnp.int32)

    pair, pair_f = struct((2, width, units), bf16), struct((2, width, units))
    w0 = call(cast_kernel, pair, (hidden_weight, output_weight), loose=(0, 1))
    wz1, wzf, wy0 = flip(w0, 4), far(w0), flip(w0, 2)
    wy1 = flip(wz1, 2)
    vectors_late = after(vectors, wz1)
    x = features.transpose(1, 0, 2)
    cot = cotangent.transpose(1, 0, 2)
    big = struct((pixels, images, width))
    keep = pltpu.VMEM((pixels, images, width), f32)
    sb, stat = call(
        pre_kernel,
        [struct((2, pixels, images, width), bf16), struct((4, images, 128))],
        (counts, x, cot, vectors_late),
        [keep, keep],
        smem=1,
        loose=(1, 2, 3),
    )
    sb = after(sb.reshape(2, rows, width), wzf, wy1, wy0)
    other = flip(sb, 1)
    wyo, wyf, wzo = diagonal(wzf), flip(wzf, 2), across(wzf)
    bias = hidden_bias.reshape(-1, 128)
    total, total_low = struct((2, rows, width)), struct((2, rows, width), bf16)

    def blocks(first, weights, results, started, old=(), loose=()):
        return call(
            functools.partial(block_kernel, first, len(weights), started),
            results,
            (place, sb, other, bias, *weights, *old),
            smem=1,
            vmem=20,
            loose=loose,
        )

    lines = struct(bias.shape)
    *old, sums1, g0, gz1, gy0, gy1 = blocks(
        0, [w0, wz1, wy0, wy1], [total, total, lines, pair_f, pair_f, pair, pair], False, loose=(5, 6, 7)
    )
    y1 = flip(gy1, 2)
    wzf, wzo, _ = lax.optimization_barrier((wzf, wzo, old[0]))
    *old, sums2, gzf, gzo = blocks(4, [wzf, wzo], [total, total, lines, pair_f, pair], True, old, loose=(4,))
    wyf, wyo, _ = lax.optimization_barrier((wyf, wyo, old[0]))
    block = struct((width, units), bf16)
    mine, theirs, sums3, *gy = blocks(6, [wyf, wyo], [total, total_low, lines] + [block] * 4, True, old)
    xs = across(gzo)
    ds, yf = [diagonal(gy[2]), diagonal(gy[3])], [flip(gy[0], 2), flip(gy[1], 2)]
    theirs, y1, xs = lax.optimization_barrier((theirs, y1, xs))
    got = flip(theirs, 1)
    z1 = flip(wide_sum(gz1, y1).astype(bf16), 4)

    shape = (2, pixels, images, width)
    payload = struct((bias.shape[0] + vectors.size // 128, 128))
    block_out, input_grad, sums = call(
        post_kernel,
        [big, big, payload],
        (counts, x, cot, vectors, stat, mine.reshape(shape), got.reshape(shape), sums1, sums2, sums3),
        [keep, keep, keep],
        smem=1,
        hold=False,
    )
    y0 = flip(after(gy0, sums), 2)
    xs, ya, da, yb, db, z1, _ = lax.optimization_barrier((xs, yf[0], ds[0], yf[1], ds[1], z1, sums))
    sum_f = jnp.stack([wide_sum(gzf[0], xs[0], ya, da), wide_sum(gzf[1], xs[1], yb, db)]).astype(bf16)
    zf = far(sum_f)
    sums = sums + flip(sums, 1)
    sums = after(sums, sum_f)
    sums = sums + across(sums)
    sums = sums + flip(sums, 2)
    own = wide_sum(g0, y0, z1, zf).astype(bf16)
    own, sums = lax.optimization_barrier((own, sums))
    got = across(own)
    for bit in (4, 8):
        sums = sums + flip(sums, bit)
    state = (
        (hidden_weight, hidden_moment, hidden_square),
        tuple(v.reshape(bias.shape) for v in (hidden_bias, bias_moment, bias_square)),
        (output_weight, output_moment, output_square),
        (vectors, vector_moment, vector_square),
    )
    new = call(
        update_kernel,
        [struct(v.shape) for group in state for v in group],
        (own, got, sums, *(v for group in state for v in group)),
        hold=False,
    )
    hidden_new, output_new, vector_new = new[:3], new[6:9], new[9:]
    bias_new = [v.reshape(hidden_bias.shape) for v in new[3:6]]
    return (
        block_out.transpose(1, 0, 2),
        input_grad.transpose(1, 0, 2),
        *hidden_new,
        *bias_new,
        *output_new,
        *vector_new,
    )


def solution(mesh):
    in_specs = (
        P(("narrow", "wide"), None, None),
        P(("narrow", "wide"), None, None),
        P(("narrow", "wide")),
        P(None, "wide"),
        P(),
        P("wide", None),
        P(),
        P(None, "wide"),
        P(None, "wide"),
        P(),
        P(),
        P("wide", None),
        P("wide", None),
        P(),
        P(),
    )
    out_specs = (
        P(("narrow", "wide"), None, None),
        P(("narrow", "wide"), None, None),
        P(None, "wide"),
        P(None, "wide"),
        P(None, "wide"),
        P(),
        P(),
        P(),
        P("wide", None),
        P("wide", None),
        P("wide", None),
        P(),
        P(),
        P(),
    )
    body = local_tree if dict(mesh.shape) == {"narrow": 2, "wide": 16} else local
    return jax.shard_map(body, mesh=mesh, in_specs=in_specs, out_specs=out_specs, check_vma=False)
```

```python
import functools
import math

import jax
import jax.numpy as jnp
from jax import lax
from jax.experimental import pallas as pl
from jax.experimental.pallas import tpu as pltpu
from jax.sharding import PartitionSpec as P

SIDE = 7
STEP = 5


norm_epsilon = 1e-05
first_decay = 0.9
second_decay = 0.999
adam_epsilon = 1e-08
weight_shrink = 0.05


def pool_matrix(side):
    places = jnp.arange(side * side, dtype=jnp.int32)
    place_row = places // side
    place_col = places % side
    nearby = (jnp.abs(place_row[:, None] - place_row[None, :]) <= 1) & (
        jnp.abs(place_col[:, None] - place_col[None, :]) <= 1
    )
    nearby = nearby.astype(jnp.float32)
    return nearby / jnp.sum(nearby, axis=1, keepdims=True)


def norm_parts(values, gain, shift):
    centre = jnp.mean(values, axis=(1, 2), keepdims=True)
    spread = jnp.mean((values - centre) ** 2, axis=(1, 2), keepdims=True)
    inverse = lax.rsqrt(spread + norm_epsilon)
    scaled = (values - centre) * inverse
    return (scaled * gain + shift, scaled, inverse)


def norm_back(upstream, scaled, inverse):
    first_mean = jnp.mean(upstream, axis=(1, 2), keepdims=True)
    second_mean = jnp.mean(upstream * scaled, axis=(1, 2), keepdims=True)
    return inverse * (upstream - first_mean - scaled * second_mean)


def gelu_slope(values):
    return 0.5 * (1.0 + lax.erf(values / math.sqrt(2.0))) + values * jnp.exp(
        -0.5 * values * values
    ) / math.sqrt(2.0 * math.pi)


def contract_rows(left, right):
    return lax.dot_general(
        left, right, (((0,), (0,)), ((), ())), preferred_element_type=jnp.float32
    )


def contract_cols(left, right):
    return lax.dot_general(
        left, right, (((1,), (1,)), ((), ())), preferred_element_type=jnp.float32
    )


def adamw_update(param, grad, moment, square, rate, shrink):
    moment_new = first_decay * moment + (1.0 - first_decay) * grad
    square_new = second_decay * square + (1.0 - second_decay) * grad * grad
    moment_hat = moment_new / (1.0 - first_decay**STEP)
    square_hat = square_new / (1.0 - second_decay**STEP)
    param_new = param - rate * (moment_hat / (jnp.sqrt(square_hat) + adam_epsilon) + shrink * param)
    return (param_new, moment_new, square_new)


def local(
    features,
    cotangent,
    counts,
    hidden_weight,
    hidden_bias,
    output_weight,
    vectors,
    hidden_moment,
    hidden_square,
    bias_moment,
    bias_square,
    output_moment,
    output_square,
    vector_moment,
    vector_square,
):
    images, pixels, width = features.shape
    rows = images * pixels
    units = hidden_weight.shape[1]
    pool = pool_matrix(SIDE)
    valid = (jnp.arange(images, dtype=jnp.int32) < counts[0]).astype(jnp.float32)
    weighted = cotangent.astype(jnp.float32) * valid[:, None, None]
    normed, first_scaled, first_inverse = norm_parts(features, vectors[0], vectors[1])
    mixed = jnp.einsum("pq,iqc->ipc", pool, normed, precision=lax.Precision.HIGHEST) - normed
    middle = features + vectors[2] * mixed
    second, second_scaled, second_inverse = norm_parts(middle, vectors[3], vectors[4])
    second_low = second.reshape(rows, width).astype(jnp.bfloat16)
    hidden_low = hidden_weight.astype(jnp.bfloat16)
    output_low = output_weight.astype(jnp.bfloat16)
    branch_grad = (weighted * vectors[5]).reshape(rows, width)
    branch_low = branch_grad.astype(jnp.bfloat16)
    offset = lax.axis_index("wide") * units
    local_bias = lax.dynamic_slice_in_dim(hidden_bias, offset, units)
    hidden_all = (
        jnp.dot(
            lax.all_gather(second_low, "wide", axis=0, tiled=True),
            hidden_low,
            preferred_element_type=jnp.float32,
        )
        + local_bias
    )
    active_all = jax.nn.gelu(hidden_all, approximate=False).astype(jnp.bfloat16)
    slope_all = gelu_slope(hidden_all)
    block = active_all
    branch = lax.psum_scatter(
        jnp.dot(block, output_low, preferred_element_type=jnp.float32),
        "wide",
        scatter_dimension=0,
        tiled=True,
    )
    piece = lax.all_gather(branch_low, "wide", axis=0, tiled=True)
    block = active_all
    output_total = contract_rows(block, piece)
    active_grad = contract_cols(piece, output_low)
    hidden_grad = (active_grad * slope_all).astype(jnp.bfloat16)
    local_bias_grad = jnp.sum(hidden_grad.astype(jnp.float32), axis=0)
    bias_part = lax.dynamic_update_slice_in_dim(
        jnp.zeros(hidden_bias.shape, jnp.float32), local_bias_grad, offset, 0
    )
    block = hidden_grad
    second_grad = lax.psum_scatter(
        contract_cols(block, hidden_low), "wide", scatter_dimension=0, tiled=True
    )
    block = hidden_grad
    hidden_part = contract_rows(lax.all_gather(second_low, "wide", axis=0, tiled=True), block)
    branch_full = (branch + vectors[6]).reshape(images, pixels, width)
    block_out = middle + vectors[5] * branch_full
    grad_scale_two = jnp.sum(weighted * branch_full, axis=(0, 1))
    grad_shift_out = jnp.sum(branch_grad, axis=0)
    second_grad = second_grad.reshape(images, pixels, width)
    grad_gain_two = jnp.sum(second_grad * second_scaled, axis=(0, 1))
    grad_shift_two = jnp.sum(second_grad, axis=(0, 1))
    middle_grad = weighted + norm_back(second_grad * vectors[3], second_scaled, second_inverse)
    grad_scale_one = jnp.sum(middle_grad * mixed, axis=(0, 1))
    mixed_grad = middle_grad * vectors[2]
    normed_grad = (
        jnp.einsum("qp,iqc->ipc", pool, mixed_grad, precision=lax.Precision.HIGHEST) - mixed_grad
    )
    grad_gain_one = jnp.sum(normed_grad * first_scaled, axis=(0, 1))
    grad_shift_one = jnp.sum(normed_grad, axis=(0, 1))
    input_grad = middle_grad + norm_back(normed_grad * vectors[0], first_scaled, first_inverse)
    vector_part = jnp.stack(
        [
            grad_gain_one,
            grad_shift_one,
            grad_scale_one,
            grad_gain_two,
            grad_shift_two,
            grad_scale_two,
            grad_shift_out,
        ]
    )
    vector_grad, bias_grad = lax.psum((vector_part, bias_part), ("narrow", "wide"))
    hidden_grad_sum, output_grad_sum = lax.psum((hidden_part, output_total), "narrow")
    hidden_new = adamw_update(
        hidden_weight, hidden_grad_sum, hidden_moment, hidden_square, 0.04, weight_shrink
    )
    bias_new = adamw_update(hidden_bias, bias_grad, bias_moment, bias_square, 0.2, 0.0)
    output_new = adamw_update(
        output_weight, output_grad_sum, output_moment, output_square, 0.02, weight_shrink
    )
    vector_new = adamw_update(vectors, vector_grad, vector_moment, vector_square, 0.3, 0.0)
    return (
        block_out,
        input_grad,
        hidden_new[0],
        hidden_new[1],
        hidden_new[2],
        bias_new[0],
        bias_new[1],
        bias_new[2],
        output_new[0],
        output_new[1],
        output_new[2],
        vector_new[0],
        vector_new[1],
        vector_new[2],
    )


f32 = jnp.float32
bf16 = jnp.bfloat16
VMEM = pl.BlockSpec(memory_space=pltpu.VMEM)
SMEM = pl.BlockSpec(memory_space=pltpu.SMEM)


def row_total(values):
    return jnp.sum(values, axis=1, keepdims=True)


def span(i):
    return min(i + 1, SIDE - 1) - max(i - 1, 0) + 1


def near_share(p):
    return 1.0 / (span(p // SIDE) * span(p % SIDE))


def along_row(load, p):
    c = p % SIDE
    total = load(p)
    if c > 0:
        total = total + load(p - 1)
    if c < SIDE - 1:
        total = total + load(p + 1)
    return total


def along_col(load, p):
    r = p // SIDE
    total = load(p)
    if r > 0:
        total = total + load(p - SIDE)
    if r < SIDE - 1:
        total = total + load(p + SIDE)
    return total


def valid_gate(counts_ref, shape):
    slots = lax.broadcasted_iota(jnp.int32, shape, 0)
    return jnp.where(slots < counts_ref[0], 1.0, 0.0)


def mixed_parts(x_ref, mu1, r1, vec_ref, h_ref, q_ref):
    for p in range(x_ref.shape[0]):
        h_ref[p] = along_row(lambda i: x_ref[i] - mu1, p)
    for p in range(x_ref.shape[0]):
        q_ref[p] = along_col(lambda i: h_ref[i], p) * near_share(p) - (x_ref[p] - mu1)
    return vec_ref[2:3, :] * (r1 * vec_ref[0:1, :])


def pre_kernel(counts_ref, x_ref, cot_ref, vec_ref, sb_ref, stat_ref, d_ref, h_ref):
    pixels, images, width = x_ref.shape
    size = pixels * width
    zero = jnp.zeros((images, width), f32)

    def loop(body, init):
        return lax.fori_loop(0, pixels, body, init, unroll=7)

    mu1 = row_total(loop(lambda p, s: s + x_ref[p], zero)) / size

    def centre(p, s):
        d = x_ref[p] - mu1
        return s + d * d

    r1 = lax.rsqrt(row_total(loop(centre, zero)) / size + norm_epsilon)
    lift = mixed_parts(x_ref, mu1, r1, vec_ref, h_ref, d_ref)

    def middle(p, s):
        m = x_ref[p] + lift * d_ref[p]
        h_ref[p] = m
        return s + m

    total = loop(middle, zero)
    mu2 = row_total(total) / size

    def spread(p, s):
        d = h_ref[p] - mu2
        d_ref[p] = d
        return s + d * d

    r2 = lax.rsqrt(row_total(loop(spread, zero)) / size + norm_epsilon)
    scale = r2 * vec_ref[3:4, :]
    shift = jnp.broadcast_to(vec_ref[4:5, :], (images, width))
    gate = valid_gate(counts_ref, (images, width)) * vec_ref[5:6, :]

    def finish(p, carry):
        sb_ref[0, p] = (d_ref[p] * scale + shift).astype(bf16)
        sb_ref[1, p] = (cot_ref[p].astype(f32) * gate).astype(bf16)
        return carry

    loop(finish, 0)
    for i, stat in enumerate((mu1, r1, mu2, r2)):
        stat_ref[i] = jnp.broadcast_to(stat, (images, 128))


def normal_parts(h):
    d = 1.0 + (0.3275911 / math.sqrt(2.0)) * jnp.abs(h)
    t = pl.reciprocal(d, approx=True)
    t = t * (2.0 - d * t)
    series = 0.5 * 1.061405429
    for c in (-1.453152027, 1.421413741, -0.284496736, 0.254829592):
        series = series * t + 0.5 * c
    e = jnp.exp2((-0.5 * math.log2(math.e)) * (h * h))
    tail = series * t * e
    phi = jnp.where(h < 0.0, tail, 1.0 - tail)
    return phi, phi + h * (e * (1.0 / math.sqrt(2.0 * math.pi)))


def dot(left, right, dims):
    return lax.dot_general(left, right, (dims, ((), ())), preferred_element_type=f32)


def side_by_side(refs, j):
    left, right = refs[2 * j], refs[2 * j + 1]
    return jnp.concatenate([left[...], right[...]], axis=1)


def cast_kernel(a_ref, b_ref, out_ref):
    out_ref[0] = a_ref[...].astype(bf16)
    out_ref[1] = b_ref[...].T.astype(bf16)


def joined(refs, i):
    return jnp.concatenate([refs[0][i], refs[1][i]], axis=1)


def block_kernel(first, count, place_ref, own_ref, oth_ref, bias_ref, *refs):
    w_refs, (act_ref, low_ref, sums_ref), outs = refs[:count], refs[count : count + 3], refs[count + 3 :]
    sums_ref[...] = jnp.zeros_like(sums_ref)
    for j in range(count // 2):
        lines = [pl.ds(place_ref[first + 2 * j + k], 1) for k in range(2)]
        bias = jnp.concatenate([bias_ref[line, :] for line in lines], axis=1)
        a, b = (joined(w_refs[2 * j : 2 * j + 2], i) for i in range(2))
        columns = slice(j * 256, (j + 1) * 256)
        grads = [None, None]
        sums = None
        for r, sb_ref in enumerate((own_ref, oth_ref)):
            h = dot(sb_ref[0], a, ((1,), (0,))) + bias
            back = dot(sb_ref[1], b, ((1,), (0,)))
            phi, slope = normal_parts(h)
            active = (h * phi).astype(bf16)
            low = (back * slope).astype(bf16)
            act_ref[r, :, columns] = active
            low_ref[r, :, columns] = low
            column = jnp.sum(low.astype(f32), axis=0, keepdims=True)
            sums = column if r == 0 else sums + column
            for i, (left, right) in enumerate(((sb_ref[0], low), (sb_ref[1], active))):
                part = dot(left, right, ((0,), (0,)))
                grads[i] = part if r == 0 else grads[i] + part
        for k in range(2):
            half = slice(k * 128, (k + 1) * 128)
            sums_ref[lines[k], :] = sums[:, half]
            for i, grad in enumerate(grads):
                outs[2 * j + k][i] = grad[:, half].astype(outs[2 * j + k].dtype)


def back_kernel(sides, counts, started, *refs):
    n = len(counts)
    acts, lows, refs = refs[:n], refs[n : 2 * n], refs[2 * n :]
    w_refs, refs = refs[: sum(counts)], refs[sum(counts) :]
    old, totals = (refs[: len(sides)], refs[len(sides) :]) if started else (None, refs)
    for at, r in enumerate(sides):
        for i, lefts in enumerate((acts, lows)):
            total = None if old is None else old[at][i]
            w = 0
            for left_ref in lefts:
                for j in range(left_ref.shape[2] // 256):
                    left = left_ref[r, :, j * 256 : (j + 1) * 256]
                    part = dot(left, joined(w_refs[w : w + 2], 1 - i), ((1,), (1,)))
                    total = part if total is None else total + part
                    w += 2
            totals[at][i] = total.astype(totals[at].dtype)


def update_kernel(own_ref, got_ref, sums_ref, *refs):
    state, outs = [refs[i : i + 3] for i in range(0, 12, 3)], refs[12:]
    grads = wide_sum(own_ref[...], got_ref[...])
    lines = state[1][0].shape[0]
    wide = [
        jnp.concatenate([sums_ref[lines + 4 * i + k : lines + 4 * i + k + 1, :] for k in range(4)], axis=1)
        for i in range(state[3][0].shape[0])
    ]
    settings = (
        (grads[0], 0.04, weight_shrink),
        (sums_ref[:lines, :], 0.2, 0.0),
        (grads[1].T, 0.02, weight_shrink),
        (jnp.concatenate(wide, axis=0), 0.3, 0.0),
    )
    for n, (grad, rate, shrink) in enumerate(settings):
        param, moment, square = (ref[...] for ref in state[n])
        new = adamw_update(param, grad, moment, square, rate, shrink)
        for ref, values in zip(outs[3 * n : 3 * n + 3], new):
            ref[...] = values


def post_kernel(
    counts_ref, x_ref, cot_ref, vec_ref, stat_ref, own_ref, got_ref, *refs
):
    bias_refs, (out_ref, grad_ref, sums_ref, t_ref, h_ref, q_ref) = refs[:-6], refs[-6:]
    pixels, images, width = x_ref.shape
    size = pixels * width
    zero = jnp.zeros((images, width), f32)
    gate = valid_gate(counts_ref, (images, width))
    mu1, r1, mu2, r2 = (stat_ref[i][:, 0:1] for i in range(4))
    gain1, mix, gain2, scale, lower = (vec_ref[i : i + 1, :] for i in (0, 2, 3, 5, 6))
    lift = mixed_parts(x_ref, mu1, r1, vec_ref, h_ref, q_ref)

    def loop(body, init):
        return lax.fori_loop(0, pixels, body, init, unroll=7)

    def column(values):
        return jnp.sum(values, axis=0, keepdims=True)

    def first(p, carry):
        g_scale, g_lower, g_gain2, g_shift2 = carry
        middle = x_ref[p] + lift * q_ref[p]
        branch = own_ref[0, p] + got_ref[0, p].astype(f32) + lower
        out_ref[p] = middle + scale * branch
        weighted = cot_ref[p].astype(f32) * gate
        back = own_ref[1, p] + got_ref[1, p].astype(f32)
        h2 = (middle - mu2) * r2
        return (g_scale + weighted * branch, g_lower + weighted, g_gain2 + back * h2, g_shift2 + back)

    g_scale, g_lower, g_gain2, g_shift2 = loop(first, (zero,) * 4)
    mean2 = row_total(g_shift2 * gain2) / size
    mean2h = row_total(g_gain2 * gain2) / size

    def second(p, g_mix):
        middle = x_ref[p] + lift * q_ref[p]
        back = own_ref[1, p] + got_ref[1, p].astype(f32)
        h2 = (middle - mu2) * r2
        grad = cot_ref[p].astype(f32) * gate + r2 * (back * gain2 - mean2 - h2 * mean2h)
        grad_ref[p] = grad
        t_ref[p] = grad * mix
        return g_mix + grad * q_ref[p]

    g_mix = loop(second, zero) * (r1 * gain1)
    for p in range(pixels):
        h_ref[p] = along_row(lambda i: t_ref[i] * near_share(i), p)
    g_gain1 = g_shift1 = zero
    for p in range(pixels):
        ng = along_col(lambda i: h_ref[i], p) - t_ref[p]
        t_ref[p] = ng
        g_gain1 = g_gain1 + ng * ((x_ref[p] - mu1) * r1)
        g_shift1 = g_shift1 + ng
    mean1 = row_total(g_shift1 * gain1) / size
    mean1h = row_total(g_gain1 * gain1) / size

    def third(p, carry):
        h1 = (x_ref[p] - mu1) * r1
        grad_ref[p] = grad_ref[p] + r1 * (t_ref[p] * gain1 - mean1 - h1 * mean1h)
        return carry

    loop(third, 0)
    lines = bias_refs[0].shape[0]
    sums_ref[:lines, :] = bias_refs[0][...] + bias_refs[1][...] + bias_refs[2][...]
    for i, total in enumerate((g_gain1, g_shift1, g_mix, g_gain2, g_shift2, g_scale, g_lower * scale)):
        total = column(total)
        for k in range(width // 128):
            row = lines + (width // 128) * i + k
            sums_ref[row : row + 1, :] = total[:, k * 128 : (k + 1) * 128]


def call(kernel, outs, ins, scratch=(), vmem=12, smem=0, hold=True, loose=()):
    many = isinstance(outs, (list, tuple))
    arrays = (*ins, *(outs if many else [outs]))
    moved = sum(math.prod(v.shape) * v.dtype.itemsize for v in arrays)
    if hold:
        outs = [pltpu.VMEM(v.shape, v.dtype) for v in outs] if many else pltpu.VMEM(outs.shape, outs.dtype)
    ins = [
        v
        if i < smem or not (hold or i in loose)
        else pltpu.with_memory_space_constraint(v, pltpu.HBM if i in loose else pltpu.VMEM)
        for i, v in enumerate(ins)
    ]
    return pl.pallas_call(
        kernel,
        out_shape=outs,
        in_specs=[SMEM] * smem + [VMEM] * (len(ins) - smem),
        out_specs=[VMEM] * len(outs) if many else VMEM,
        scratch_shapes=list(scratch),
        name=getattr(kernel, "func", kernel).__name__,
        compiler_params=pltpu.CompilerParams(vmem_limit_bytes=vmem * 2**20),
        cost_estimate=pl.CostEstimate(flops=0, bytes_accessed=moved, transcendentals=0),
    )(*ins)


def struct(shape, dtype=f32):
    return jax.ShapeDtypeStruct(shape, dtype)


BOTH = ("narrow", "wide")


def joint(values, change):
    pairs = [(n * 16 + w, change(n, w)) for n in range(2) for w in range(16)]
    return lax.ppermute(values, BOTH, [(s, n * 16 + w) for s, (n, w) in pairs])


def flip(values, bit):
    return lax.ppermute(values, "wide", [(w, w ^ bit) for w in range(16)])


def far(values):
    return joint(values, lambda n, w: (n, w ^ (12 if n else 8)))


def across(values):
    return lax.ppermute(values, "narrow", [(0, 1), (1, 0)])


def diagonal(values):
    return joint(values, lambda n, w: (1 - n, w ^ 2))


def after(values, *others):
    return lax.optimization_barrier((values, *others))[0]


def wide_sum(*parts):
    total = parts[0].astype(f32)
    for part in parts[1:]:
        total = total + part.astype(f32)
    return total


def local_tree(
    features,
    cotangent,
    counts,
    hidden_weight,
    hidden_bias,
    output_weight,
    vectors,
    hidden_moment,
    hidden_square,
    bias_moment,
    bias_square,
    output_moment,
    output_square,
    vector_moment,
    vector_square,
):
    images, pixels, width = features.shape
    rows = images * pixels
    units = hidden_weight.shape[1]
    near, wide = lax.axis_index("narrow"), lax.axis_index("wide")
    first_far = jnp.where(near == 0, 8, 12)
    last_far = 20 - first_far
    zero = 0 * first_far
    place = [zero, zero + 4, first_far, zero + 2, first_far ^ 2, last_far, last_far ^ 2, zero + 6]
    place = (wide ^ jnp.stack(place)).astype(jnp.int32)

    pair, pair_f = struct((2, width, units), bf16), struct((2, width, units))
    w0 = call(cast_kernel, pair, (hidden_weight, output_weight), loose=(0, 1))
    wz1, wzf, wy0 = flip(w0, 4), far(w0), flip(w0, 2)
    vectors_late = after(vectors, wz1)
    x = features.transpose(1, 0, 2)
    cot = cotangent.transpose(1, 0, 2)
    big = struct((pixels, images, width))
    keep = pltpu.VMEM((pixels, images, width), f32)
    sb, stat = call(
        pre_kernel,
        [struct((2, pixels, images, width), bf16), struct((4, images, 128))],
        (counts, x, cot, vectors_late),
        [keep, keep],
        smem=1,
        loose=(1, 2, 3),
    )
    sb = after(sb.reshape(2, rows, width), wzf, wy0)
    other = flip(sb, 1)
    wyo, wyf, wzo = diagonal(wzf), flip(wzf, 2), across(wzf)
    bias = hidden_bias.reshape(-1, 128)
    total, total_low = struct((2, rows, width)), struct((2, rows, width), bf16)

    lines = struct(bias.shape)

    def blocks(first, weights, results, **kw):
        tall = struct((2, rows, 128 * len(weights)), bf16)
        return call(
            functools.partial(block_kernel, first, len(weights)),
            [tall, tall, lines, *results],
            (place, sb, other, bias, *weights),
            smem=1,
            vmem=20,
            **kw,
        )

    def back(sides, results, hidden, weights, old=(), loose=()):
        acts, lows = zip(*hidden)
        counts = [act.shape[2] // 128 for act in acts]
        kernel = functools.partial(back_kernel, sides, counts, bool(old))
        return call(kernel, results, (*acts, *lows, *weights, *old), loose=loose)

    w_near = [w0, wz1, wzf, wy0]
    *near_hidden, sums1, g0, gz1, gzf, gy0 = blocks(0, w_near, [pair_f, pair, pair_f, pair], loose=(5, 6, 7))
    z1 = flip(gz1, 4)
    wy1 = flip(after(wz1, sums1), 2)
    wyf, wzo, _ = lax.optimization_barrier((wyf, wzo, sums1))
    *far_hidden, sums2, gyf, gzo = blocks(4, [wyf, wzo], [pair, pair])
    yf, xs = flip(gyf, 2), across(gzo)
    old = back((0, 1), [total, total], (near_hidden, far_hidden), [*w_near, wyf, wzo], loose=(5, 6, 7))
    wyo, wy1, _ = lax.optimization_barrier((wyo, wy1, old[0]))
    *last_hidden, sums3, gyo, gy1 = blocks(6, [wyo, wy1], [pair, pair])
    ds, zy = diagonal(gyo), flip(gy1, 4)
    theirs = back((1,), [total_low], (last_hidden,), [wyo, wy1], old[1:])[0]
    theirs, yf, xs, z1 = lax.optimization_barrier((theirs, yf, xs, z1))
    got = flip(theirs, 1)
    mine = back((0,), [total], (last_hidden,), [wyo, wy1], old[:1])[0]

    shape = (2, pixels, images, width)
    payload = struct((bias.shape[0] + vectors.size // 128, 128))
    block_out, input_grad, sums = call(
        post_kernel,
        [big, big, payload],
        (counts, x, cot, vectors, stat, mine.reshape(shape), got.reshape(shape), sums1, sums2, sums3),
        [keep, keep, keep],
        smem=1,
        hold=False,
    )
    ds, zy, _ = lax.optimization_barrier((ds, zy, sums))
    sum_f = wide_sum(gzf, xs, yf, ds).astype(bf16)
    y0 = flip(after(wide_sum(gy0, zy).astype(bf16), sum_f), 2)
    zf = far(sum_f)
    sums = sums + flip(sums, 1)
    sums = after(sums, sum_f)
    sums = sums + across(sums)
    sums = sums + flip(sums, 2)
    own = wide_sum(g0, y0, z1, zf).astype(bf16)
    own, sums = lax.optimization_barrier((own, sums))
    got = across(own)
    for bit in (4, 8):
        sums = sums + flip(sums, bit)
    state = (
        (hidden_weight, hidden_moment, hidden_square),
        tuple(v.reshape(bias.shape) for v in (hidden_bias, bias_moment, bias_square)),
        (output_weight, output_moment, output_square),
        (vectors, vector_moment, vector_square),
    )
    new = call(
        update_kernel,
        [struct(v.shape) for group in state for v in group],
        (own, got, sums, *(v for group in state for v in group)),
        hold=False,
    )
    hidden_new, output_new, vector_new = new[:3], new[6:9], new[9:]
    bias_new = [v.reshape(hidden_bias.shape) for v in new[3:6]]
    return (
        block_out.transpose(1, 0, 2),
        input_grad.transpose(1, 0, 2),
        *hidden_new,
        *bias_new,
        *output_new,
        *vector_new,
    )


def solution(mesh):
    in_specs = (
        P(("narrow", "wide"), None, None),
        P(("narrow", "wide"), None, None),
        P(("narrow", "wide")),
        P(None, "wide"),
        P(),
        P("wide", None),
        P(),
        P(None, "wide"),
        P(None, "wide"),
        P(),
        P(),
        P("wide", None),
        P("wide", None),
        P(),
        P(),
    )
    out_specs = (
        P(("narrow", "wide"), None, None),
        P(("narrow", "wide"), None, None),
        P(None, "wide"),
        P(None, "wide"),
        P(None, "wide"),
        P(),
        P(),
        P(),
        P("wide", None),
        P("wide", None),
        P("wide", None),
        P(),
        P(),
        P(),
    )
    body = local_tree if dict(mesh.shape) == {"narrow": 2, "wide": 16} else local
    return jax.shard_map(body, mesh=mesh, in_specs=in_specs, out_specs=out_specs, check_vma=False)
```

```python
import functools
import math

import jax
import jax.numpy as jnp
from jax import lax
from jax.experimental import pallas as pl
from jax.experimental.pallas import tpu as pltpu
from jax.sharding import PartitionSpec as P

SIDE = 7
STEP = 5


norm_epsilon = 1e-05
first_decay = 0.9
second_decay = 0.999
adam_epsilon = 1e-08
weight_shrink = 0.05


def pool_matrix(side):
    places = jnp.arange(side * side, dtype=jnp.int32)
    place_row = places // side
    place_col = places % side
    nearby = (jnp.abs(place_row[:, None] - place_row[None, :]) <= 1) & (
        jnp.abs(place_col[:, None] - place_col[None, :]) <= 1
    )
    nearby = nearby.astype(jnp.float32)
    return nearby / jnp.sum(nearby, axis=1, keepdims=True)


def norm_parts(values, gain, shift):
    centre = jnp.mean(values, axis=(1, 2), keepdims=True)
    spread = jnp.mean((values - centre) ** 2, axis=(1, 2), keepdims=True)
    inverse = lax.rsqrt(spread + norm_epsilon)
    scaled = (values - centre) * inverse
    return (scaled * gain + shift, scaled, inverse)


def norm_back(upstream, scaled, inverse):
    first_mean = jnp.mean(upstream, axis=(1, 2), keepdims=True)
    second_mean = jnp.mean(upstream * scaled, axis=(1, 2), keepdims=True)
    return inverse * (upstream - first_mean - scaled * second_mean)


def gelu_slope(values):
    return 0.5 * (1.0 + lax.erf(values / math.sqrt(2.0))) + values * jnp.exp(
        -0.5 * values * values
    ) / math.sqrt(2.0 * math.pi)


def contract_rows(left, right):
    return lax.dot_general(
        left, right, (((0,), (0,)), ((), ())), preferred_element_type=jnp.float32
    )


def contract_cols(left, right):
    return lax.dot_general(
        left, right, (((1,), (1,)), ((), ())), preferred_element_type=jnp.float32
    )


def adamw_update(param, grad, moment, square, rate, shrink):
    moment_new = first_decay * moment + (1.0 - first_decay) * grad
    square_new = second_decay * square + (1.0 - second_decay) * grad * grad
    moment_hat = moment_new / (1.0 - first_decay**STEP)
    square_hat = square_new / (1.0 - second_decay**STEP)
    param_new = param - rate * (moment_hat / (jnp.sqrt(square_hat) + adam_epsilon) + shrink * param)
    return (param_new, moment_new, square_new)


def local(
    features,
    cotangent,
    counts,
    hidden_weight,
    hidden_bias,
    output_weight,
    vectors,
    hidden_moment,
    hidden_square,
    bias_moment,
    bias_square,
    output_moment,
    output_square,
    vector_moment,
    vector_square,
):
    images, pixels, width = features.shape
    rows = images * pixels
    units = hidden_weight.shape[1]
    pool = pool_matrix(SIDE)
    valid = (jnp.arange(images, dtype=jnp.int32) < counts[0]).astype(jnp.float32)
    weighted = cotangent.astype(jnp.float32) * valid[:, None, None]
    normed, first_scaled, first_inverse = norm_parts(features, vectors[0], vectors[1])
    mixed = jnp.einsum("pq,iqc->ipc", pool, normed, precision=lax.Precision.HIGHEST) - normed
    middle = features + vectors[2] * mixed
    second, second_scaled, second_inverse = norm_parts(middle, vectors[3], vectors[4])
    second_low = second.reshape(rows, width).astype(jnp.bfloat16)
    hidden_low = hidden_weight.astype(jnp.bfloat16)
    output_low = output_weight.astype(jnp.bfloat16)
    branch_grad = (weighted * vectors[5]).reshape(rows, width)
    branch_low = branch_grad.astype(jnp.bfloat16)
    offset = lax.axis_index("wide") * units
    local_bias = lax.dynamic_slice_in_dim(hidden_bias, offset, units)
    hidden_all = (
        jnp.dot(
            lax.all_gather(second_low, "wide", axis=0, tiled=True),
            hidden_low,
            preferred_element_type=jnp.float32,
        )
        + local_bias
    )
    active_all = jax.nn.gelu(hidden_all, approximate=False).astype(jnp.bfloat16)
    slope_all = gelu_slope(hidden_all)
    block = active_all
    branch = lax.psum_scatter(
        jnp.dot(block, output_low, preferred_element_type=jnp.float32),
        "wide",
        scatter_dimension=0,
        tiled=True,
    )
    piece = lax.all_gather(branch_low, "wide", axis=0, tiled=True)
    block = active_all
    output_total = contract_rows(block, piece)
    active_grad = contract_cols(piece, output_low)
    hidden_grad = (active_grad * slope_all).astype(jnp.bfloat16)
    local_bias_grad = jnp.sum(hidden_grad.astype(jnp.float32), axis=0)
    bias_part = lax.dynamic_update_slice_in_dim(
        jnp.zeros(hidden_bias.shape, jnp.float32), local_bias_grad, offset, 0
    )
    block = hidden_grad
    second_grad = lax.psum_scatter(
        contract_cols(block, hidden_low), "wide", scatter_dimension=0, tiled=True
    )
    block = hidden_grad
    hidden_part = contract_rows(lax.all_gather(second_low, "wide", axis=0, tiled=True), block)
    branch_full = (branch + vectors[6]).reshape(images, pixels, width)
    block_out = middle + vectors[5] * branch_full
    grad_scale_two = jnp.sum(weighted * branch_full, axis=(0, 1))
    grad_shift_out = jnp.sum(branch_grad, axis=0)
    second_grad = second_grad.reshape(images, pixels, width)
    grad_gain_two = jnp.sum(second_grad * second_scaled, axis=(0, 1))
    grad_shift_two = jnp.sum(second_grad, axis=(0, 1))
    middle_grad = weighted + norm_back(second_grad * vectors[3], second_scaled, second_inverse)
    grad_scale_one = jnp.sum(middle_grad * mixed, axis=(0, 1))
    mixed_grad = middle_grad * vectors[2]
    normed_grad = (
        jnp.einsum("qp,iqc->ipc", pool, mixed_grad, precision=lax.Precision.HIGHEST) - mixed_grad
    )
    grad_gain_one = jnp.sum(normed_grad * first_scaled, axis=(0, 1))
    grad_shift_one = jnp.sum(normed_grad, axis=(0, 1))
    input_grad = middle_grad + norm_back(normed_grad * vectors[0], first_scaled, first_inverse)
    vector_part = jnp.stack(
        [
            grad_gain_one,
            grad_shift_one,
            grad_scale_one,
            grad_gain_two,
            grad_shift_two,
            grad_scale_two,
            grad_shift_out,
        ]
    )
    vector_grad, bias_grad = lax.psum((vector_part, bias_part), ("narrow", "wide"))
    hidden_grad_sum, output_grad_sum = lax.psum((hidden_part, output_total), "narrow")
    hidden_new = adamw_update(
        hidden_weight, hidden_grad_sum, hidden_moment, hidden_square, 0.04, weight_shrink
    )
    bias_new = adamw_update(hidden_bias, bias_grad, bias_moment, bias_square, 0.2, 0.0)
    output_new = adamw_update(
        output_weight, output_grad_sum, output_moment, output_square, 0.02, weight_shrink
    )
    vector_new = adamw_update(vectors, vector_grad, vector_moment, vector_square, 0.3, 0.0)
    return (
        block_out,
        input_grad,
        hidden_new[0],
        hidden_new[1],
        hidden_new[2],
        bias_new[0],
        bias_new[1],
        bias_new[2],
        output_new[0],
        output_new[1],
        output_new[2],
        vector_new[0],
        vector_new[1],
        vector_new[2],
    )


f32 = jnp.float32
bf16 = jnp.bfloat16
VMEM = pl.BlockSpec(memory_space=pltpu.VMEM)
SMEM = pl.BlockSpec(memory_space=pltpu.SMEM)


def row_total(values):
    return jnp.sum(values, axis=1, keepdims=True)


def span(i):
    return min(i + 1, SIDE - 1) - max(i - 1, 0) + 1


def near_share(p):
    return 1.0 / (span(p // SIDE) * span(p % SIDE))


def along_row(load, p):
    c = p % SIDE
    total = load(p)
    if c > 0:
        total = total + load(p - 1)
    if c < SIDE - 1:
        total = total + load(p + 1)
    return total


def along_col(load, p):
    r = p // SIDE
    total = load(p)
    if r > 0:
        total = total + load(p - SIDE)
    if r < SIDE - 1:
        total = total + load(p + SIDE)
    return total


def valid_gate(counts_ref, shape):
    slots = lax.broadcasted_iota(jnp.int32, shape, 0)
    return jnp.where(slots < counts_ref[0], 1.0, 0.0)


def mixed_parts(x_ref, mu1, r1, vec_ref, h_ref, q_ref):
    for p in range(x_ref.shape[0]):
        h_ref[p] = along_row(lambda i: x_ref[i] - mu1, p)
    for p in range(x_ref.shape[0]):
        q_ref[p] = along_col(lambda i: h_ref[i], p) * near_share(p) - (x_ref[p] - mu1)
    return vec_ref[2:3, :] * (r1 * vec_ref[0:1, :])


def pre_kernel(counts_ref, x_ref, cot_ref, vec_ref, sb_ref, stat_ref, d_ref, h_ref):
    pixels, images, width = x_ref.shape
    size = pixels * width
    zero = jnp.zeros((images, width), f32)

    def loop(body, init):
        return lax.fori_loop(0, pixels, body, init, unroll=7)

    mu1 = row_total(loop(lambda p, s: s + x_ref[p], zero)) / size

    def centre(p, s):
        d = x_ref[p] - mu1
        return s + d * d

    r1 = lax.rsqrt(row_total(loop(centre, zero)) / size + norm_epsilon)
    lift = mixed_parts(x_ref, mu1, r1, vec_ref, h_ref, d_ref)

    def middle(p, s):
        m = x_ref[p] + lift * d_ref[p]
        h_ref[p] = m
        return s + m

    total = loop(middle, zero)
    mu2 = row_total(total) / size

    def spread(p, s):
        d = h_ref[p] - mu2
        d_ref[p] = d
        return s + d * d

    r2 = lax.rsqrt(row_total(loop(spread, zero)) / size + norm_epsilon)
    scale = r2 * vec_ref[3:4, :]
    shift = jnp.broadcast_to(vec_ref[4:5, :], (images, width))
    gate = valid_gate(counts_ref, (images, width)) * vec_ref[5:6, :]

    def finish(p, carry):
        sb_ref[0, p] = (d_ref[p] * scale + shift).astype(bf16)
        sb_ref[1, p] = (cot_ref[p].astype(f32) * gate).astype(bf16)
        return carry

    loop(finish, 0)
    for i, stat in enumerate((mu1, r1, mu2, r2)):
        stat_ref[i] = jnp.broadcast_to(stat, (images, 128))


def normal_parts(h):
    d = 1.0 + (0.3275911 / math.sqrt(2.0)) * jnp.abs(h)
    t = pl.reciprocal(d, approx=True)
    t = t * (2.0 - d * t)
    series = 0.5 * 1.061405429
    for c in (-1.453152027, 1.421413741, -0.284496736, 0.254829592):
        series = series * t + 0.5 * c
    e = jnp.exp2((-0.5 * math.log2(math.e)) * (h * h))
    tail = series * t * e
    phi = jnp.where(h < 0.0, tail, 1.0 - tail)
    return phi, phi + h * (e * (1.0 / math.sqrt(2.0 * math.pi)))


def dot(left, right, dims):
    return lax.dot_general(left, right, (dims, ((), ())), preferred_element_type=f32)


def side_by_side(refs, j):
    left, right = refs[2 * j], refs[2 * j + 1]
    return jnp.concatenate([left[...], right[...]], axis=1)


def cast_kernel(a_ref, b_ref, out_ref):
    out_ref[0] = a_ref[...].astype(bf16)
    out_ref[1] = b_ref[...].T.astype(bf16)


def joined(refs, i):
    return jnp.concatenate([refs[0][i], refs[1][i]], axis=1)


def block_places():
    near, wide = lax.axis_index("narrow"), lax.axis_index("wide")
    far_step = 8 + 4 * near
    other_step = 12 - 4 * near
    return [wide ^ step for step in (0, 4, far_step, 2, far_step ^ 2, other_step, other_step ^ 2, 6)]


def block_kernel(first, count, own_ref, oth_ref, bias_ref, *refs):
    w_refs, (act_ref, low_ref, sums_ref), outs = refs[:count], refs[count : count + 3], refs[count + 3 :]
    sums_ref[...] = jnp.zeros_like(sums_ref)
    places = block_places()
    for j in range(count // 2):
        lines = [pl.ds(places[first + 2 * j + k], 1) for k in range(2)]
        bias = jnp.concatenate([bias_ref[line, :] for line in lines], axis=1)
        a, b = (joined(w_refs[2 * j : 2 * j + 2], i) for i in range(2))
        columns = slice(j * 256, (j + 1) * 256)
        grads = [None, None]
        sums = None
        for r, sb_ref in enumerate((own_ref, oth_ref)):
            h = dot(sb_ref[0], a, ((1,), (0,))) + bias
            back = dot(sb_ref[1], b, ((1,), (0,)))
            phi, slope = normal_parts(h)
            active = (h * phi).astype(bf16)
            low = (back * slope).astype(bf16)
            act_ref[r, :, columns] = active
            low_ref[r, :, columns] = low
            column = jnp.sum(low.astype(f32), axis=0, keepdims=True)
            sums = column if r == 0 else sums + column
            for i, (left, right) in enumerate(((sb_ref[0], low), (sb_ref[1], active))):
                part = dot(left, right, ((0,), (0,)))
                grads[i] = part if r == 0 else grads[i] + part
        for k in range(2):
            half = slice(k * 128, (k + 1) * 128)
            sums_ref[lines[k], :] = sums[:, half]
            for i, grad in enumerate(grads):
                outs[2 * j + k][i] = grad[:, half].astype(outs[2 * j + k].dtype)


def back_kernel(sides, counts, started, *refs):
    n = len(counts)
    acts, lows, refs = refs[:n], refs[n : 2 * n], refs[2 * n :]
    w_refs, refs = refs[: sum(counts)], refs[sum(counts) :]
    old, totals = (refs[: len(sides)], refs[len(sides) :]) if started else (None, refs)
    for at, r in enumerate(sides):
        for i, lefts in enumerate((acts, lows)):
            total = None if old is None else old[at][i]
            w = 0
            for left_ref in lefts:
                for j in range(left_ref.shape[2] // 256):
                    left = left_ref[r, :, j * 256 : (j + 1) * 256]
                    part = dot(left, joined(w_refs[w : w + 2], 1 - i), ((1,), (1,)))
                    total = part if total is None else total + part
                    w += 2
            totals[at][i] = total.astype(totals[at].dtype)


def update_kernel(own_ref, got_ref, sums_ref, *refs):
    state, outs = [refs[i : i + 3] for i in range(0, 12, 3)], refs[12:]
    grads = wide_sum(own_ref[...], got_ref[...])
    lines = state[1][0].shape[0]
    wide = [
        jnp.concatenate([sums_ref[lines + 4 * i + k : lines + 4 * i + k + 1, :] for k in range(4)], axis=1)
        for i in range(state[3][0].shape[0])
    ]
    settings = (
        (grads[0], 0.04, weight_shrink),
        (sums_ref[:lines, :], 0.2, 0.0),
        (grads[1].T, 0.02, weight_shrink),
        (jnp.concatenate(wide, axis=0), 0.3, 0.0),
    )
    for n, (grad, rate, shrink) in enumerate(settings):
        param, moment, square = (ref[...] for ref in state[n])
        new = adamw_update(param, grad, moment, square, rate, shrink)
        for ref, values in zip(outs[3 * n : 3 * n + 3], new):
            ref[...] = values


def post_kernel(
    counts_ref, x_ref, cot_ref, vec_ref, stat_ref, own_ref, got_ref, *refs
):
    bias_refs, (out_ref, grad_ref, sums_ref, t_ref, h_ref, q_ref) = refs[:-6], refs[-6:]
    pixels, images, width = x_ref.shape
    size = pixels * width
    zero = jnp.zeros((images, width), f32)
    gate = valid_gate(counts_ref, (images, width))
    mu1, r1, mu2, r2 = (stat_ref[i][:, 0:1] for i in range(4))
    gain1, mix, gain2, scale, lower = (vec_ref[i : i + 1, :] for i in (0, 2, 3, 5, 6))
    lift = mixed_parts(x_ref, mu1, r1, vec_ref, h_ref, q_ref)

    def loop(body, init):
        return lax.fori_loop(0, pixels, body, init, unroll=7)

    def column(values):
        return jnp.sum(values, axis=0, keepdims=True)

    def first(p, carry):
        g_scale, g_lower, g_gain2, g_shift2 = carry
        middle = x_ref[p] + lift * q_ref[p]
        branch = own_ref[0, p] + got_ref[0, p].astype(f32) + lower
        out_ref[p] = middle + scale * branch
        weighted = cot_ref[p].astype(f32) * gate
        back = own_ref[1, p] + got_ref[1, p].astype(f32)
        h2 = (middle - mu2) * r2
        return (g_scale + weighted * branch, g_lower + weighted, g_gain2 + back * h2, g_shift2 + back)

    g_scale, g_lower, g_gain2, g_shift2 = loop(first, (zero,) * 4)
    mean2 = row_total(g_shift2 * gain2) / size
    mean2h = row_total(g_gain2 * gain2) / size

    def second(p, g_mix):
        middle = x_ref[p] + lift * q_ref[p]
        back = own_ref[1, p] + got_ref[1, p].astype(f32)
        h2 = (middle - mu2) * r2
        grad = cot_ref[p].astype(f32) * gate + r2 * (back * gain2 - mean2 - h2 * mean2h)
        grad_ref[p] = grad
        t_ref[p] = grad * mix
        return g_mix + grad * q_ref[p]

    g_mix = loop(second, zero) * (r1 * gain1)
    for p in range(pixels):
        h_ref[p] = along_row(lambda i: t_ref[i] * near_share(i), p)
    g_gain1 = g_shift1 = zero
    for p in range(pixels):
        ng = along_col(lambda i: h_ref[i], p) - t_ref[p]
        t_ref[p] = ng
        g_gain1 = g_gain1 + ng * ((x_ref[p] - mu1) * r1)
        g_shift1 = g_shift1 + ng
    mean1 = row_total(g_shift1 * gain1) / size
    mean1h = row_total(g_gain1 * gain1) / size

    def third(p, carry):
        h1 = (x_ref[p] - mu1) * r1
        grad_ref[p] = grad_ref[p] + r1 * (t_ref[p] * gain1 - mean1 - h1 * mean1h)
        return carry

    loop(third, 0)
    lines = bias_refs[0].shape[0]
    sums_ref[:lines, :] = bias_refs[0][...] + bias_refs[1][...] + bias_refs[2][...]
    for i, total in enumerate((g_gain1, g_shift1, g_mix, g_gain2, g_shift2, g_scale, g_lower * scale)):
        total = column(total)
        for k in range(width // 128):
            row = lines + (width // 128) * i + k
            sums_ref[row : row + 1, :] = total[:, k * 128 : (k + 1) * 128]


def call(kernel, outs, ins, scratch=(), vmem=12, smem=0, hold=True, loose=()):
    many = isinstance(outs, (list, tuple))
    arrays = (*ins, *(outs if many else [outs]))
    moved = sum(math.prod(v.shape) * v.dtype.itemsize for v in arrays)
    if hold:
        outs = [pltpu.VMEM(v.shape, v.dtype) for v in outs] if many else pltpu.VMEM(outs.shape, outs.dtype)
    ins = [
        v
        if i < smem or not (hold or i in loose)
        else pltpu.with_memory_space_constraint(v, pltpu.HBM if i in loose else pltpu.VMEM)
        for i, v in enumerate(ins)
    ]
    return pl.pallas_call(
        kernel,
        out_shape=outs,
        in_specs=[SMEM] * smem + [VMEM] * (len(ins) - smem),
        out_specs=[VMEM] * len(outs) if many else VMEM,
        scratch_shapes=list(scratch),
        name=getattr(kernel, "func", kernel).__name__,
        compiler_params=pltpu.CompilerParams(vmem_limit_bytes=vmem * 2**20),
        cost_estimate=pl.CostEstimate(flops=0, bytes_accessed=moved, transcendentals=0),
    )(*ins)


def struct(shape, dtype=f32):
    return jax.ShapeDtypeStruct(shape, dtype)


BOTH = ("narrow", "wide")


def joint(values, change):
    pairs = [(n * 16 + w, change(n, w)) for n in range(2) for w in range(16)]
    return lax.ppermute(values, BOTH, [(s, n * 16 + w) for s, (n, w) in pairs])


def flip(values, bit):
    return lax.ppermute(values, "wide", [(w, w ^ bit) for w in range(16)])


def far(values):
    return joint(values, lambda n, w: (n, w ^ (12 if n else 8)))


def across(values):
    return lax.ppermute(values, "narrow", [(0, 1), (1, 0)])


def diagonal(values):
    return joint(values, lambda n, w: (1 - n, w ^ 2))


def after(values, *others):
    return lax.optimization_barrier((values, *others))[0]


def wide_sum(*parts):
    total = parts[0].astype(f32)
    for part in parts[1:]:
        total = total + part.astype(f32)
    return total


def local_tree(
    features,
    cotangent,
    counts,
    hidden_weight,
    hidden_bias,
    output_weight,
    vectors,
    hidden_moment,
    hidden_square,
    bias_moment,
    bias_square,
    output_moment,
    output_square,
    vector_moment,
    vector_square,
):
    images, pixels, width = features.shape
    rows = images * pixels
    units = hidden_weight.shape[1]
    pair, pair_f = struct((2, width, units), bf16), struct((2, width, units))
    w0 = call(cast_kernel, pair, (hidden_weight, output_weight), loose=(0, 1))
    wz1, wzf, wy0 = flip(w0, 4), far(w0), flip(w0, 2)
    vectors_late = after(vectors, wy0)
    x = features.transpose(1, 0, 2)
    cot = cotangent.transpose(1, 0, 2)
    big = struct((pixels, images, width))
    keep = pltpu.VMEM((pixels, images, width), f32)
    sb, stat = call(
        pre_kernel,
        [struct((2, pixels, images, width), bf16), struct((4, images, 128))],
        (counts, x, cot, vectors_late),
        [keep, keep],
        smem=1,
        loose=(1, 2, 3),
    )
    sb = after(sb.reshape(2, rows, width), wzf, wz1, wy0)
    other = flip(sb, 1)
    wyf, wzo = flip(wzf, 2), across(wzf)
    bias = hidden_bias.reshape(-1, 128)
    total, total_low = struct((2, rows, width)), struct((2, rows, width), bf16)

    lines = struct(bias.shape)

    def blocks(first, weights, results, **kw):
        tall = struct((2, rows, 128 * len(weights)), bf16)
        return call(
            functools.partial(block_kernel, first, len(weights)),
            [tall, tall, lines, *results],
            (sb, other, bias, *weights),
            vmem=20,
            **kw,
        )

    def back(sides, results, hidden, weights, old=(), loose=()):
        acts, lows = zip(*hidden)
        counts = [act.shape[2] // 128 for act in acts]
        kernel = functools.partial(back_kernel, sides, counts, bool(old))
        return call(kernel, results, (*acts, *lows, *weights, *old), loose=loose)

    w_near = [w0, wz1, wzf, wy0]
    *near_hidden, sums1, g0, gz1, gzf, gy0 = blocks(0, w_near, [pair_f, pair, pair_f, pair])
    z1 = flip(gz1, 4)
    wy1 = flip(after(wz1, sums1), 2)
    wyf, wzo, _ = lax.optimization_barrier((wyf, wzo, sums1))
    wyo = across(wyf)
    *far_hidden, sums2, gyf, gzo = blocks(4, [wyf, wzo], [pair, pair])
    yf, xs = flip(gyf, 2), across(gzo)
    old = back((0, 1), [total, total], (near_hidden, far_hidden), [*w_near, wyf, wzo])
    wyo, wy1, _ = lax.optimization_barrier((wyo, wy1, old[0]))
    *last_hidden, sums3, gyo, gy1 = blocks(6, [wyo, wy1], [pair, pair])
    ds, zy = diagonal(gyo), flip(gy1, 4)
    theirs = back((1,), [total_low], (last_hidden,), [wyo, wy1], old[1:])[0]
    theirs, yf, xs, z1 = lax.optimization_barrier((theirs, yf, xs, z1))
    got = flip(theirs, 1)
    mine = back((0,), [total], (last_hidden,), [wyo, wy1], old[:1])[0]

    shape = (2, pixels, images, width)
    payload = struct((bias.shape[0] + vectors.size // 128, 128))
    block_out, input_grad, sums = call(
        post_kernel,
        [big, big, payload],
        (counts, x, cot, vectors, stat, mine.reshape(shape), got.reshape(shape), sums1, sums2, sums3),
        [keep, keep, keep],
        smem=1,
        hold=False,
    )
    ds, zy, _ = lax.optimization_barrier((ds, zy, sums))
    sum_f = wide_sum(gzf, xs, yf, ds).astype(bf16)
    y0 = flip(after(wide_sum(gy0, zy).astype(bf16), sum_f), 2)
    zf = far(sum_f)
    sums = sums + flip(sums, 1)
    sums = after(sums, sum_f)
    sums = sums + across(sums)
    sums = sums + flip(sums, 2)
    own = wide_sum(g0, y0, z1, zf).astype(bf16)
    own, sums = lax.optimization_barrier((own, sums))
    got = across(own)
    for bit in (4, 8):
        sums = sums + flip(sums, bit)
    state = (
        (hidden_weight, hidden_moment, hidden_square),
        tuple(v.reshape(bias.shape) for v in (hidden_bias, bias_moment, bias_square)),
        (output_weight, output_moment, output_square),
        (vectors, vector_moment, vector_square),
    )
    new = call(
        update_kernel,
        [struct(v.shape) for group in state for v in group],
        (own, got, sums, *(v for group in state for v in group)),
        hold=False,
    )
    hidden_new, output_new, vector_new = new[:3], new[6:9], new[9:]
    bias_new = [v.reshape(hidden_bias.shape) for v in new[3:6]]
    return (
        block_out.transpose(1, 0, 2),
        input_grad.transpose(1, 0, 2),
        *hidden_new,
        *bias_new,
        *output_new,
        *vector_new,
    )


def solution(mesh):
    in_specs = (
        P(("narrow", "wide"), None, None),
        P(("narrow", "wide"), None, None),
        P(("narrow", "wide")),
        P(None, "wide"),
        P(),
        P("wide", None),
        P(),
        P(None, "wide"),
        P(None, "wide"),
        P(),
        P(),
        P("wide", None),
        P("wide", None),
        P(),
        P(),
    )
    out_specs = (
        P(("narrow", "wide"), None, None),
        P(("narrow", "wide"), None, None),
        P(None, "wide"),
        P(None, "wide"),
        P(None, "wide"),
        P(),
        P(),
        P(),
        P("wide", None),
        P("wide", None),
        P("wide", None),
        P(),
        P(),
        P(),
    )
    body = local_tree if dict(mesh.shape) == {"narrow": 2, "wide": 16} else local
    return jax.shard_map(body, mesh=mesh, in_specs=in_specs, out_specs=out_specs, check_vma=False)
```

```python
import functools
import math

import jax
import jax.numpy as jnp
from jax import lax
from jax.experimental import pallas as pl
from jax.experimental.pallas import tpu as pltpu
from jax.sharding import PartitionSpec as P

SIDE = 7
STEP = 5


norm_epsilon = 1e-05
first_decay = 0.9
second_decay = 0.999
adam_epsilon = 1e-08
weight_shrink = 0.05


def pool_matrix(side):
    places = jnp.arange(side * side, dtype=jnp.int32)
    place_row = places // side
    place_col = places % side
    nearby = (jnp.abs(place_row[:, None] - place_row[None, :]) <= 1) & (
        jnp.abs(place_col[:, None] - place_col[None, :]) <= 1
    )
    nearby = nearby.astype(jnp.float32)
    return nearby / jnp.sum(nearby, axis=1, keepdims=True)


def norm_parts(values, gain, shift):
    centre = jnp.mean(values, axis=(1, 2), keepdims=True)
    spread = jnp.mean((values - centre) ** 2, axis=(1, 2), keepdims=True)
    inverse = lax.rsqrt(spread + norm_epsilon)
    scaled = (values - centre) * inverse
    return (scaled * gain + shift, scaled, inverse)


def norm_back(upstream, scaled, inverse):
    first_mean = jnp.mean(upstream, axis=(1, 2), keepdims=True)
    second_mean = jnp.mean(upstream * scaled, axis=(1, 2), keepdims=True)
    return inverse * (upstream - first_mean - scaled * second_mean)


def gelu_slope(values):
    return 0.5 * (1.0 + lax.erf(values / math.sqrt(2.0))) + values * jnp.exp(
        -0.5 * values * values
    ) / math.sqrt(2.0 * math.pi)


def contract_rows(left, right):
    return lax.dot_general(
        left, right, (((0,), (0,)), ((), ())), preferred_element_type=jnp.float32
    )


def contract_cols(left, right):
    return lax.dot_general(
        left, right, (((1,), (1,)), ((), ())), preferred_element_type=jnp.float32
    )


def adamw_update(param, grad, moment, square, rate, shrink):
    moment_new = first_decay * moment + (1.0 - first_decay) * grad
    square_new = second_decay * square + (1.0 - second_decay) * grad * grad
    moment_hat = moment_new / (1.0 - first_decay**STEP)
    square_hat = square_new / (1.0 - second_decay**STEP)
    param_new = param - rate * (moment_hat / (jnp.sqrt(square_hat) + adam_epsilon) + shrink * param)
    return (param_new, moment_new, square_new)


def local(
    features,
    cotangent,
    counts,
    hidden_weight,
    hidden_bias,
    output_weight,
    vectors,
    hidden_moment,
    hidden_square,
    bias_moment,
    bias_square,
    output_moment,
    output_square,
    vector_moment,
    vector_square,
):
    images, pixels, width = features.shape
    rows = images * pixels
    units = hidden_weight.shape[1]
    pool = pool_matrix(SIDE)
    valid = (jnp.arange(images, dtype=jnp.int32) < counts[0]).astype(jnp.float32)
    weighted = cotangent.astype(jnp.float32) * valid[:, None, None]
    normed, first_scaled, first_inverse = norm_parts(features, vectors[0], vectors[1])
    mixed = jnp.einsum("pq,iqc->ipc", pool, normed, precision=lax.Precision.HIGHEST) - normed
    middle = features + vectors[2] * mixed
    second, second_scaled, second_inverse = norm_parts(middle, vectors[3], vectors[4])
    second_low = second.reshape(rows, width).astype(jnp.bfloat16)
    hidden_low = hidden_weight.astype(jnp.bfloat16)
    output_low = output_weight.astype(jnp.bfloat16)
    branch_grad = (weighted * vectors[5]).reshape(rows, width)
    branch_low = branch_grad.astype(jnp.bfloat16)
    offset = lax.axis_index("wide") * units
    local_bias = lax.dynamic_slice_in_dim(hidden_bias, offset, units)
    hidden_all = (
        jnp.dot(
            lax.all_gather(second_low, "wide", axis=0, tiled=True),
            hidden_low,
            preferred_element_type=jnp.float32,
        )
        + local_bias
    )
    active_all = jax.nn.gelu(hidden_all, approximate=False).astype(jnp.bfloat16)
    slope_all = gelu_slope(hidden_all)
    block = active_all
    branch = lax.psum_scatter(
        jnp.dot(block, output_low, preferred_element_type=jnp.float32),
        "wide",
        scatter_dimension=0,
        tiled=True,
    )
    piece = lax.all_gather(branch_low, "wide", axis=0, tiled=True)
    block = active_all
    output_total = contract_rows(block, piece)
    active_grad = contract_cols(piece, output_low)
    hidden_grad = (active_grad * slope_all).astype(jnp.bfloat16)
    local_bias_grad = jnp.sum(hidden_grad.astype(jnp.float32), axis=0)
    bias_part = lax.dynamic_update_slice_in_dim(
        jnp.zeros(hidden_bias.shape, jnp.float32), local_bias_grad, offset, 0
    )
    block = hidden_grad
    second_grad = lax.psum_scatter(
        contract_cols(block, hidden_low), "wide", scatter_dimension=0, tiled=True
    )
    block = hidden_grad
    hidden_part = contract_rows(lax.all_gather(second_low, "wide", axis=0, tiled=True), block)
    branch_full = (branch + vectors[6]).reshape(images, pixels, width)
    block_out = middle + vectors[5] * branch_full
    grad_scale_two = jnp.sum(weighted * branch_full, axis=(0, 1))
    grad_shift_out = jnp.sum(branch_grad, axis=0)
    second_grad = second_grad.reshape(images, pixels, width)
    grad_gain_two = jnp.sum(second_grad * second_scaled, axis=(0, 1))
    grad_shift_two = jnp.sum(second_grad, axis=(0, 1))
    middle_grad = weighted + norm_back(second_grad * vectors[3], second_scaled, second_inverse)
    grad_scale_one = jnp.sum(middle_grad * mixed, axis=(0, 1))
    mixed_grad = middle_grad * vectors[2]
    normed_grad = (
        jnp.einsum("qp,iqc->ipc", pool, mixed_grad, precision=lax.Precision.HIGHEST) - mixed_grad
    )
    grad_gain_one = jnp.sum(normed_grad * first_scaled, axis=(0, 1))
    grad_shift_one = jnp.sum(normed_grad, axis=(0, 1))
    input_grad = middle_grad + norm_back(normed_grad * vectors[0], first_scaled, first_inverse)
    vector_part = jnp.stack(
        [
            grad_gain_one,
            grad_shift_one,
            grad_scale_one,
            grad_gain_two,
            grad_shift_two,
            grad_scale_two,
            grad_shift_out,
        ]
    )
    vector_grad, bias_grad = lax.psum((vector_part, bias_part), ("narrow", "wide"))
    hidden_grad_sum, output_grad_sum = lax.psum((hidden_part, output_total), "narrow")
    hidden_new = adamw_update(
        hidden_weight, hidden_grad_sum, hidden_moment, hidden_square, 0.04, weight_shrink
    )
    bias_new = adamw_update(hidden_bias, bias_grad, bias_moment, bias_square, 0.2, 0.0)
    output_new = adamw_update(
        output_weight, output_grad_sum, output_moment, output_square, 0.02, weight_shrink
    )
    vector_new = adamw_update(vectors, vector_grad, vector_moment, vector_square, 0.3, 0.0)
    return (
        block_out,
        input_grad,
        hidden_new[0],
        hidden_new[1],
        hidden_new[2],
        bias_new[0],
        bias_new[1],
        bias_new[2],
        output_new[0],
        output_new[1],
        output_new[2],
        vector_new[0],
        vector_new[1],
        vector_new[2],
    )


f32 = jnp.float32
bf16 = jnp.bfloat16
VMEM = pl.BlockSpec(memory_space=pltpu.VMEM)
SMEM = pl.BlockSpec(memory_space=pltpu.SMEM)


def row_total(values):
    return jnp.sum(values, axis=1, keepdims=True)


def span(i):
    return min(i + 1, SIDE - 1) - max(i - 1, 0) + 1


def near_share(p):
    return 1.0 / (span(p // SIDE) * span(p % SIDE))


def along_row(load, p):
    c = p % SIDE
    total = load(p)
    if c > 0:
        total = total + load(p - 1)
    if c < SIDE - 1:
        total = total + load(p + 1)
    return total


def along_col(load, p):
    r = p // SIDE
    total = load(p)
    if r > 0:
        total = total + load(p - SIDE)
    if r < SIDE - 1:
        total = total + load(p + SIDE)
    return total


def valid_gate(counts_ref, shape):
    slots = lax.broadcasted_iota(jnp.int32, shape, 0)
    return jnp.where(slots < counts_ref[0], 1.0, 0.0)


def mixed_parts(x_ref, mu1, r1, vec_ref, h_ref, q_ref):
    for p in range(x_ref.shape[0]):
        h_ref[p] = along_row(lambda i: x_ref[i] - mu1, p)
    for p in range(x_ref.shape[0]):
        q_ref[p] = along_col(lambda i: h_ref[i], p) * near_share(p) - (x_ref[p] - mu1)
    return vec_ref[2:3, :] * (r1 * vec_ref[0:1, :])


def normal_parts(h):
    d = 1.0 + (0.3275911 / math.sqrt(2.0)) * jnp.abs(h)
    t = pl.reciprocal(d, approx=True)
    t = t * (2.0 - d * t)
    series = 0.5 * 1.061405429
    for c in (-1.453152027, 1.421413741, -0.284496736, 0.254829592):
        series = series * t + 0.5 * c
    e = jnp.exp2((-0.5 * math.log2(math.e)) * (h * h))
    tail = series * t * e
    phi = jnp.where(h < 0.0, tail, 1.0 - tail)
    return phi, phi + h * (e * (1.0 / math.sqrt(2.0 * math.pi)))


def dot(left, right, dims):
    return lax.dot_general(left, right, (dims, ((), ())), preferred_element_type=f32)


def joined(refs, i):
    return jnp.concatenate([refs[0][i], refs[1][i]], axis=1)


def block_places():
    near, wide = lax.axis_index("narrow"), lax.axis_index("wide")
    far_step = 8 + 4 * near
    other_step = 12 - 4 * near
    return [wide ^ step for step in (0, 2, 4, far_step, far_step ^ 2, other_step, other_step ^ 2, 6)]


def block_bias(bias_ref, places, at):
    return jnp.concatenate([bias_ref[pl.ds(places[at + k], 1), :] for k in range(2)], axis=1)


def block_rows(second, upstream, a, b, bias):
    h = dot(second, a, ((1,), (0,))) + bias
    back = dot(upstream, b, ((1,), (0,)))
    phi, slope = normal_parts(h)
    active = (h * phi).astype(bf16)
    low = (back * slope).astype(bf16)
    column = jnp.sum(low.astype(f32), axis=0, keepdims=True)
    grads = [dot(left, right, ((0,), (0,))) for left, right in ((second, low), (upstream, active))]
    return active, low, column, grads


def pre_kernel(
    counts_ref, x_ref, cot_ref, vec_ref, bias_ref, w0_ref, w1_ref,
    sb_ref, stat_ref, act_ref, low_ref, column_ref, part_ref, d_ref, h_ref,
):
    pixels, images, width = x_ref.shape
    size = pixels * width
    zero = jnp.zeros((images, width), f32)

    def loop(body, init):
        return lax.fori_loop(0, pixels, body, init, unroll=7)

    mu1 = row_total(loop(lambda p, s: s + x_ref[p], zero)) / size

    def centre(p, s):
        d = x_ref[p] - mu1
        return s + d * d

    r1 = lax.rsqrt(row_total(loop(centre, zero)) / size + norm_epsilon)
    lift = mixed_parts(x_ref, mu1, r1, vec_ref, h_ref, d_ref)

    def middle(p, s):
        m = x_ref[p] + lift * d_ref[p]
        h_ref[p] = m
        return s + m

    total = loop(middle, zero)
    mu2 = row_total(total) / size

    def spread(p, s):
        d = h_ref[p] - mu2
        d_ref[p] = d
        return s + d * d

    r2 = lax.rsqrt(row_total(loop(spread, zero)) / size + norm_epsilon)
    scale = r2 * vec_ref[3:4, :]
    shift = jnp.broadcast_to(vec_ref[4:5, :], (images, width))
    gate = valid_gate(counts_ref, (images, width)) * vec_ref[5:6, :]

    def finish(p, carry):
        sb_ref[0, p] = (d_ref[p] * scale + shift).astype(bf16)
        sb_ref[1, p] = (cot_ref[p].astype(f32) * gate).astype(bf16)
        return carry

    loop(finish, 0)
    for i, stat in enumerate((mu1, r1, mu2, r2)):
        stat_ref[i] = jnp.broadcast_to(stat, (images, 128))
    second, upstream = (sb_ref[i].reshape(pixels * images, width) for i in range(2))
    a, b = (joined((w0_ref, w1_ref), i) for i in range(2))
    bias = block_bias(bias_ref, block_places(), 0)
    act_ref[...], low_ref[...], column_ref[...], grads = block_rows(second, upstream, a, b, bias)
    for i, grad in enumerate(grads):
        part_ref[i] = grad


def side_by_side(refs, j):
    left, right = refs[2 * j], refs[2 * j + 1]
    return jnp.concatenate([left[...], right[...]], axis=1)


def cast_kernel(a_ref, b_ref, out_ref):
    out_ref[0] = a_ref[...].astype(bf16)
    out_ref[1] = b_ref[...].T.astype(bf16)


def block_kernel(first, count, own_ref, oth_ref, bias_ref, *refs):
    w_refs, refs = refs[:count], refs[count:]
    begun, refs = (refs[:4], refs[4:]) if first == 0 else (None, refs)
    act_ref, low_ref, sums_ref, *outs = refs
    sums_ref[...] = jnp.zeros_like(sums_ref)
    places = block_places()
    for j in range(count // 2):
        bias = block_bias(bias_ref, places, first + 2 * j)
        a, b = (joined(w_refs[2 * j : 2 * j + 2], i) for i in range(2))
        columns = slice(j * 256, (j + 1) * 256)
        grads = sums = None
        for r, sb_ref in enumerate((own_ref, oth_ref)):
            if begun is not None and j == r == 0:
                active, low, column, parts = begun[0][...], begun[1][...], begun[2][...], begun[3]
            else:
                active, low, column, parts = block_rows(sb_ref[0], sb_ref[1], a, b, bias)
            act_ref[r, :, columns] = active
            low_ref[r, :, columns] = low
            sums = column if r == 0 else sums + column
            grads = [parts[0], parts[1]] if r == 0 else [total + part for total, part in zip(grads, parts)]
        for k in range(2):
            half = slice(k * 128, (k + 1) * 128)
            sums_ref[pl.ds(places[first + 2 * j + k], 1), :] = sums[:, half]
            for i, grad in enumerate(grads):
                outs[2 * j + k][i] = grad[:, half].astype(outs[2 * j + k].dtype)


def back_kernel(sides, counts, started, *refs):
    n = len(counts)
    acts, lows, refs = refs[:n], refs[n : 2 * n], refs[2 * n :]
    w_refs, refs = refs[: sum(counts)], refs[sum(counts) :]
    old, totals = (refs[: len(sides)], refs[len(sides) :]) if started else (None, refs)
    for at, r in enumerate(sides):
        for i, lefts in enumerate((acts, lows)):
            total = None if old is None else old[at][i]
            w = 0
            for left_ref in lefts:
                for j in range(left_ref.shape[2] // 256):
                    left = left_ref[r, :, j * 256 : (j + 1) * 256]
                    part = dot(left, joined(w_refs[w : w + 2], 1 - i), ((1,), (1,)))
                    total = part if total is None else total + part
                    w += 2
            totals[at][i] = total.astype(totals[at].dtype)


def update_kernel(own_ref, got_ref, sums_ref, *refs):
    state, outs = [refs[i : i + 3] for i in range(0, 12, 3)], refs[12:]
    grads = wide_sum(own_ref[...], got_ref[...])
    lines = state[1][0].shape[0]
    wide = [
        jnp.concatenate([sums_ref[lines + 4 * i + k : lines + 4 * i + k + 1, :] for k in range(4)], axis=1)
        for i in range(state[3][0].shape[0])
    ]
    settings = (
        (grads[0], 0.04, weight_shrink),
        (sums_ref[:lines, :], 0.2, 0.0),
        (grads[1].T, 0.02, weight_shrink),
        (jnp.concatenate(wide, axis=0), 0.3, 0.0),
    )
    for n, (grad, rate, shrink) in enumerate(settings):
        param, moment, square = (ref[...] for ref in state[n])
        new = adamw_update(param, grad, moment, square, rate, shrink)
        for ref, values in zip(outs[3 * n : 3 * n + 3], new):
            ref[...] = values


def post_kernel(
    counts_ref, x_ref, cot_ref, vec_ref, stat_ref, own_ref, got_ref, *refs
):
    bias_refs, (out_ref, grad_ref, sums_ref, t_ref, h_ref, q_ref) = refs[:-6], refs[-6:]
    pixels, images, width = x_ref.shape
    size = pixels * width
    zero = jnp.zeros((images, width), f32)
    gate = valid_gate(counts_ref, (images, width))
    mu1, r1, mu2, r2 = (stat_ref[i][:, 0:1] for i in range(4))
    gain1, mix, gain2, scale, lower = (vec_ref[i : i + 1, :] for i in (0, 2, 3, 5, 6))
    lift = mixed_parts(x_ref, mu1, r1, vec_ref, h_ref, q_ref)

    def loop(body, init):
        return lax.fori_loop(0, pixels, body, init, unroll=7)

    def column(values):
        return jnp.sum(values, axis=0, keepdims=True)

    def first(p, carry):
        g_scale, g_lower, g_gain2, g_shift2 = carry
        middle = x_ref[p] + lift * q_ref[p]
        branch = own_ref[0, p] + got_ref[0, p].astype(f32) + lower
        out_ref[p] = middle + scale * branch
        weighted = cot_ref[p].astype(f32) * gate
        back = own_ref[1, p] + got_ref[1, p].astype(f32)
        h2 = (middle - mu2) * r2
        return (g_scale + weighted * branch, g_lower + weighted, g_gain2 + back * h2, g_shift2 + back)

    g_scale, g_lower, g_gain2, g_shift2 = loop(first, (zero,) * 4)
    mean2 = row_total(g_shift2 * gain2) / size
    mean2h = row_total(g_gain2 * gain2) / size

    def second(p, g_mix):
        middle = x_ref[p] + lift * q_ref[p]
        back = own_ref[1, p] + got_ref[1, p].astype(f32)
        h2 = (middle - mu2) * r2
        grad = cot_ref[p].astype(f32) * gate + r2 * (back * gain2 - mean2 - h2 * mean2h)
        grad_ref[p] = grad
        t_ref[p] = grad * mix
        return g_mix + grad * q_ref[p]

    g_mix = loop(second, zero) * (r1 * gain1)
    for p in range(pixels):
        h_ref[p] = along_row(lambda i: t_ref[i] * near_share(i), p)
    g_gain1 = g_shift1 = zero
    for p in range(pixels):
        ng = along_col(lambda i: h_ref[i], p) - t_ref[p]
        t_ref[p] = ng
        g_gain1 = g_gain1 + ng * ((x_ref[p] - mu1) * r1)
        g_shift1 = g_shift1 + ng
    mean1 = row_total(g_shift1 * gain1) / size
    mean1h = row_total(g_gain1 * gain1) / size

    def third(p, carry):
        h1 = (x_ref[p] - mu1) * r1
        grad_ref[p] = grad_ref[p] + r1 * (t_ref[p] * gain1 - mean1 - h1 * mean1h)
        return carry

    loop(third, 0)
    lines = bias_refs[0].shape[0]
    sums_ref[:lines, :] = bias_refs[0][...] + bias_refs[1][...] + bias_refs[2][...]
    for i, total in enumerate((g_gain1, g_shift1, g_mix, g_gain2, g_shift2, g_scale, g_lower * scale)):
        total = column(total)
        for k in range(width // 128):
            row = lines + (width // 128) * i + k
            sums_ref[row : row + 1, :] = total[:, k * 128 : (k + 1) * 128]


def call(kernel, outs, ins, scratch=(), vmem=12, smem=0, hold=True, loose=()):
    many = isinstance(outs, (list, tuple))
    arrays = (*ins, *(outs if many else [outs]))
    moved = sum(math.prod(v.shape) * v.dtype.itemsize for v in arrays)
    if hold:
        outs = [pltpu.VMEM(v.shape, v.dtype) for v in outs] if many else pltpu.VMEM(outs.shape, outs.dtype)
    ins = [
        v
        if i < smem or not (hold or i in loose)
        else pltpu.with_memory_space_constraint(v, pltpu.HBM if i in loose else pltpu.VMEM)
        for i, v in enumerate(ins)
    ]
    return pl.pallas_call(
        kernel,
        out_shape=outs,
        in_specs=[SMEM] * smem + [VMEM] * (len(ins) - smem),
        out_specs=[VMEM] * len(outs) if many else VMEM,
        scratch_shapes=list(scratch),
        name=getattr(kernel, "func", kernel).__name__,
        compiler_params=pltpu.CompilerParams(vmem_limit_bytes=vmem * 2**20),
        cost_estimate=pl.CostEstimate(flops=0, bytes_accessed=moved, transcendentals=0),
    )(*ins)


def struct(shape, dtype=f32):
    return jax.ShapeDtypeStruct(shape, dtype)


BOTH = ("narrow", "wide")


def joint(values, change):
    pairs = [(n * 16 + w, change(n, w)) for n in range(2) for w in range(16)]
    return lax.ppermute(values, BOTH, [(s, n * 16 + w) for s, (n, w) in pairs])


def flip(values, bit):
    return lax.ppermute(values, "wide", [(w, w ^ bit) for w in range(16)])


def far(values):
    return joint(values, lambda n, w: (n, w ^ (12 if n else 8)))


def across(values):
    return lax.ppermute(values, "narrow", [(0, 1), (1, 0)])


def diagonal(values):
    return joint(values, lambda n, w: (1 - n, w ^ 2))


def after(values, *others):
    return lax.optimization_barrier((values, *others))[0]


def wide_sum(*parts):
    total = parts[0].astype(f32)
    for part in parts[1:]:
        total = total + part.astype(f32)
    return total


def local_tree(
    features,
    cotangent,
    counts,
    hidden_weight,
    hidden_bias,
    output_weight,
    vectors,
    hidden_moment,
    hidden_square,
    bias_moment,
    bias_square,
    output_moment,
    output_square,
    vector_moment,
    vector_square,
):
    images, pixels, width = features.shape
    rows = images * pixels
    units = hidden_weight.shape[1]
    pair, pair_f = struct((2, width, units), bf16), struct((2, width, units))
    w0 = call(cast_kernel, pair, (hidden_weight, output_weight), loose=(0, 1))
    wz1, wzf, wy0 = flip(w0, 4), far(w0), flip(w0, 2)
    vectors_late, wy0 = lax.optimization_barrier((vectors, wy0))
    bias = hidden_bias.reshape(-1, 128)
    x = features.transpose(1, 0, 2)
    cot = cotangent.transpose(1, 0, 2)
    big = struct((pixels, images, width))
    keep = pltpu.VMEM((pixels, images, width), f32)
    tile = struct((rows, 256), bf16)
    sb, stat, *begun = call(
        pre_kernel,
        [
            struct((2, pixels, images, width), bf16),
            struct((4, images, 128)),
            tile,
            tile,
            struct((1, 256)),
            struct((2, width, 256)),
        ],
        (counts, x, cot, vectors_late, bias, w0, wy0),
        [keep, keep],
        smem=1,
        loose=(1, 2, 3),
        vmem=20,
    )
    sb = after(sb.reshape(2, rows, width), wzf, wz1, wy0)
    other = flip(sb, 1)
    wyf, wzo = flip(wzf, 2), across(wzf)
    total, total_low = struct((2, rows, width)), struct((2, rows, width), bf16)

    lines = struct(bias.shape)

    def blocks(first, weights, results, begun=()):
        tall = struct((2, rows, 128 * len(weights)), bf16)
        return call(
            functools.partial(block_kernel, first, len(weights)),
            [tall, tall, lines, *results],
            (sb, other, bias, *weights, *begun),
            vmem=20,
        )

    def back(sides, results, hidden, weights, old=(), loose=()):
        acts, lows = zip(*hidden)
        counts = [act.shape[2] // 128 for act in acts]
        kernel = functools.partial(back_kernel, sides, counts, bool(old))
        return call(kernel, results, (*acts, *lows, *weights, *old), loose=loose)

    w_near = [w0, wy0, wz1, wzf]
    *near_hidden, sums1, g0, gy0, gz1, gzf = blocks(0, w_near, [pair_f, pair, pair, pair_f], begun)
    z1 = flip(gz1, 4)
    wy1 = flip(after(wz1, sums1), 2)
    wyf = after(wyf, sums1)
    wyo = across(wyf)
    *far_hidden, sums2, gyf, gzo = blocks(4, [wyf, wzo], [pair, pair])
    yf, xs = flip(gyf, 2), across(gzo)
    old = back((0, 1), [total, total], (near_hidden, far_hidden), [*w_near, wyf, wzo])
    wyo, wy1, _ = lax.optimization_barrier((wyo, wy1, old[0]))
    *last_hidden, sums3, gyo, gy1 = blocks(6, [wyo, wy1], [pair, pair])
    ds, zy = diagonal(gyo), flip(gy1, 4)
    theirs = back((1,), [total_low], (last_hidden,), [wyo, wy1], old[1:])[0]
    theirs, yf, xs, z1 = lax.optimization_barrier((theirs, yf, xs, z1))
    got = flip(theirs, 1)
    mine = back((0,), [total], (last_hidden,), [wyo, wy1], old[:1])[0]

    shape = (2, pixels, images, width)
    payload = struct((bias.shape[0] + vectors.size // 128, 128))
    block_out, input_grad, sums = call(
        post_kernel,
        [big, big, payload],
        (counts, x, cot, vectors, stat, mine.reshape(shape), got.reshape(shape), sums1, sums2, sums3),
        [keep, keep, keep],
        smem=1,
        hold=False,
    )
    ds, zy, _ = lax.optimization_barrier((ds, zy, sums))
    sum_f = wide_sum(gzf, xs, yf, ds).astype(bf16)
    y0 = flip(after(wide_sum(gy0, zy).astype(bf16), sum_f), 2)
    zf = far(sum_f)
    sums = sums + flip(sums, 1)
    sums = after(sums, sum_f)
    sums = sums + across(sums)
    sums = sums + flip(sums, 2)
    own = wide_sum(g0, y0, z1, zf).astype(bf16)
    own, sums = lax.optimization_barrier((own, sums))
    got = across(own)
    for bit in (4, 8):
        sums = sums + flip(sums, bit)
    state = (
        (hidden_weight, hidden_moment, hidden_square),
        tuple(v.reshape(bias.shape) for v in (hidden_bias, bias_moment, bias_square)),
        (output_weight, output_moment, output_square),
        (vectors, vector_moment, vector_square),
    )
    new = call(
        update_kernel,
        [struct(v.shape) for group in state for v in group],
        (own, got, sums, *(v for group in state for v in group)),
        hold=False,
    )
    hidden_new, output_new, vector_new = new[:3], new[6:9], new[9:]
    bias_new = [v.reshape(hidden_bias.shape) for v in new[3:6]]
    return (
        block_out.transpose(1, 0, 2),
        input_grad.transpose(1, 0, 2),
        *hidden_new,
        *bias_new,
        *output_new,
        *vector_new,
    )


def solution(mesh):
    in_specs = (
        P(("narrow", "wide"), None, None),
        P(("narrow", "wide"), None, None),
        P(("narrow", "wide")),
        P(None, "wide"),
        P(),
        P("wide", None),
        P(),
        P(None, "wide"),
        P(None, "wide"),
        P(),
        P(),
        P("wide", None),
        P("wide", None),
        P(),
        P(),
    )
    out_specs = (
        P(("narrow", "wide"), None, None),
        P(("narrow", "wide"), None, None),
        P(None, "wide"),
        P(None, "wide"),
        P(None, "wide"),
        P(),
        P(),
        P(),
        P("wide", None),
        P("wide", None),
        P("wide", None),
        P(),
        P(),
        P(),
    )
    body = local_tree if dict(mesh.shape) == {"narrow": 2, "wide": 16} else local
    return jax.shard_map(body, mesh=mesh, in_specs=in_specs, out_specs=out_specs, check_vma=False)
```

```python
import functools
import math

import jax
import jax.numpy as jnp
from jax import lax
from jax.experimental import pallas as pl
from jax.experimental.pallas import tpu as pltpu
from jax.sharding import PartitionSpec as P

SIDE = 7
STEP = 5


norm_epsilon = 1e-05
first_decay = 0.9
second_decay = 0.999
adam_epsilon = 1e-08
weight_shrink = 0.05


def pool_matrix(side):
    places = jnp.arange(side * side, dtype=jnp.int32)
    place_row = places // side
    place_col = places % side
    nearby = (jnp.abs(place_row[:, None] - place_row[None, :]) <= 1) & (
        jnp.abs(place_col[:, None] - place_col[None, :]) <= 1
    )
    nearby = nearby.astype(jnp.float32)
    return nearby / jnp.sum(nearby, axis=1, keepdims=True)


def norm_parts(values, gain, shift):
    centre = jnp.mean(values, axis=(1, 2), keepdims=True)
    spread = jnp.mean((values - centre) ** 2, axis=(1, 2), keepdims=True)
    inverse = lax.rsqrt(spread + norm_epsilon)
    scaled = (values - centre) * inverse
    return (scaled * gain + shift, scaled, inverse)


def norm_back(upstream, scaled, inverse):
    first_mean = jnp.mean(upstream, axis=(1, 2), keepdims=True)
    second_mean = jnp.mean(upstream * scaled, axis=(1, 2), keepdims=True)
    return inverse * (upstream - first_mean - scaled * second_mean)


def gelu_slope(values):
    return 0.5 * (1.0 + lax.erf(values / math.sqrt(2.0))) + values * jnp.exp(
        -0.5 * values * values
    ) / math.sqrt(2.0 * math.pi)


def contract_rows(left, right):
    return lax.dot_general(
        left, right, (((0,), (0,)), ((), ())), preferred_element_type=jnp.float32
    )


def contract_cols(left, right):
    return lax.dot_general(
        left, right, (((1,), (1,)), ((), ())), preferred_element_type=jnp.float32
    )


def adamw_update(param, grad, moment, square, rate, shrink):
    moment_new = first_decay * moment + (1.0 - first_decay) * grad
    square_new = second_decay * square + (1.0 - second_decay) * grad * grad
    moment_hat = moment_new / (1.0 - first_decay**STEP)
    square_hat = square_new / (1.0 - second_decay**STEP)
    param_new = param - rate * (moment_hat / (jnp.sqrt(square_hat) + adam_epsilon) + shrink * param)
    return (param_new, moment_new, square_new)


def local(
    features,
    cotangent,
    counts,
    hidden_weight,
    hidden_bias,
    output_weight,
    vectors,
    hidden_moment,
    hidden_square,
    bias_moment,
    bias_square,
    output_moment,
    output_square,
    vector_moment,
    vector_square,
):
    images, pixels, width = features.shape
    rows = images * pixels
    units = hidden_weight.shape[1]
    pool = pool_matrix(SIDE)
    valid = (jnp.arange(images, dtype=jnp.int32) < counts[0]).astype(jnp.float32)
    weighted = cotangent.astype(jnp.float32) * valid[:, None, None]
    normed, first_scaled, first_inverse = norm_parts(features, vectors[0], vectors[1])
    mixed = jnp.einsum("pq,iqc->ipc", pool, normed, precision=lax.Precision.HIGHEST) - normed
    middle = features + vectors[2] * mixed
    second, second_scaled, second_inverse = norm_parts(middle, vectors[3], vectors[4])
    second_low = second.reshape(rows, width).astype(jnp.bfloat16)
    hidden_low = hidden_weight.astype(jnp.bfloat16)
    output_low = output_weight.astype(jnp.bfloat16)
    branch_grad = (weighted * vectors[5]).reshape(rows, width)
    branch_low = branch_grad.astype(jnp.bfloat16)
    offset = lax.axis_index("wide") * units
    local_bias = lax.dynamic_slice_in_dim(hidden_bias, offset, units)
    hidden_all = (
        jnp.dot(
            lax.all_gather(second_low, "wide", axis=0, tiled=True),
            hidden_low,
            preferred_element_type=jnp.float32,
        )
        + local_bias
    )
    active_all = jax.nn.gelu(hidden_all, approximate=False).astype(jnp.bfloat16)
    slope_all = gelu_slope(hidden_all)
    block = active_all
    branch = lax.psum_scatter(
        jnp.dot(block, output_low, preferred_element_type=jnp.float32),
        "wide",
        scatter_dimension=0,
        tiled=True,
    )
    piece = lax.all_gather(branch_low, "wide", axis=0, tiled=True)
    block = active_all
    output_total = contract_rows(block, piece)
    active_grad = contract_cols(piece, output_low)
    hidden_grad = (active_grad * slope_all).astype(jnp.bfloat16)
    local_bias_grad = jnp.sum(hidden_grad.astype(jnp.float32), axis=0)
    bias_part = lax.dynamic_update_slice_in_dim(
        jnp.zeros(hidden_bias.shape, jnp.float32), local_bias_grad, offset, 0
    )
    block = hidden_grad
    second_grad = lax.psum_scatter(
        contract_cols(block, hidden_low), "wide", scatter_dimension=0, tiled=True
    )
    block = hidden_grad
    hidden_part = contract_rows(lax.all_gather(second_low, "wide", axis=0, tiled=True), block)
    branch_full = (branch + vectors[6]).reshape(images, pixels, width)
    block_out = middle + vectors[5] * branch_full
    grad_scale_two = jnp.sum(weighted * branch_full, axis=(0, 1))
    grad_shift_out = jnp.sum(branch_grad, axis=0)
    second_grad = second_grad.reshape(images, pixels, width)
    grad_gain_two = jnp.sum(second_grad * second_scaled, axis=(0, 1))
    grad_shift_two = jnp.sum(second_grad, axis=(0, 1))
    middle_grad = weighted + norm_back(second_grad * vectors[3], second_scaled, second_inverse)
    grad_scale_one = jnp.sum(middle_grad * mixed, axis=(0, 1))
    mixed_grad = middle_grad * vectors[2]
    normed_grad = (
        jnp.einsum("qp,iqc->ipc", pool, mixed_grad, precision=lax.Precision.HIGHEST) - mixed_grad
    )
    grad_gain_one = jnp.sum(normed_grad * first_scaled, axis=(0, 1))
    grad_shift_one = jnp.sum(normed_grad, axis=(0, 1))
    input_grad = middle_grad + norm_back(normed_grad * vectors[0], first_scaled, first_inverse)
    vector_part = jnp.stack(
        [
            grad_gain_one,
            grad_shift_one,
            grad_scale_one,
            grad_gain_two,
            grad_shift_two,
            grad_scale_two,
            grad_shift_out,
        ]
    )
    vector_grad, bias_grad = lax.psum((vector_part, bias_part), ("narrow", "wide"))
    hidden_grad_sum, output_grad_sum = lax.psum((hidden_part, output_total), "narrow")
    hidden_new = adamw_update(
        hidden_weight, hidden_grad_sum, hidden_moment, hidden_square, 0.04, weight_shrink
    )
    bias_new = adamw_update(hidden_bias, bias_grad, bias_moment, bias_square, 0.2, 0.0)
    output_new = adamw_update(
        output_weight, output_grad_sum, output_moment, output_square, 0.02, weight_shrink
    )
    vector_new = adamw_update(vectors, vector_grad, vector_moment, vector_square, 0.3, 0.0)
    return (
        block_out,
        input_grad,
        hidden_new[0],
        hidden_new[1],
        hidden_new[2],
        bias_new[0],
        bias_new[1],
        bias_new[2],
        output_new[0],
        output_new[1],
        output_new[2],
        vector_new[0],
        vector_new[1],
        vector_new[2],
    )


f32 = jnp.float32
bf16 = jnp.bfloat16
VMEM = pl.BlockSpec(memory_space=pltpu.VMEM)
SMEM = pl.BlockSpec(memory_space=pltpu.SMEM)


def row_total(values):
    return jnp.sum(values, axis=1, keepdims=True)


def span(i):
    return min(i + 1, SIDE - 1) - max(i - 1, 0) + 1


def near_share(p):
    return 1.0 / (span(p // SIDE) * span(p % SIDE))


def along_row(load, p):
    c = p % SIDE
    total = load(p)
    if c > 0:
        total = total + load(p - 1)
    if c < SIDE - 1:
        total = total + load(p + 1)
    return total


def along_col(load, p):
    r = p // SIDE
    total = load(p)
    if r > 0:
        total = total + load(p - SIDE)
    if r < SIDE - 1:
        total = total + load(p + SIDE)
    return total


def valid_gate(counts_ref, shape):
    slots = lax.broadcasted_iota(jnp.int32, shape, 0)
    return jnp.where(slots < counts_ref[0], 1.0, 0.0)


def mixed_parts(x_ref, mu1, r1, vec_ref, h_ref, q_ref):
    for p in range(x_ref.shape[0]):
        h_ref[p] = along_row(lambda i: x_ref[i] - mu1, p)
    for p in range(x_ref.shape[0]):
        q_ref[p] = along_col(lambda i: h_ref[i], p) * near_share(p) - (x_ref[p] - mu1)
    return vec_ref[2:3, :] * (r1 * vec_ref[0:1, :])


def normal_parts(h):
    d = 1.0 + (0.3275911 / math.sqrt(2.0)) * jnp.abs(h)
    t = pl.reciprocal(d, approx=True)
    t = t * (2.0 - d * t)
    series = 0.5 * 1.061405429
    for c in (-1.453152027, 1.421413741, -0.284496736, 0.254829592):
        series = series * t + 0.5 * c
    e = jnp.exp2((-0.5 * math.log2(math.e)) * (h * h))
    tail = series * t * e
    phi = jnp.where(h < 0.0, tail, 1.0 - tail)
    return phi, phi + h * (e * (1.0 / math.sqrt(2.0 * math.pi)))


def dot(left, right, dims):
    return lax.dot_general(left, right, (dims, ((), ())), preferred_element_type=f32)


def joined(refs):
    chunks = [[ref[1, c * 128 : (c + 1) * 128, :] for c in range(4)] for ref in refs]
    return (
        jnp.concatenate([ref[0] for ref in refs], axis=1),
        jnp.concatenate([jnp.concatenate(row, axis=1) for row in chunks], axis=0),
    )


def block_places():
    near, wide = lax.axis_index("narrow"), lax.axis_index("wide")
    far_step = 8 + 4 * near
    other_step = 12 - 4 * near
    return [wide ^ step for step in (0, 2, 4, far_step, far_step ^ 2, other_step, other_step ^ 2, 6)]


def block_bias(bias_ref, places, at):
    return jnp.concatenate([bias_ref[pl.ds(places[at + k], 1), :] for k in range(2)], axis=1)


def block_rows(second, upstream, a, b, bias):
    h = dot(second, a, ((1,), (0,))) + bias
    back = dot(upstream, b, ((1,), (1,)))
    phi, slope = normal_parts(h)
    active = (h * phi).astype(bf16)
    low = (back * slope).astype(bf16)
    column = jnp.sum(low.astype(f32), axis=0, keepdims=True)
    grads = [dot(left, right, ((0,), (0,))) for left, right in ((second, low), (active, upstream))]
    return active, low, column, grads


def pre_kernel(
    counts_ref, x_ref, cot_ref, vec_ref, bias_ref, w0_ref, w1_ref,
    sb_ref, stat_ref, act_ref, low_ref, column_ref, part_a, part_b, d_ref, h_ref,
):
    pixels, images, width = x_ref.shape
    size = pixels * width
    zero = jnp.zeros((images, width), f32)

    def loop(body, init):
        return lax.fori_loop(0, pixels, body, init, unroll=7)

    mu1 = row_total(loop(lambda p, s: s + x_ref[p], zero)) / size

    def centre(p, s):
        d = x_ref[p] - mu1
        return s + d * d

    r1 = lax.rsqrt(row_total(loop(centre, zero)) / size + norm_epsilon)
    lift = mixed_parts(x_ref, mu1, r1, vec_ref, h_ref, d_ref)

    def middle(p, s):
        m = x_ref[p] + lift * d_ref[p]
        h_ref[p] = m
        return s + m

    total = loop(middle, zero)
    mu2 = row_total(total) / size

    def spread(p, s):
        d = h_ref[p] - mu2
        d_ref[p] = d
        return s + d * d

    r2 = lax.rsqrt(row_total(loop(spread, zero)) / size + norm_epsilon)
    scale = r2 * vec_ref[3:4, :]
    shift = jnp.broadcast_to(vec_ref[4:5, :], (images, width))
    gate = valid_gate(counts_ref, (images, width)) * vec_ref[5:6, :]

    def finish(p, carry):
        sb_ref[0, p] = (d_ref[p] * scale + shift).astype(bf16)
        sb_ref[1, p] = (cot_ref[p].astype(f32) * gate).astype(bf16)
        return carry

    loop(finish, 0)
    for i, stat in enumerate((mu1, r1, mu2, r2)):
        stat_ref[i] = jnp.broadcast_to(stat, (images, 128))
    second, upstream = (sb_ref[i].reshape(pixels * images, width) for i in range(2))
    a, b = joined((w0_ref, w1_ref))
    bias = block_bias(bias_ref, block_places(), 0)
    act_ref[...], low_ref[...], column_ref[...], grads = block_rows(second, upstream, a, b, bias)
    part_a[...], part_b[...] = grads


def side_by_side(refs, j):
    left, right = refs[2 * j], refs[2 * j + 1]
    return jnp.concatenate([left[...], right[...]], axis=1)


def cast_kernel(a_ref, b_ref, out_ref):
    out_ref[0] = a_ref[...].astype(bf16)
    low = b_ref[...].astype(bf16)
    for c in range(4):
        out_ref[1, c * 128 : (c + 1) * 128, :] = low[:, c * 128 : (c + 1) * 128]


def block_kernel(first, count, own_ref, oth_ref, bias_ref, *refs):
    w_refs, refs = refs[:count], refs[count:]
    begun, refs = (refs[:5], refs[5:]) if first == 0 else (None, refs)
    act_ref, low_ref, sums_ref, *outs = refs
    sums_ref[...] = jnp.zeros_like(sums_ref)
    places = block_places()
    for j in range(count // 2):
        bias = block_bias(bias_ref, places, first + 2 * j)
        a, b = joined(w_refs[2 * j : 2 * j + 2])
        columns = slice(j * 256, (j + 1) * 256)
        grads = sums = None
        for r, sb_ref in enumerate((own_ref, oth_ref)):
            if begun is not None and j == r == 0:
                active, low, column, *parts = (ref[...] for ref in begun)
            else:
                active, low, column, parts = block_rows(sb_ref[0], sb_ref[1], a, b, bias)
            act_ref[r, :, columns] = active
            low_ref[r, :, columns] = low
            sums = column if r == 0 else sums + column
            grads = parts if r == 0 else [total + part for total, part in zip(grads, parts)]
        for k in range(2):
            half = slice(k * 128, (k + 1) * 128)
            sums_ref[pl.ds(places[first + 2 * j + k], 1), :] = sums[:, half]
            out_ref = outs[2 * j + k]
            out_ref[0] = grads[0][:, half].astype(out_ref.dtype)
            for c in range(4):
                chunk = slice(c * 128, (c + 1) * 128)
                out_ref[1, chunk, :] = grads[1][half, chunk].astype(out_ref.dtype)


def back_kernel(sides, counts, started, *refs):
    n = len(counts)
    acts, lows, refs = refs[:n], refs[n : 2 * n], refs[2 * n :]
    w_refs, refs = refs[: sum(counts)], refs[sum(counts) :]
    old, totals = (refs[: len(sides)], refs[len(sides) :]) if started else (None, refs)
    for at, r in enumerate(sides):
        for i, lefts in enumerate((acts, lows)):
            total = None if old is None else old[at][i]
            w = 0
            for left_ref in lefts:
                for j in range(left_ref.shape[2] // 256):
                    left = left_ref[r, :, j * 256 : (j + 1) * 256]
                    weight = joined(w_refs[w : w + 2])[1 - i]
                    part = dot(left, weight, ((1,), (i,)))
                    total = part if total is None else total + part
                    w += 2
            totals[at][i] = total.astype(totals[at].dtype)


def update_kernel(own_ref, got_ref, sums_ref, *refs):
    state, outs = [refs[i : i + 3] for i in range(0, 12, 3)], refs[12:]
    grads = wide_sum(own_ref[...], got_ref[...])
    lines = state[1][0].shape[0]
    wide = [
        jnp.concatenate([sums_ref[lines + 4 * i + k : lines + 4 * i + k + 1, :] for k in range(4)], axis=1)
        for i in range(state[3][0].shape[0])
    ]
    settings = (
        (grads[0], 0.04, weight_shrink),
        (sums_ref[:lines, :], 0.2, 0.0),
        (jnp.concatenate([grads[1, c * 128 : (c + 1) * 128, :] for c in range(4)], axis=1), 0.02, weight_shrink),
        (jnp.concatenate(wide, axis=0), 0.3, 0.0),
    )
    for n, (grad, rate, shrink) in enumerate(settings):
        param, moment, square = (ref[...] for ref in state[n])
        new = adamw_update(param, grad, moment, square, rate, shrink)
        for ref, values in zip(outs[3 * n : 3 * n + 3], new):
            ref[...] = values


def post_kernel(
    counts_ref, x_ref, cot_ref, vec_ref, stat_ref, own_ref, got_ref, *refs
):
    bias_refs, (out_ref, grad_ref, sums_ref, t_ref, h_ref, q_ref) = refs[:-6], refs[-6:]
    pixels, images, width = x_ref.shape
    size = pixels * width
    zero = jnp.zeros((images, width), f32)
    gate = valid_gate(counts_ref, (images, width))
    mu1, r1, mu2, r2 = (stat_ref[i][:, 0:1] for i in range(4))
    gain1, mix, gain2, scale, lower = (vec_ref[i : i + 1, :] for i in (0, 2, 3, 5, 6))
    lift = mixed_parts(x_ref, mu1, r1, vec_ref, h_ref, q_ref)

    def loop(body, init):
        return lax.fori_loop(0, pixels, body, init, unroll=7)

    def column(values):
        return jnp.sum(values, axis=0, keepdims=True)

    def first(p, carry):
        g_scale, g_lower, g_gain2, g_shift2 = carry
        middle = x_ref[p] + lift * q_ref[p]
        branch = own_ref[0, p] + got_ref[0, p].astype(f32) + lower
        out_ref[p] = middle + scale * branch
        weighted = cot_ref[p].astype(f32) * gate
        back = own_ref[1, p] + got_ref[1, p].astype(f32)
        h2 = (middle - mu2) * r2
        return (g_scale + weighted * branch, g_lower + weighted, g_gain2 + back * h2, g_shift2 + back)

    g_scale, g_lower, g_gain2, g_shift2 = loop(first, (zero,) * 4)
    mean2 = row_total(g_shift2 * gain2) / size
    mean2h = row_total(g_gain2 * gain2) / size

    def second(p, g_mix):
        middle = x_ref[p] + lift * q_ref[p]
        back = own_ref[1, p] + got_ref[1, p].astype(f32)
        h2 = (middle - mu2) * r2
        grad = cot_ref[p].astype(f32) * gate + r2 * (back * gain2 - mean2 - h2 * mean2h)
        grad_ref[p] = grad
        t_ref[p] = grad * mix
        return g_mix + grad * q_ref[p]

    g_mix = loop(second, zero) * (r1 * gain1)
    for p in range(pixels):
        h_ref[p] = along_row(lambda i: t_ref[i] * near_share(i), p)
    g_gain1 = g_shift1 = zero
    for p in range(pixels):
        ng = along_col(lambda i: h_ref[i], p) - t_ref[p]
        t_ref[p] = ng
        g_gain1 = g_gain1 + ng * ((x_ref[p] - mu1) * r1)
        g_shift1 = g_shift1 + ng
    mean1 = row_total(g_shift1 * gain1) / size
    mean1h = row_total(g_gain1 * gain1) / size

    def third(p, carry):
        h1 = (x_ref[p] - mu1) * r1
        grad_ref[p] = grad_ref[p] + r1 * (t_ref[p] * gain1 - mean1 - h1 * mean1h)
        return carry

    loop(third, 0)
    lines = bias_refs[0].shape[0]
    sums_ref[:lines, :] = bias_refs[0][...] + bias_refs[1][...] + bias_refs[2][...]
    for i, total in enumerate((g_gain1, g_shift1, g_mix, g_gain2, g_shift2, g_scale, g_lower * scale)):
        total = column(total)
        for k in range(width // 128):
            row = lines + (width // 128) * i + k
            sums_ref[row : row + 1, :] = total[:, k * 128 : (k + 1) * 128]


def call(kernel, outs, ins, scratch=(), vmem=12, smem=0, hold=True, loose=()):
    many = isinstance(outs, (list, tuple))
    arrays = (*ins, *(outs if many else [outs]))
    moved = sum(math.prod(v.shape) * v.dtype.itemsize for v in arrays)
    if hold:
        outs = [pltpu.VMEM(v.shape, v.dtype) for v in outs] if many else pltpu.VMEM(outs.shape, outs.dtype)
    ins = [
        v
        if i < smem or not (hold or i in loose)
        else pltpu.with_memory_space_constraint(v, pltpu.HBM if i in loose else pltpu.VMEM)
        for i, v in enumerate(ins)
    ]
    return pl.pallas_call(
        kernel,
        out_shape=outs,
        in_specs=[SMEM] * smem + [VMEM] * (len(ins) - smem),
        out_specs=[VMEM] * len(outs) if many else VMEM,
        scratch_shapes=list(scratch),
        name=getattr(kernel, "func", kernel).__name__,
        compiler_params=pltpu.CompilerParams(vmem_limit_bytes=vmem * 2**20),
        cost_estimate=pl.CostEstimate(flops=0, bytes_accessed=moved, transcendentals=0),
    )(*ins)


def struct(shape, dtype=f32):
    return jax.ShapeDtypeStruct(shape, dtype)


BOTH = ("narrow", "wide")


def joint(values, change):
    pairs = [(n * 16 + w, change(n, w)) for n in range(2) for w in range(16)]
    return lax.ppermute(values, BOTH, [(s, n * 16 + w) for s, (n, w) in pairs])


def flip(values, bit):
    return lax.ppermute(values, "wide", [(w, w ^ bit) for w in range(16)])


def far(values):
    return joint(values, lambda n, w: (n, w ^ (12 if n else 8)))


def across(values):
    return lax.ppermute(values, "narrow", [(0, 1), (1, 0)])


def diagonal(values):
    return joint(values, lambda n, w: (1 - n, w ^ 2))


def after(values, *others):
    return lax.optimization_barrier((values, *others))[0]


def wide_sum(*parts):
    total = parts[0].astype(f32)
    for part in parts[1:]:
        total = total + part.astype(f32)
    return total


def local_tree(
    features,
    cotangent,
    counts,
    hidden_weight,
    hidden_bias,
    output_weight,
    vectors,
    hidden_moment,
    hidden_square,
    bias_moment,
    bias_square,
    output_moment,
    output_square,
    vector_moment,
    vector_square,
):
    images, pixels, width = features.shape
    rows = images * pixels
    units = hidden_weight.shape[1]
    pair, pair_f = struct((2, width, units), bf16), struct((2, width, units))
    w0 = call(cast_kernel, pair, (hidden_weight, output_weight), loose=(0, 1))
    wz1, wzf, wy0 = flip(w0, 4), far(w0), flip(w0, 2)
    vectors_late, wy0 = lax.optimization_barrier((vectors, wy0))
    bias = hidden_bias.reshape(-1, 128)
    x = features.transpose(1, 0, 2)
    cot = cotangent.transpose(1, 0, 2)
    big = struct((pixels, images, width))
    keep = pltpu.VMEM((pixels, images, width), f32)
    tile = struct((rows, 256), bf16)
    sb, stat, *begun = call(
        pre_kernel,
        [
            struct((2, pixels, images, width), bf16),
            struct((4, images, 128)),
            tile,
            tile,
            struct((1, 256)),
            struct((width, 256)),
            struct((256, width)),
        ],
        (counts, x, cot, vectors_late, bias, w0, wy0),
        [keep, keep],
        smem=1,
        loose=(1, 2, 3),
        vmem=20,
    )
    sb = after(sb.reshape(2, rows, width), wzf, wz1, wy0)
    other = flip(sb, 1)
    wyf, wzo = flip(wzf, 2), across(wzf)
    total, total_low = struct((2, rows, width)), struct((2, rows, width), bf16)

    lines = struct(bias.shape)

    def blocks(first, weights, results, begun=()):
        tall = struct((2, rows, 128 * len(weights)), bf16)
        return call(
            functools.partial(block_kernel, first, len(weights)),
            [tall, tall, lines, *results],
            (sb, other, bias, *weights, *begun),
            vmem=20,
        )

    def back(sides, results, hidden, weights, old=(), loose=()):
        acts, lows = zip(*hidden)
        counts = [act.shape[2] // 128 for act in acts]
        kernel = functools.partial(back_kernel, sides, counts, bool(old))
        return call(kernel, results, (*acts, *lows, *weights, *old), loose=loose)

    w_near = [w0, wy0, wz1, wzf]
    *near_hidden, sums1, g0, gy0, gz1, gzf = blocks(0, w_near, [pair_f, pair, pair, pair_f], begun)
    z1 = flip(gz1, 4)
    wy1 = flip(after(wz1, sums1), 2)
    wyf = after(wyf, sums1)
    wyo = across(wyf)
    *far_hidden, sums2, gyf, gzo = blocks(4, [wyf, wzo], [pair, pair])
    yf, xs = flip(gyf, 2), across(gzo)
    old = back((0, 1), [total, total], (near_hidden, far_hidden), [*w_near, wyf, wzo])
    wyo, wy1, _ = lax.optimization_barrier((wyo, wy1, old[0]))
    *last_hidden, sums3, gyo, gy1 = blocks(6, [wyo, wy1], [pair, pair])
    ds, zy = diagonal(gyo), flip(gy1, 4)
    theirs = back((1,), [total_low], (last_hidden,), [wyo, wy1], old[1:])[0]
    theirs, yf, xs, z1 = lax.optimization_barrier((theirs, yf, xs, z1))
    got = flip(theirs, 1)
    mine = back((0,), [total], (last_hidden,), [wyo, wy1], old[:1])[0]

    shape = (2, pixels, images, width)
    payload = struct((bias.shape[0] + vectors.size // 128, 128))
    block_out, input_grad, sums = call(
        post_kernel,
        [big, big, payload],
        (counts, x, cot, vectors, stat, mine.reshape(shape), got.reshape(shape), sums1, sums2, sums3),
        [keep, keep, keep],
        smem=1,
        hold=False,
    )
    ds, zy, _ = lax.optimization_barrier((ds, zy, sums))
    sum_f = wide_sum(gzf, xs, yf, ds).astype(bf16)
    zf = far(sum_f)
    sums = sums + flip(sums, 1)
    sums = after(sums, sum_f)
    y0 = flip(after(wide_sum(gy0, zy).astype(bf16), sums), 2)
    sums = sums + across(sums)
    sums = sums + flip(sums, 2)
    own = wide_sum(g0, y0, z1, zf).astype(bf16)
    own, sums = lax.optimization_barrier((own, sums))
    got = across(own)
    for bit in (4, 8):
        sums = sums + flip(sums, bit)
    state = (
        (hidden_weight, hidden_moment, hidden_square),
        tuple(v.reshape(bias.shape) for v in (hidden_bias, bias_moment, bias_square)),
        (output_weight, output_moment, output_square),
        (vectors, vector_moment, vector_square),
    )
    new = call(
        update_kernel,
        [struct(v.shape) for group in state for v in group],
        (own, got, sums, *(v for group in state for v in group)),
        hold=False,
    )
    hidden_new, output_new, vector_new = new[:3], new[6:9], new[9:]
    bias_new = [v.reshape(hidden_bias.shape) for v in new[3:6]]
    return (
        block_out.transpose(1, 0, 2),
        input_grad.transpose(1, 0, 2),
        *hidden_new,
        *bias_new,
        *output_new,
        *vector_new,
    )


def solution(mesh):
    in_specs = (
        P(("narrow", "wide"), None, None),
        P(("narrow", "wide"), None, None),
        P(("narrow", "wide")),
        P(None, "wide"),
        P(),
        P("wide", None),
        P(),
        P(None, "wide"),
        P(None, "wide"),
        P(),
        P(),
        P("wide", None),
        P("wide", None),
        P(),
        P(),
    )
    out_specs = (
        P(("narrow", "wide"), None, None),
        P(("narrow", "wide"), None, None),
        P(None, "wide"),
        P(None, "wide"),
        P(None, "wide"),
        P(),
        P(),
        P(),
        P("wide", None),
        P("wide", None),
        P("wide", None),
        P(),
        P(),
        P(),
    )
    body = local_tree if dict(mesh.shape) == {"narrow": 2, "wide": 16} else local
    return jax.shard_map(body, mesh=mesh, in_specs=in_specs, out_specs=out_specs, check_vma=False)
```

```python
import functools
import math

import jax
import jax.numpy as jnp
from jax import lax
from jax.experimental import pallas as pl
from jax.experimental.pallas import tpu as pltpu
from jax.sharding import PartitionSpec as P

SIDE = 7
STEP = 5


norm_epsilon = 1e-05
first_decay = 0.9
second_decay = 0.999
adam_epsilon = 1e-08
weight_shrink = 0.05


def pool_matrix(side):
    places = jnp.arange(side * side, dtype=jnp.int32)
    place_row = places // side
    place_col = places % side
    nearby = (jnp.abs(place_row[:, None] - place_row[None, :]) <= 1) & (
        jnp.abs(place_col[:, None] - place_col[None, :]) <= 1
    )
    nearby = nearby.astype(jnp.float32)
    return nearby / jnp.sum(nearby, axis=1, keepdims=True)


def norm_parts(values, gain, shift):
    centre = jnp.mean(values, axis=(1, 2), keepdims=True)
    spread = jnp.mean((values - centre) ** 2, axis=(1, 2), keepdims=True)
    inverse = lax.rsqrt(spread + norm_epsilon)
    scaled = (values - centre) * inverse
    return (scaled * gain + shift, scaled, inverse)


def norm_back(upstream, scaled, inverse):
    first_mean = jnp.mean(upstream, axis=(1, 2), keepdims=True)
    second_mean = jnp.mean(upstream * scaled, axis=(1, 2), keepdims=True)
    return inverse * (upstream - first_mean - scaled * second_mean)


def gelu_slope(values):
    return 0.5 * (1.0 + lax.erf(values / math.sqrt(2.0))) + values * jnp.exp(
        -0.5 * values * values
    ) / math.sqrt(2.0 * math.pi)


def contract_rows(left, right):
    return lax.dot_general(
        left, right, (((0,), (0,)), ((), ())), preferred_element_type=jnp.float32
    )


def contract_cols(left, right):
    return lax.dot_general(
        left, right, (((1,), (1,)), ((), ())), preferred_element_type=jnp.float32
    )


def adamw_update(param, grad, moment, square, rate, shrink):
    moment_new = first_decay * moment + (1.0 - first_decay) * grad
    square_new = second_decay * square + (1.0 - second_decay) * grad * grad
    moment_hat = moment_new / (1.0 - first_decay**STEP)
    square_hat = square_new / (1.0 - second_decay**STEP)
    param_new = param - rate * (moment_hat / (jnp.sqrt(square_hat) + adam_epsilon) + shrink * param)
    return (param_new, moment_new, square_new)


def local(
    features,
    cotangent,
    counts,
    hidden_weight,
    hidden_bias,
    output_weight,
    vectors,
    hidden_moment,
    hidden_square,
    bias_moment,
    bias_square,
    output_moment,
    output_square,
    vector_moment,
    vector_square,
):
    images, pixels, width = features.shape
    rows = images * pixels
    units = hidden_weight.shape[1]
    pool = pool_matrix(SIDE)
    valid = (jnp.arange(images, dtype=jnp.int32) < counts[0]).astype(jnp.float32)
    weighted = cotangent.astype(jnp.float32) * valid[:, None, None]
    normed, first_scaled, first_inverse = norm_parts(features, vectors[0], vectors[1])
    mixed = jnp.einsum("pq,iqc->ipc", pool, normed, precision=lax.Precision.HIGHEST) - normed
    middle = features + vectors[2] * mixed
    second, second_scaled, second_inverse = norm_parts(middle, vectors[3], vectors[4])
    second_low = second.reshape(rows, width).astype(jnp.bfloat16)
    hidden_low = hidden_weight.astype(jnp.bfloat16)
    output_low = output_weight.astype(jnp.bfloat16)
    branch_grad = (weighted * vectors[5]).reshape(rows, width)
    branch_low = branch_grad.astype(jnp.bfloat16)
    offset = lax.axis_index("wide") * units
    local_bias = lax.dynamic_slice_in_dim(hidden_bias, offset, units)
    hidden_all = (
        jnp.dot(
            lax.all_gather(second_low, "wide", axis=0, tiled=True),
            hidden_low,
            preferred_element_type=jnp.float32,
        )
        + local_bias
    )
    active_all = jax.nn.gelu(hidden_all, approximate=False).astype(jnp.bfloat16)
    slope_all = gelu_slope(hidden_all)
    block = active_all
    branch = lax.psum_scatter(
        jnp.dot(block, output_low, preferred_element_type=jnp.float32),
        "wide",
        scatter_dimension=0,
        tiled=True,
    )
    piece = lax.all_gather(branch_low, "wide", axis=0, tiled=True)
    block = active_all
    output_total = contract_rows(block, piece)
    active_grad = contract_cols(piece, output_low)
    hidden_grad = (active_grad * slope_all).astype(jnp.bfloat16)
    local_bias_grad = jnp.sum(hidden_grad.astype(jnp.float32), axis=0)
    bias_part = lax.dynamic_update_slice_in_dim(
        jnp.zeros(hidden_bias.shape, jnp.float32), local_bias_grad, offset, 0
    )
    block = hidden_grad
    second_grad = lax.psum_scatter(
        contract_cols(block, hidden_low), "wide", scatter_dimension=0, tiled=True
    )
    block = hidden_grad
    hidden_part = contract_rows(lax.all_gather(second_low, "wide", axis=0, tiled=True), block)
    branch_full = (branch + vectors[6]).reshape(images, pixels, width)
    block_out = middle + vectors[5] * branch_full
    grad_scale_two = jnp.sum(weighted * branch_full, axis=(0, 1))
    grad_shift_out = jnp.sum(branch_grad, axis=0)
    second_grad = second_grad.reshape(images, pixels, width)
    grad_gain_two = jnp.sum(second_grad * second_scaled, axis=(0, 1))
    grad_shift_two = jnp.sum(second_grad, axis=(0, 1))
    middle_grad = weighted + norm_back(second_grad * vectors[3], second_scaled, second_inverse)
    grad_scale_one = jnp.sum(middle_grad * mixed, axis=(0, 1))
    mixed_grad = middle_grad * vectors[2]
    normed_grad = (
        jnp.einsum("qp,iqc->ipc", pool, mixed_grad, precision=lax.Precision.HIGHEST) - mixed_grad
    )
    grad_gain_one = jnp.sum(normed_grad * first_scaled, axis=(0, 1))
    grad_shift_one = jnp.sum(normed_grad, axis=(0, 1))
    input_grad = middle_grad + norm_back(normed_grad * vectors[0], first_scaled, first_inverse)
    vector_part = jnp.stack(
        [
            grad_gain_one,
            grad_shift_one,
            grad_scale_one,
            grad_gain_two,
            grad_shift_two,
            grad_scale_two,
            grad_shift_out,
        ]
    )
    vector_grad, bias_grad = lax.psum((vector_part, bias_part), ("narrow", "wide"))
    hidden_grad_sum, output_grad_sum = lax.psum((hidden_part, output_total), "narrow")
    hidden_new = adamw_update(
        hidden_weight, hidden_grad_sum, hidden_moment, hidden_square, 0.04, weight_shrink
    )
    bias_new = adamw_update(hidden_bias, bias_grad, bias_moment, bias_square, 0.2, 0.0)
    output_new = adamw_update(
        output_weight, output_grad_sum, output_moment, output_square, 0.02, weight_shrink
    )
    vector_new = adamw_update(vectors, vector_grad, vector_moment, vector_square, 0.3, 0.0)
    return (
        block_out,
        input_grad,
        hidden_new[0],
        hidden_new[1],
        hidden_new[2],
        bias_new[0],
        bias_new[1],
        bias_new[2],
        output_new[0],
        output_new[1],
        output_new[2],
        vector_new[0],
        vector_new[1],
        vector_new[2],
    )


f32 = jnp.float32
bf16 = jnp.bfloat16
VMEM = pl.BlockSpec(memory_space=pltpu.VMEM)
SMEM = pl.BlockSpec(memory_space=pltpu.SMEM)


def row_total(values):
    return jnp.sum(values, axis=1, keepdims=True)


def span(i):
    return min(i + 1, SIDE - 1) - max(i - 1, 0) + 1


def near_share(p):
    return 1.0 / (span(p // SIDE) * span(p % SIDE))


def along_row(load, p):
    c = p % SIDE
    total = load(p)
    if c > 0:
        total = total + load(p - 1)
    if c < SIDE - 1:
        total = total + load(p + 1)
    return total


def along_col(load, p):
    r = p // SIDE
    total = load(p)
    if r > 0:
        total = total + load(p - SIDE)
    if r < SIDE - 1:
        total = total + load(p + SIDE)
    return total


def valid_gate(counts_ref, shape):
    slots = lax.broadcasted_iota(jnp.int32, shape, 0)
    return jnp.where(slots < counts_ref[0], 1.0, 0.0)


def mixed_parts(x_ref, mu1, r1, vec_ref, h_ref, q_ref):
    for p in range(x_ref.shape[0]):
        h_ref[p] = along_row(lambda i: x_ref[i] - mu1, p)
    for p in range(x_ref.shape[0]):
        q_ref[p] = along_col(lambda i: h_ref[i], p) * near_share(p) - (x_ref[p] - mu1)
    return vec_ref[2:3, :] * (r1 * vec_ref[0:1, :])


def normal_parts(h):
    d = 1.0 + (0.3275911 / math.sqrt(2.0)) * jnp.abs(h)
    t = pl.reciprocal(d, approx=True)
    t = t * (2.0 - d * t)
    series = 0.5 * 1.061405429
    for c in (-1.453152027, 1.421413741, -0.284496736, 0.254829592):
        series = series * t + 0.5 * c
    e = jnp.exp2((-0.5 * math.log2(math.e)) * (h * h))
    tail = series * t * e
    phi = jnp.where(h < 0.0, tail, 1.0 - tail)
    return phi, phi + h * (e * (1.0 / math.sqrt(2.0 * math.pi)))


def dot(left, right, dims):
    return lax.dot_general(left, right, (dims, ((), ())), preferred_element_type=f32)


def joined(refs):
    chunks = [[ref[1, c * 128 : (c + 1) * 128, :] for c in range(4)] for ref in refs]
    return (
        jnp.concatenate([ref[0] for ref in refs], axis=1),
        jnp.concatenate([jnp.concatenate(row, axis=1) for row in chunks], axis=0),
    )


def block_places():
    near, wide = lax.axis_index("narrow"), lax.axis_index("wide")
    far_step = 8 + 4 * near
    other_step = 12 - 4 * near
    return [wide ^ step for step in (0, 2, 4, far_step, far_step ^ 2, other_step, other_step ^ 2, 6)]


def block_bias(bias_ref, places, at):
    return jnp.concatenate([bias_ref[pl.ds(places[at + k], 1), :] for k in range(2)], axis=1)


def block_rows(second, upstream, a, b, bias):
    h = dot(second, a, ((1,), (0,))) + bias
    back = dot(upstream, b, ((1,), (1,)))
    phi, slope = normal_parts(h)
    active = (h * phi).astype(bf16)
    low = (back * slope).astype(bf16)
    column = jnp.sum(low.astype(f32), axis=0, keepdims=True)
    grads = [dot(left, right, ((0,), (0,))) for left, right in ((second, low), (active, upstream))]
    return active, low, column, grads


def pre_kernel(
    counts_ref, x_ref, cot_ref, vec_ref, bias_ref, w0_ref, w1_ref,
    sb_ref, stat_ref, act_ref, low_ref, column_ref, part_a, part_b, d_ref, h_ref,
):
    pixels, images, width = x_ref.shape
    size = pixels * width
    zero = jnp.zeros((images, width), f32)

    def loop(body, init):
        return lax.fori_loop(0, pixels, body, init, unroll=7)

    mu1 = row_total(loop(lambda p, s: s + x_ref[p], zero)) / size

    def centre(p, s):
        d = x_ref[p] - mu1
        return s + d * d

    r1 = lax.rsqrt(row_total(loop(centre, zero)) / size + norm_epsilon)
    lift = mixed_parts(x_ref, mu1, r1, vec_ref, h_ref, d_ref)

    def middle(p, s):
        m = x_ref[p] + lift * d_ref[p]
        h_ref[p] = m
        return s + m

    total = loop(middle, zero)
    mu2 = row_total(total) / size

    def spread(p, s):
        d = h_ref[p] - mu2
        d_ref[p] = d
        return s + d * d

    r2 = lax.rsqrt(row_total(loop(spread, zero)) / size + norm_epsilon)
    scale = r2 * vec_ref[3:4, :]
    shift = jnp.broadcast_to(vec_ref[4:5, :], (images, width))
    gate = valid_gate(counts_ref, (images, width)) * vec_ref[5:6, :]

    def finish(p, carry):
        sb_ref[0, p] = (d_ref[p] * scale + shift).astype(bf16)
        sb_ref[1, p] = (cot_ref[p].astype(f32) * gate).astype(bf16)
        return carry

    loop(finish, 0)
    for i, stat in enumerate((mu1, r1, mu2, r2)):
        stat_ref[i] = jnp.broadcast_to(stat, (images, 128))
    second, upstream = (sb_ref[i].reshape(pixels * images, width) for i in range(2))
    a, b = joined((w0_ref, w1_ref))
    bias = block_bias(bias_ref, block_places(), 0)
    act_ref[...], low_ref[...], column_ref[...], grads = block_rows(second, upstream, a, b, bias)
    part_a[...], part_b[...] = grads


def side_by_side(refs, j):
    left, right = refs[2 * j], refs[2 * j + 1]
    return jnp.concatenate([left[...], right[...]], axis=1)


def cast_kernel(a_ref, b_ref, out_ref):
    out_ref[0] = a_ref[...].astype(bf16)
    low = b_ref[...].astype(bf16)
    for c in range(4):
        out_ref[1, c * 128 : (c + 1) * 128, :] = low[:, c * 128 : (c + 1) * 128]


def block_kernel(first, count, own_ref, oth_ref, bias_ref, *refs):
    w_refs, refs = refs[:count], refs[count:]
    begun, refs = (refs[:5], refs[5:]) if first == 0 else (None, refs)
    act_ref, low_ref, sums_ref, *outs = refs
    sums_ref[...] = jnp.zeros_like(sums_ref)
    places = block_places()
    for j in range(count // 2):
        bias = block_bias(bias_ref, places, first + 2 * j)
        a, b = joined(w_refs[2 * j : 2 * j + 2])
        columns = slice(j * 256, (j + 1) * 256)
        grads = sums = None
        for r, sb_ref in enumerate((own_ref, oth_ref)):
            if begun is not None and j == r == 0:
                active, low, column, *parts = (ref[...] for ref in begun)
            else:
                active, low, column, parts = block_rows(sb_ref[0], sb_ref[1], a, b, bias)
            act_ref[r, :, columns] = active
            low_ref[r, :, columns] = low
            sums = column if r == 0 else sums + column
            grads = parts if r == 0 else [total + part for total, part in zip(grads, parts)]
        for k in range(2):
            half = slice(k * 128, (k + 1) * 128)
            sums_ref[pl.ds(places[first + 2 * j + k], 1), :] = sums[:, half]
            out_ref = outs[2 * j + k]
            out_ref[0] = grads[0][:, half].astype(out_ref.dtype)
            for c in range(4):
                chunk = slice(c * 128, (c + 1) * 128)
                out_ref[1, chunk, :] = grads[1][half, chunk].astype(out_ref.dtype)


def back_kernel(sides, counts, started, *refs):
    n = len(counts)
    acts, lows, refs = refs[:n], refs[n : 2 * n], refs[2 * n :]
    w_refs, refs = refs[: sum(counts)], refs[sum(counts) :]
    old, totals = (refs[: len(sides)], refs[len(sides) :]) if started else (None, refs)
    for at, r in enumerate(sides):
        for i, lefts in enumerate((acts, lows)):
            total = None if old is None else old[at][i]
            w = 0
            for left_ref in lefts:
                for j in range(left_ref.shape[2] // 256):
                    left = left_ref[r, :, j * 256 : (j + 1) * 256]
                    weight = joined(w_refs[w : w + 2])[1 - i]
                    part = dot(left, weight, ((1,), (i,)))
                    total = part if total is None else total + part
                    w += 2
            totals[at][i] = total.astype(totals[at].dtype)


def update_kernel(own_ref, got_ref, sums_ref, *refs):
    state, outs = [refs[i : i + 3] for i in range(0, 12, 3)], refs[12:]
    grads = wide_sum(own_ref[...], got_ref[...])
    lines = state[1][0].shape[0]
    wide = [
        jnp.concatenate([sums_ref[lines + 4 * i + k : lines + 4 * i + k + 1, :] for k in range(4)], axis=1)
        for i in range(state[3][0].shape[0])
    ]
    settings = (
        (grads[0], 0.04, weight_shrink),
        (sums_ref[:lines, :], 0.2, 0.0),
        (jnp.concatenate([grads[1, c * 128 : (c + 1) * 128, :] for c in range(4)], axis=1), 0.02, weight_shrink),
        (jnp.concatenate(wide, axis=0), 0.3, 0.0),
    )
    for n, (grad, rate, shrink) in enumerate(settings):
        param, moment, square = (ref[...] for ref in state[n])
        new = adamw_update(param, grad, moment, square, rate, shrink)
        for ref, values in zip(outs[3 * n : 3 * n + 3], new):
            ref[...] = values


def post_kernel(
    counts_ref, x_ref, cot_ref, vec_ref, stat_ref, own_ref, got_ref, *refs
):
    bias_refs, (out_ref, grad_ref, sums_ref, t_ref, h_ref, q_ref) = refs[:-6], refs[-6:]
    pixels, images, width = x_ref.shape
    size = pixels * width
    zero = jnp.zeros((images, width), f32)
    gate = valid_gate(counts_ref, (images, width))
    mu1, r1, mu2, r2 = (stat_ref[i][:, 0:1] for i in range(4))
    gain1, mix, gain2, scale, lower = (vec_ref[i : i + 1, :] for i in (0, 2, 3, 5, 6))
    lift = mixed_parts(x_ref, mu1, r1, vec_ref, h_ref, q_ref)

    def loop(body, init):
        return lax.fori_loop(0, pixels, body, init, unroll=7)

    def column(values):
        return jnp.sum(values, axis=0, keepdims=True)

    def first(p, carry):
        g_scale, g_lower, g_gain2, g_shift2 = carry
        middle = x_ref[p] + lift * q_ref[p]
        branch = own_ref[0, p] + got_ref[0, p].astype(f32) + lower
        out_ref[p] = middle + scale * branch
        weighted = cot_ref[p].astype(f32) * gate
        back = own_ref[1, p] + got_ref[1, p].astype(f32)
        h2 = (middle - mu2) * r2
        return (g_scale + weighted * branch, g_lower + weighted, g_gain2 + back * h2, g_shift2 + back)

    g_scale, g_lower, g_gain2, g_shift2 = loop(first, (zero,) * 4)
    mean2 = row_total(g_shift2 * gain2) / size
    mean2h = row_total(g_gain2 * gain2) / size

    def second(p, g_mix):
        middle = x_ref[p] + lift * q_ref[p]
        back = own_ref[1, p] + got_ref[1, p].astype(f32)
        h2 = (middle - mu2) * r2
        grad = cot_ref[p].astype(f32) * gate + r2 * (back * gain2 - mean2 - h2 * mean2h)
        grad_ref[p] = grad
        t_ref[p] = grad * mix
        return g_mix + grad * q_ref[p]

    g_mix = loop(second, zero) * (r1 * gain1)
    for p in range(pixels):
        h_ref[p] = along_row(lambda i: t_ref[i] * near_share(i), p)
    g_gain1 = g_shift1 = zero
    for p in range(pixels):
        ng = along_col(lambda i: h_ref[i], p) - t_ref[p]
        t_ref[p] = ng
        g_gain1 = g_gain1 + ng * ((x_ref[p] - mu1) * r1)
        g_shift1 = g_shift1 + ng
    mean1 = row_total(g_shift1 * gain1) / size
    mean1h = row_total(g_gain1 * gain1) / size

    def third(p, carry):
        h1 = (x_ref[p] - mu1) * r1
        grad_ref[p] = grad_ref[p] + r1 * (t_ref[p] * gain1 - mean1 - h1 * mean1h)
        return carry

    loop(third, 0)
    lines = bias_refs[0].shape[0]
    sums_ref[:lines, :] = bias_refs[0][...] + bias_refs[1][...] + bias_refs[2][...]
    for i, total in enumerate((g_gain1, g_shift1, g_mix, g_gain2, g_shift2, g_scale, g_lower * scale)):
        total = column(total)
        for k in range(width // 128):
            row = lines + (width // 128) * i + k
            sums_ref[row : row + 1, :] = total[:, k * 128 : (k + 1) * 128]


def call(kernel, outs, ins, scratch=(), vmem=12, smem=0, hold=True, loose=()):
    many = isinstance(outs, (list, tuple))
    arrays = (*ins, *(outs if many else [outs]))
    moved = sum(math.prod(v.shape) * v.dtype.itemsize for v in arrays)
    if hold:
        outs = [pltpu.VMEM(v.shape, v.dtype) for v in outs] if many else pltpu.VMEM(outs.shape, outs.dtype)
    ins = [
        v
        if i < smem or not (hold or i in loose)
        else pltpu.with_memory_space_constraint(v, pltpu.HBM if i in loose else pltpu.VMEM)
        for i, v in enumerate(ins)
    ]
    return pl.pallas_call(
        kernel,
        out_shape=outs,
        in_specs=[SMEM] * smem + [VMEM] * (len(ins) - smem),
        out_specs=[VMEM] * len(outs) if many else VMEM,
        scratch_shapes=list(scratch),
        name=getattr(kernel, "func", kernel).__name__,
        compiler_params=pltpu.CompilerParams(vmem_limit_bytes=vmem * 2**20),
        cost_estimate=pl.CostEstimate(flops=0, bytes_accessed=moved, transcendentals=0),
    )(*ins)


def struct(shape, dtype=f32):
    return jax.ShapeDtypeStruct(shape, dtype)


BOTH = ("narrow", "wide")


def joint(values, change):
    pairs = [(n * 16 + w, change(n, w)) for n in range(2) for w in range(16)]
    return lax.ppermute(values, BOTH, [(s, n * 16 + w) for s, (n, w) in pairs])


def flip(values, bit):
    return lax.ppermute(values, "wide", [(w, w ^ bit) for w in range(16)])


def far(values):
    return joint(values, lambda n, w: (n, w ^ (12 if n else 8)))


def across(values):
    return lax.ppermute(values, "narrow", [(0, 1), (1, 0)])


def diagonal(values):
    return joint(values, lambda n, w: (1 - n, w ^ 2))


def after(values, *others):
    return lax.optimization_barrier((values, *others))[0]


def wide_sum(*parts):
    total = parts[0].astype(f32)
    for part in parts[1:]:
        total = total + part.astype(f32)
    return total


def local_tree(
    features,
    cotangent,
    counts,
    hidden_weight,
    hidden_bias,
    output_weight,
    vectors,
    hidden_moment,
    hidden_square,
    bias_moment,
    bias_square,
    output_moment,
    output_square,
    vector_moment,
    vector_square,
):
    images, pixels, width = features.shape
    rows = images * pixels
    units = hidden_weight.shape[1]
    pair, pair_f = struct((2, width, units), bf16), struct((2, width, units))
    w0 = call(cast_kernel, pair, (hidden_weight, output_weight), loose=(0, 1))
    wz1, wzf, wy0 = flip(w0, 4), far(w0), flip(w0, 2)
    vectors_late, wy0 = lax.optimization_barrier((vectors, wy0))
    bias = hidden_bias.reshape(-1, 128)
    x = features.transpose(1, 0, 2)
    cot = cotangent.transpose(1, 0, 2)
    big = struct((pixels, images, width))
    keep = pltpu.VMEM((pixels, images, width), f32)
    tile = struct((rows, 256), bf16)
    sb, stat, *begun = call(
        pre_kernel,
        [
            struct((2, pixels, images, width), bf16),
            struct((4, images, 128)),
            tile,
            tile,
            struct((1, 256)),
            struct((width, 256)),
            struct((256, width)),
        ],
        (counts, x, cot, vectors_late, bias, w0, wy0),
        [keep, keep],
        smem=1,
        loose=(1, 2, 3),
        vmem=20,
    )
    sb = after(sb.reshape(2, rows, width), wzf, wz1, wy0)
    other = flip(sb, 1)
    wyf, wzo = flip(wzf, 2), across(wzf)
    total, total_low = struct((2, rows, width)), struct((2, rows, width), bf16)

    lines = struct(bias.shape)

    def blocks(first, weights, results, begun=()):
        tall = struct((2, rows, 128 * len(weights)), bf16)
        return call(
            functools.partial(block_kernel, first, len(weights)),
            [tall, tall, lines, *results],
            (sb, other, bias, *weights, *begun),
            vmem=20,
        )

    def back(sides, results, hidden, weights, old=(), loose=()):
        acts, lows = zip(*hidden)
        counts = [act.shape[2] // 128 for act in acts]
        kernel = functools.partial(back_kernel, sides, counts, bool(old))
        return call(kernel, results, (*acts, *lows, *weights, *old), loose=loose)

    w_near = [w0, wy0, wz1, wzf]
    *near_hidden, sums1, g0, gy0, gz1, gzf = blocks(0, w_near, [pair_f, pair, pair, pair_f], begun)
    z1 = flip(gz1, 4)
    wy1 = flip(after(wz1, sums1), 2)
    wyf = after(wyf, sums1)
    wyo = across(wyf)
    *far_hidden, sums2, gyf, gzo = blocks(4, [wyf, wzo], [pair, pair])
    yf, xs = flip(gyf, 2), across(gzo)
    old = back((0, 1), [total, total], (near_hidden, far_hidden), [*w_near, wyf, wzo])
    wyo, wy1, _ = lax.optimization_barrier((wyo, wy1, old[0]))
    *last_hidden, sums3, gyo, gy1 = blocks(6, [wyo, wy1], [pair, pair])
    ds, zy = diagonal(gyo), flip(gy1, 4)
    theirs = back((1,), [total_low], (last_hidden,), [wyo, wy1], old[1:])[0]
    theirs, yf, xs, z1 = lax.optimization_barrier((theirs, yf, xs, z1))
    got = flip(theirs, 1)
    mine = back((0,), [total], (last_hidden,), [wyo, wy1], old[:1])[0]

    shape = (2, pixels, images, width)
    payload = struct((bias.shape[0] + vectors.size // 128, 128))
    block_out, input_grad, sums = call(
        post_kernel,
        [big, big, payload],
        (counts, x, cot, vectors, stat, mine.reshape(shape), got.reshape(shape), sums1, sums2, sums3),
        [keep, keep, keep],
        smem=1,
        hold=False,
    )
    ds, zy, _ = lax.optimization_barrier((ds, zy, sums))
    sum_f = wide_sum(gzf, xs, yf, ds).astype(bf16)
    zf = far(sum_f)
    sums = sums + flip(sums, 1)
    sums = after(sums, sum_f)
    y0 = flip(after(wide_sum(gy0, zy).astype(bf16), sums), 2)
    sums = sums + flip(sums, 2)
    sums = sums + across(sums)
    own = wide_sum(g0, y0, z1, zf).astype(bf16)
    own, sums = lax.optimization_barrier((own, sums))
    got = across(own)
    for bit in (4, 8):
        sums = sums + flip(sums, bit)
    state = (
        (hidden_weight, hidden_moment, hidden_square),
        tuple(v.reshape(bias.shape) for v in (hidden_bias, bias_moment, bias_square)),
        (output_weight, output_moment, output_square),
        (vectors, vector_moment, vector_square),
    )
    new = call(
        update_kernel,
        [struct(v.shape) for group in state for v in group],
        (own, got, sums, *(v for group in state for v in group)),
        hold=False,
    )
    hidden_new, output_new, vector_new = new[:3], new[6:9], new[9:]
    bias_new = [v.reshape(hidden_bias.shape) for v in new[3:6]]
    return (
        block_out.transpose(1, 0, 2),
        input_grad.transpose(1, 0, 2),
        *hidden_new,
        *bias_new,
        *output_new,
        *vector_new,
    )


def solution(mesh):
    in_specs = (
        P(("narrow", "wide"), None, None),
        P(("narrow", "wide"), None, None),
        P(("narrow", "wide")),
        P(None, "wide"),
        P(),
        P("wide", None),
        P(),
        P(None, "wide"),
        P(None, "wide"),
        P(),
        P(),
        P("wide", None),
        P("wide", None),
        P(),
        P(),
    )
    out_specs = (
        P(("narrow", "wide"), None, None),
        P(("narrow", "wide"), None, None),
        P(None, "wide"),
        P(None, "wide"),
        P(None, "wide"),
        P(),
        P(),
        P(),
        P("wide", None),
        P("wide", None),
        P("wide", None),
        P(),
        P(),
        P(),
    )
    body = local_tree if dict(mesh.shape) == {"narrow": 2, "wide": 16} else local
    return jax.shard_map(body, mesh=mesh, in_specs=in_specs, out_specs=out_specs, check_vma=False)
```
